256 devices in a mesh: tile: 32 (over x, y, z_lo), frame: 8 (over z_hi, core).
Axes of the slice: x: 4, y: 4, z: 8 (z_hi: 4, z_lo: 2; z = z_hi * 2 + z_lo), core: 2. Of those that a mesh axis runs over, the one named last changes fastest.
Arguments:
- latents: bfloat16 [128, 8, 104, 384], P('tile', 'frame'), may hold values from -80 to 80
- row_video: int32 [128], replicated, may hold values from 0 to 3, never falling along the last dimension, each value on 1 to 90 neighbouring positions
- video_cols: int32 [4], replicated, may hold values from 52 to 104, as said below
- first_gain: float32 [384], replicated, may hold values from 0.5 to 1.5
- first_shift: float32 [384], replicated, may hold values from -3 to 3
- conv_weight: bfloat16 [3, 3, 3, 384, 384], replicated, may hold values from -0.0625 to 0.0625
- conv_bias: float32 [384], replicated, may hold values from -3 to 3
- second_gain: float32 [384], replicated, may hold values from 0.5 to 1.5
- second_shift: float32 [384], replicated, may hold values from -3 to 3
- triple_weight: bfloat16 [384, 1152], replicated, may hold values from -0.55 to 0.55
- triple_bias: float32 [1152], replicated, may hold values from -3 to 3
- output_weight: bfloat16 [384, 384], replicated, may hold values from -0.3125 to 0.3125
- output_bias: float32 [384], replicated, may hold values from -3 to 3
- upsample_weight: bfloat16 [3, 3, 384, 192], replicated, may hold values from -0.109375 to 0.109375
- upsample_bias: float32 [192], replicated, may hold values from -3 to 3
Outputs:
- decoded: bfloat16 [256, 8, 208, 192], P('tile', 'frame')
The draws below stay inside these ranges and needn't reach their ends.
Inputs may be any that keep to these rules, and one draw needn't show every extreme that they name: `row_video`: video numbers never fall along the rows; every video has 1 to 90 rows. `video_cols`: one video has all 104 columns.
All inputs are finite; a program needn't handle non-finite values.
Results may differ from the reference program's by a relative error of at most 0.013.
The reference program's roundings to bfloat16 on the way count: a program that leaves them out, or rounds other values in their place, can miss the bound.
Values may be sent and summed in bfloat16 or wider, within the bound.
A program may use at most 128 MiB of HBM per device.

```python
import math
import jax
import jax.numpy as jnp
import numpy as np
from jax import lax

CH = 384
CH_OUT = 192
GROUPS = 32
WIDTH = 104
ROWS_DEV = 4
ROWS = 128
FRAMES = 8
VIDEOS = 4
MOST_ROWS = 90
MIN_COLS = 52


def draw_latents(key, part):
    subkeys = jax.random.split(jax.random.fold_in(key, 11), 3)
    normal_part = jnp.clip(jax.random.normal(subkeys[0], (ROWS, FRAMES, WIDTH, CH), jnp.float32), -4.0, 4.0)
    cell_scale = jnp.exp(jax.random.uniform(subkeys[1], (ROWS, FRAMES, WIDTH, 1), jnp.float32, -1.15, 1.15))
    channel_scale = jnp.exp(jax.random.uniform(subkeys[2], (CH,), jnp.float32, -0.69, 0.69))
    height = jnp.arange(ROWS, dtype=jnp.float32) / (ROWS - 1) - 0.5
    rising = (3.0 ** height)[:, None, None, None]
    drawn = normal_part * cell_scale * channel_scale * rising
    return drawn.astype(jnp.bfloat16)


def draw_triple_weight(key, part):
    subkeys = jax.random.split(jax.random.fold_in(key, 23), 4)
    spread = CH ** (-0.5)
    query_part = 1.7 * spread * jnp.clip(jax.random.normal(subkeys[0], (CH, CH), jnp.float32), -4.0, 4.0)
    key_part = 1.7 * spread * jnp.clip(jax.random.normal(subkeys[1], (CH, CH), jnp.float32), -4.0, 4.0)
    value_part = spread * jnp.clip(jax.random.normal(subkeys[3], (CH, CH), jnp.float32), -4.0, 4.0)
    joined = jnp.concatenate([query_part, key_part, value_part], axis=1)
    return jnp.clip(joined, -0.546, 0.546).astype(jnp.bfloat16)


def draw_video_cols(key, part):
    subkeys = jax.random.split(jax.random.fold_in(key, 37), 2)
    columns = jax.random.randint(subkeys[0], (VIDEOS,), MIN_COLS, WIDTH + 1)
    chosen = jax.random.randint(subkeys[1], (), 0, VIDEOS)
    return jnp.where(jnp.arange(VIDEOS) == chosen, WIDTH, columns).astype(jnp.int32)


def split_up(amount, total, reach, slope):
    weights = [(1 << 20) // math.isqrt(rank ** slope) + 1 for rank in range(2, amount + 1)]
    spare, given = total - reach - (amount - 1), [1] * (amount - 1)
    while spare > 0:
        free = [i for i in range(amount - 1) if given[i] < reach]
        mass, budget = sum([weights[i] for i in free]), spare
        for i in free:
            addition = min(reach - given[i], max(1, budget * weights[i] // mass), spare)
            given[i] = given[i] + addition
            spare = spare - addition
    return np.array([reach] + given)


def uneven(own_key, number_of, total, reach, skew):
    if number_of == 2:
        one = jax.random.randint(own_key, (), max(1, total - reach), min(reach, total - 1) + 1)
        return jnp.stack([one, total - one])
    tallies = jnp.asarray(split_up(number_of, total, reach, skew), jnp.int32)
    couples = (number_of - 1) // 2
    giver, receiver = tallies[1:1 + 2 * couples:2], tallies[2:2 + 2 * couples:2]
    slack = jnp.minimum(giver - 1, reach - receiver)
    shifted = jax.random.randint(jax.random.fold_in(own_key, 1), (couples,), 0, 1 << 20) % (slack + 1)
    tallies = tallies.at[1:1 + 2 * couples:2].set(giver - shifted).at[2:2 + 2 * couples:2].set(receiver + shifted)
    return tallies[jax.random.permutation(jax.random.fold_in(own_key, 2), number_of)]


def centred(key, dims, scale, limit, held_as=jnp.bfloat16):
    values = scale * jax.random.normal(key, dims, jnp.float32)
    return jnp.clip(values, min=-limit, max=limit).astype(held_as)


def setup_inputs(seed: int = 0) -> dict:
    seeds = jax.random.split(jax.random.key(seed), 16)
    return {
        "latents": draw_latents(jax.random.fold_in(seeds[15], 71), 0),
        "row_video": jnp.searchsorted(jnp.cumsum(uneven(seeds[1], VIDEOS, ROWS, MOST_ROWS, 1)), jnp.arange(ROWS), side="right").astype(jnp.int32),
        "video_cols": draw_video_cols(jax.random.fold_in(seeds[15], 71), 0),
        "first_gain": jnp.clip(1.0 + 0.1 * jax.random.normal(seeds[3], (CH,), jnp.float32), 0.5, 1.5),
        "first_shift": centred(seeds[4], (CH,), 0.5, 3.0, jnp.float32),
        "conv_weight": centred(seeds[5], (3, 3, 3, CH, CH), (27 * CH) ** -0.5, 0.0625),
        "conv_bias": centred(seeds[6], (CH,), 0.5, 3.0, jnp.float32),
        "second_gain": jnp.clip(1.0 + 0.1 * jax.random.normal(seeds[7], (CH,), jnp.float32), 0.5, 1.5),
        "second_shift": centred(seeds[8], (CH,), 0.5, 3.0, jnp.float32),
        "triple_weight": draw_triple_weight(jax.random.fold_in(seeds[15], 71), 0),
        "triple_bias": centred(seeds[10], (3 * CH,), 0.5, 3.0, jnp.float32),
        "output_weight": centred(seeds[11], (CH, CH), CH ** -0.5, 0.3125),
        "output_bias": centred(seeds[12], (CH,), 0.5, 3.0, jnp.float32),
        "upsample_weight": centred(seeds[13], (3, 3, CH, CH_OUT), (9 * CH) ** -0.5, 0.109375),
        "upsample_bias": centred(seeds[14], (CH_OUT,), 0.5, 3.0, jnp.float32),
    }


EPSILON = 1e-05
MASKED = -1e+30
HIGHEST = lax.Precision.HIGHEST

def video_tables(row_video, video_cols):
    matches = row_video[:, None] == jnp.arange(VIDEOS, dtype=jnp.int32)[None, :]
    widths = lax.optimization_barrier(jnp.sum(jnp.where(matches, video_cols[None, :], 0), axis=1))
    return (matches.astype(jnp.float32), widths)

def group_norm(values, norm_gain, norm_shift, onehot, valid_mask, counts):
    channels = values.shape[3]
    per_group = channels // GROUPS
    member = (jnp.arange(channels, dtype=jnp.int32)[:, None] // per_group == jnp.arange(GROUPS, dtype=jnp.int32)[None, :]).astype(jnp.float32)
    mask_four = valid_mask.astype(jnp.float32)[:, None, :, None]
    masked = values * mask_four
    group_sum = jnp.einsum('rfwc,cg,rv->fvg', masked, member, onehot, precision=HIGHEST)
    group_mean = group_sum / counts
    mean_full = jnp.einsum('fvg,rv,cg->rfc', group_mean, onehot, member, precision=HIGHEST)
    centered = (values - mean_full[:, :, None, :]) * mask_four
    variance = jnp.einsum('rfwc,cg,rv->fvg', centered * centered, member, onehot, precision=HIGHEST) / counts
    scale_full = jnp.einsum('fvg,rv,cg->rfc', lax.rsqrt(variance + EPSILON), onehot, member, precision=HIGHEST)
    return centered * scale_full[:, :, None, :] * norm_gain + norm_shift

def causal_conv(hidden, conv_weight, row_video):
    row_count, frame_count, col_count, channels = hidden.shape
    padded = jnp.pad(hidden, ((1, 1), (2, 0), (1, 1), (0, 0)))
    labels = jnp.pad(row_video, 1, constant_values=-1)
    total = jnp.zeros((row_count * frame_count * col_count, conv_weight.shape[-1]), jnp.float32)
    for row_tap in range(3):
        same = (labels[row_tap:row_tap + row_count] == row_video).astype(hidden.dtype)[:, None, None, None]
        for time_tap in range(3):
            for col_tap in range(3):
                window = padded[row_tap:row_tap + row_count, time_tap:time_tap + frame_count, col_tap:col_tap + col_count] * same
                total = total + jnp.dot(window.reshape(-1, channels), conv_weight[time_tap, row_tap, col_tap], preferred_element_type=jnp.float32)
    return total.reshape(row_count, frame_count, col_count, -1)

def attend_all(queries, keys_all, values_all, row_video, valid_mask):
    row_count, frame_count, col_count, channels = queries.shape
    blocks = row_count // ROWS_DEV
    key_labels = jnp.repeat(row_video, col_count)
    key_valid = valid_mask.reshape(-1)
    scale = CH ** (-0.5)
    zero = jnp.zeros((), jnp.int32)

    def one_block(index):
        frame_index = (index // blocks).astype(jnp.int32)
        first_row = (index % blocks * ROWS_DEV).astype(jnp.int32)
        query_block = lax.dynamic_slice(queries, (first_row, frame_index, zero, zero), (ROWS_DEV, 1, col_count, channels)).reshape(-1, channels)
        key_frame = lax.dynamic_slice(keys_all, (zero, frame_index, zero, zero), (row_count, 1, col_count, channels)).reshape(-1, channels)
        value_frame = lax.dynamic_slice(values_all, (zero, frame_index, zero, zero), (row_count, 1, col_count, channels)).reshape(-1, channels)
        query_labels = jnp.repeat(lax.dynamic_slice(row_video, (first_row,), (ROWS_DEV,)), col_count)
        scores = jnp.dot(query_block, key_frame.T, preferred_element_type=jnp.float32) * scale
        allowed = (query_labels[:, None] == key_labels[None, :]) & key_valid[None, :]
        scores = jnp.where(allowed, scores, MASKED)
        largest = lax.optimization_barrier(jnp.max(scores, axis=1, keepdims=True))
        weights = jnp.where(allowed, jnp.exp(scores - largest), 0.0)
        denominator = lax.optimization_barrier(jnp.sum(weights, axis=1, keepdims=True))
        mixed = jnp.dot(weights.astype(jnp.bfloat16), value_frame, preferred_element_type=jnp.float32) / denominator
        return mixed.astype(jnp.bfloat16).reshape(ROWS_DEV, col_count, channels)
    results = lax.map(one_block, jnp.arange(frame_count * blocks, dtype=jnp.int32))
    results = results.reshape(frame_count, row_count, col_count, channels)
    return jnp.transpose(results, (1, 0, 2, 3))

def upsample_conv(values, weight, row_video):
    row_count, frame_count, col_count, channels = values.shape
    doubled = jnp.repeat(jnp.repeat(values, 2, axis=0), 2, axis=2)
    up_labels = jnp.repeat(row_video, 2)
    padded = jnp.pad(doubled, ((1, 1), (0, 0), (1, 1), (0, 0)))
    labels = jnp.pad(up_labels, 1, constant_values=-1)
    total = jnp.zeros((4 * row_count * frame_count * col_count, weight.shape[-1]), jnp.float32)
    for row_tap in range(3):
        same = (labels[row_tap:row_tap + 2 * row_count] == up_labels).astype(values.dtype)[:, None, None, None]
        for col_tap in range(3):
            window = padded[row_tap:row_tap + 2 * row_count, :, col_tap:col_tap + 2 * col_count] * same
            total = total + jnp.dot(window.reshape(-1, channels), weight[row_tap, col_tap], preferred_element_type=jnp.float32)
    return total.reshape(2 * row_count, frame_count, 2 * col_count, -1)

def reference(latents, row_video, video_cols, first_gain, first_shift, conv_weight, conv_bias, second_gain, second_shift, triple_weight, triple_bias, output_weight, output_bias, upsample_weight, upsample_bias):
    onehot, row_widths = video_tables(row_video, video_cols)
    valid_mask = jnp.arange(WIDTH, dtype=jnp.int32)[None, :] < row_widths[:, None]
    mask_four = valid_mask[:, None, :, None]
    counts = (lax.optimization_barrier(jnp.sum(onehot, axis=0)) * video_cols.astype(jnp.float32) * (CH // GROUPS))[None, :, None]
    source = latents.astype(jnp.float32)
    first_normed = group_norm(source, first_gain, first_shift, onehot, valid_mask, counts)
    hidden = jnp.where(mask_four, jax.nn.silu(first_normed), 0.0).astype(jnp.bfloat16)
    branch = causal_conv(hidden, conv_weight, row_video)
    after_conv = jnp.where(mask_four, source + branch + conv_bias, 0.0).astype(jnp.bfloat16)
    second_normed = jnp.where(mask_four, group_norm(after_conv.astype(jnp.float32), second_gain, second_shift, onehot, valid_mask, counts), 0.0).astype(jnp.bfloat16)
    triple = (jnp.dot(second_normed.reshape(-1, CH), triple_weight, preferred_element_type=jnp.float32) + triple_bias).astype(jnp.bfloat16)
    triple = triple.reshape(ROWS, FRAMES, WIDTH, 3 * CH)
    mixed = attend_all(triple[..., :CH], triple[..., CH:2 * CH], triple[..., 2 * CH:], row_video, valid_mask)
    attended = jnp.dot(mixed.reshape(-1, CH), output_weight, preferred_element_type=jnp.float32).reshape(ROWS, FRAMES, WIDTH, CH)
    after_attention = jnp.where(mask_four, after_conv.astype(jnp.float32) + attended + output_bias, 0.0).astype(jnp.bfloat16)
    decoded = upsample_conv(after_attention, upsample_weight, row_video)
    up_valid = jnp.arange(2 * WIDTH, dtype=jnp.int32)[None, :] < 2 * jnp.repeat(row_widths, 2)[:, None]
    return jnp.where(up_valid[:, None, :, None], decoded + upsample_bias, 0.0).astype(jnp.bfloat16)
```

```python
import jax
import jax.numpy as jnp
from jax import lax
from jax.sharding import PartitionSpec as P

GROUPS = 32


EPSILON = 1e-05
MASKED = -1e30
HIGHEST = lax.Precision.HIGHEST


def shifted(shard, axis, by):
    length = lax.axis_size(axis)
    pairs = [(i, i + by) for i in range(length) if 0 <= i + by < length]
    return lax.ppermute(shard, axis, pairs)


def padded_2(shard, sides, width):
    for axis, dim in sides:
        size, length = (lax.axis_size(axis), shard.shape[dim])
        up = [(i, (i + 1) % size) for i in range(size - 1)]
        down = [(j, i) for i, j in up]
        last = lax.slice_in_dim(shard, length - width, length, axis=dim)
        leading = lax.slice_in_dim(shard, 0, width, axis=dim)
        before = lax.ppermute(last, axis, up)
        after = lax.ppermute(leading, axis, down)
        shard = jnp.concatenate([before, shard, after], axis=dim)
    return shard


def video_lookup(labels, video_cols):
    numbers = jnp.arange(video_cols.shape[0], dtype=jnp.int32)
    matches = labels[:, None] == numbers[None, :]
    widths = jnp.sum(jnp.where(matches, video_cols[None, :], 0), axis=1)
    return (matches.astype(jnp.float32), widths)


def group_norm(values, norm_gain, norm_shift, onehot, valid_mask, counts):
    channels = values.shape[3]
    per_group = channels // GROUPS
    member = (
        jnp.arange(channels, dtype=jnp.int32)[:, None] // per_group
        == jnp.arange(GROUPS, dtype=jnp.int32)[None, :]
    ).astype(jnp.float32)
    mask_four = valid_mask.astype(jnp.float32)[:, None, :, None]
    masked = values * mask_four
    partial_sum = jnp.einsum("rfwc,cg,rv->fvg", masked, member, onehot, precision=HIGHEST)
    group_mean = lax.psum(partial_sum, "tile") / counts
    mean_full = jnp.einsum("fvg,rv,cg->rfc", group_mean, onehot, member, precision=HIGHEST)
    centered = (values - mean_full[:, :, None, :]) * mask_four
    partial_spread = jnp.einsum(
        "rfwc,cg,rv->fvg", centered * centered, member, onehot, precision=HIGHEST
    )
    variance = lax.psum(partial_spread, "tile") / counts
    scale_full = jnp.einsum(
        "fvg,rv,cg->rfc", lax.rsqrt(variance + EPSILON), onehot, member, precision=HIGHEST
    )
    return centered * scale_full[:, :, None, :] * norm_gain + norm_shift


def causal_context(hidden):
    earlier = shifted(hidden, "frame", 1)
    farther = shifted(hidden, "frame", 2)
    earlier = jnp.concatenate([farther, earlier], axis=1)
    stacked = jnp.concatenate([earlier, hidden], axis=1)
    context = padded_2(stacked, (("tile", 0),), 1)
    return context


def conv_taps(context, conv_weight, near_labels, own_labels):
    row_count = own_labels.shape[0]
    frame_count = context.shape[1] - 2
    col_count = context.shape[2]
    channels = context.shape[3]
    padded = jnp.pad(context, ((0, 0), (0, 0), (1, 1), (0, 0)))
    total = jnp.zeros((row_count * frame_count * col_count, conv_weight.shape[-1]), jnp.float32)
    for row_tap in range(3):
        same = (near_labels[row_tap : row_tap + row_count] == own_labels).astype(context.dtype)[
            :, None, None, None
        ]
        for time_tap in range(3):
            window = padded[row_tap : row_tap + row_count, time_tap : time_tap + frame_count] * same
            columns = jnp.concatenate(
                [window[:, :, col_tap : col_tap + col_count] for col_tap in range(3)], axis=-1
            )
            total = total + jnp.dot(
                columns.reshape(-1, 3 * channels),
                conv_weight[time_tap, row_tap].reshape(3 * channels, -1),
                preferred_element_type=jnp.float32,
            )
    return total.reshape(row_count, frame_count, col_count, -1)


def upsample_conv(rimmed, weight, near_labels, own_labels):
    row_count = own_labels.shape[0]
    frame_count = rimmed.shape[1]
    wide_count = 2 * rimmed.shape[2]
    channels = rimmed.shape[3]
    doubled = jnp.repeat(jnp.repeat(rimmed, 2, axis=0), 2, axis=2)[1 : 2 * row_count + 3]
    doubled = jnp.pad(doubled, ((0, 0), (0, 0), (1, 1), (0, 0)))
    up_labels = jnp.repeat(near_labels, 2)[1 : 2 * row_count + 3]
    target_labels = jnp.repeat(own_labels, 2)
    total = jnp.zeros((2 * row_count * frame_count * wide_count, weight.shape[-1]), jnp.float32)
    for row_tap in range(3):
        same = (up_labels[row_tap : row_tap + 2 * row_count] == target_labels).astype(rimmed.dtype)[
            :, None, None, None
        ]
        window = doubled[row_tap : row_tap + 2 * row_count] * same
        columns = jnp.concatenate(
            [window[:, :, col_tap : col_tap + wide_count] for col_tap in range(3)], axis=-1
        )
        total = total + jnp.dot(
            columns.reshape(-1, 3 * channels),
            weight[row_tap].reshape(3 * channels, -1),
            preferred_element_type=jnp.float32,
        )
    return total.reshape(2 * row_count, frame_count, wide_count, -1)


def shards(
    latents,
    row_video,
    video_cols,
    first_gain,
    first_shift,
    conv_weight,
    conv_bias,
    second_gain,
    second_shift,
    triple_weight,
    triple_bias,
    output_weight,
    output_bias,
    upsample_weight,
    upsample_bias,
):
    row_count, frame_count, col_count, channels = latents.shape
    first_row = lax.axis_index("tile") * row_count
    canvas_onehot, canvas_widths = video_lookup(row_video, video_cols)
    counts = (
        jnp.sum(canvas_onehot, axis=0) * video_cols.astype(jnp.float32) * (channels // GROUPS)
    )[None, :, None]
    bordered = jnp.pad(row_video, 1, constant_values=-1)
    near_labels = lax.dynamic_slice_in_dim(bordered, first_row, row_count + 2)
    own_labels = near_labels[1 : row_count + 1]
    onehot, own_widths = video_lookup(own_labels, video_cols)
    column_ids = jnp.arange(col_count, dtype=jnp.int32)
    valid_mask = column_ids[None, :] < own_widths[:, None]
    mask_four = valid_mask[:, None, :, None]
    source = latents.astype(jnp.float32)
    first_normed = group_norm(source, first_gain, first_shift, onehot, valid_mask, counts)
    hidden = jnp.where(mask_four, jax.nn.silu(first_normed), 0.0).astype(jnp.bfloat16)
    context = causal_context(hidden)
    branch = conv_taps(context, conv_weight, near_labels, own_labels)
    after_conv = jnp.where(mask_four, source + branch + conv_bias, 0.0).astype(jnp.bfloat16)
    second_normed = jnp.where(
        mask_four,
        group_norm(
            after_conv.astype(jnp.float32), second_gain, second_shift, onehot, valid_mask, counts
        ),
        0.0,
    ).astype(jnp.bfloat16)
    flat_normed = second_normed.reshape(-1, channels)
    scale = channels ** (-0.5)
    lowest = own_labels[0]
    highest = own_labels[row_count - 1]
    block_rows = row_count
    while block_rows * col_count < 1024:
        block_rows = block_rows * 2

    def attend_block(state, block, block_first, queries, query_shift):
        rows_here = block.shape[0]
        block_labels = lax.dynamic_slice_in_dim(row_video, block_first, rows_here)
        block_widths = lax.dynamic_slice_in_dim(canvas_widths, block_first, rows_here)

        def update(carried):
            running_max, running_total, accum = carried
            cells_flat = jnp.moveaxis(block, 1, 0).reshape(frame_count, -1, channels)
            scores = (
                jnp.einsum("rfwc,fkc->rfwk", queries, cells_flat, preferred_element_type=jnp.float32)
                + query_shift[..., None]
            )
            same_video = own_labels[:, None] == block_labels[None, :]
            key_valid = column_ids[None, :] < block_widths[:, None]
            allowed = (same_video[:, :, None] & key_valid[None, :, :]).reshape(row_count, -1)[
                :, None, None, :
            ]
            scores = jnp.where(allowed, scores, MASKED)
            new_max = jnp.maximum(running_max, jnp.max(scores, axis=3))
            weights = jnp.where(allowed, jnp.exp(scores - new_max[..., None]), 0.0)
            factor = jnp.exp(running_max - new_max)
            running_total = running_total * factor + jnp.sum(weights, axis=3)
            accum = accum * factor[..., None] + jnp.einsum(
                "rfwk,fkc->rfwc",
                weights.astype(jnp.bfloat16),
                cells_flat,
                preferred_element_type=jnp.float32,
            )
            return (new_max, running_total, accum)

        def unchanged(carried):
            return carried

        touches = (block_labels[rows_here - 1] >= lowest) & (block_labels[0] <= highest)
        return lax.cond(touches, update, unchanged, state)

    initial = (
        jnp.full((row_count, frame_count, col_count), MASKED, jnp.float32),
        jnp.zeros((row_count, frame_count, col_count), jnp.float32),
        jnp.zeros((row_count, frame_count, col_count, channels), jnp.float32),
    )
    key_weight = triple_weight[:, channels : 2 * channels]
    value_weight = triple_weight[:, 2 * channels :]
    plain = (
        jnp.dot(flat_normed, triple_weight[:, :channels], preferred_element_type=jnp.float32)
        + triple_bias[:channels]
    ).astype(jnp.bfloat16)
    query_shift = (
        jnp.dot(plain.astype(jnp.float32), triple_bias[channels : 2 * channels], precision=HIGHEST)
        * scale
    ).reshape(row_count, frame_count, col_count)
    queries = (
        jnp.einsum("nd,cd->nc", plain, key_weight, preferred_element_type=jnp.float32) * scale
    ).astype(jnp.bfloat16)
    queries = queries.reshape(row_count, frame_count, col_count, channels)
    shard_piece = lax.all_gather(second_normed, "tile", axis=0, tiled=True)
    piece_rows = shard_piece.shape[0]
    step_rows = block_rows

    def advance(position, carried):
        offset = position * step_rows
        block = lax.dynamic_slice_in_dim(shard_piece, offset, step_rows)
        return attend_block(carried, block, offset, queries, query_shift)

    folded = lax.fori_loop(0, piece_rows // step_rows, advance, initial)
    running_max, running_total, accum = folded
    averaged = (accum / running_total[..., None]).astype(jnp.bfloat16)
    mixed = (
        jnp.dot(
            averaged.reshape(-1, channels), value_weight, preferred_element_type=jnp.float32
        )
        + triple_bias[2 * channels :]
    ).astype(jnp.bfloat16)
    attended = jnp.dot(
        mixed.reshape(-1, channels), output_weight, preferred_element_type=jnp.float32
    ).reshape(row_count, frame_count, col_count, channels)
    after_attention = jnp.where(
        mask_four, after_conv.astype(jnp.float32) + attended + output_bias, 0.0
    ).astype(jnp.bfloat16)
    rimmed = padded_2(after_attention, (("tile", 0),), 1)
    decoded = upsample_conv(rimmed, upsample_weight, near_labels, own_labels)
    up_valid = (
        jnp.arange(2 * col_count, dtype=jnp.int32)[None, :] < 2 * jnp.repeat(own_widths, 2)[:, None]
    )
    return jnp.where(up_valid[:, None, :, None], decoded + upsample_bias, 0.0).astype(jnp.bfloat16)


def solution(mesh):
    in_specs = (
        P("tile", "frame", None, None),
        P(),
        P(),
        P(),
        P(),
        P(),
        P(),
        P(),
        P(),
        P(),
        P(),
        P(),
        P(),
        P(),
        P(),
    )
    out_specs = P("tile", "frame", None, None)
    return jax.shard_map(shards, mesh=mesh, in_specs=in_specs, out_specs=out_specs, check_vma=False)
```

```python
import functools
import math

import jax
import jax.numpy as jnp
import numpy as np
from jax import lax
from jax.experimental import pallas as pl
from jax.experimental.pallas import tpu as pltpu
from jax.sharding import PartitionSpec as P

GROUPS = 32
EPSILON = 1e-05
MASKED = -1e30
HIGHEST = lax.Precision.HIGHEST
MESH = pl.DeviceIdType.MESH
F32 = jnp.float32
BF16 = jnp.bfloat16
CH = 384
OUT = 192
ROWS = 4
COLS = 104
WIDE = 112
CELLS = ROWS * COLS
PADDED = ROWS * WIDE
LAST = CELLS - WIDE
LANES = 128
EXT = CH + LANES
TILES = 32
FRAMES = 8
KEYS = 8 * CELLS
NT = (((1,), (1,)), ((), ()))


def remote(src, dst, send_sem, recv_sem, tile, frame):
    return pltpu.make_async_remote_copy(
        src_ref=src,
        dst_ref=dst,
        send_sem=send_sem,
        recv_sem=recv_sem,
        device_id={"tile": tile, "frame": frame},
        device_id_type=MESH,
    )


def place():
    tile = lax.axis_index("tile")
    frame = lax.axis_index("frame")
    x = lax.div(tile, 8)
    y = lax.rem(lax.div(tile, 2), 4)
    z = lax.rem(tile, 2)
    return tile, frame, x, y, z


def tile_at(x, y, z):
    return lax.rem(x, 4) * 8 + lax.rem(y, 4) * 2 + lax.rem(z, 2)


def greet(barrier, tile, frame):
    pl.semaphore_signal(
        barrier, inc=1, device_id={"tile": tile, "frame": frame}, device_id_type=MESH
    )


def exact(a, b):
    return jnp.dot(a, b, precision=HIGHEST, preferred_element_type=F32)


def pick(table, label):
    rows = lax.broadcasted_iota(jnp.int32, (8, CH), 0)
    chosen = rows == label
    mean = jnp.sum(jnp.where(chosen, table[0:8, :], 0.0), axis=0, keepdims=True)
    scale = jnp.sum(jnp.where(chosen, table[8:16, :], 0.0), axis=0, keepdims=True)
    return mean, scale


def local_sums(values, labels, widths, first, member, member_t, st):
    column = lax.broadcasted_iota(jnp.int32, (COLS, CH), 0)
    line = lax.broadcasted_iota(jnp.int32, (8, 1), 0)
    per_row = jnp.ones((8, 1), F32)
    for r in range(ROWS):
        width = widths[first + r]
        mask = column < width
        cells = values[r * COLS : (r + 1) * COLS]
        total = jnp.sum(jnp.where(mask, cells, 0.0), axis=0, keepdims=True)
        mean = total / width.astype(F32)
        apart = jnp.where(mask, cells - mean, 0.0)
        st[r : r + 1, :] = total
        st[ROWS + r : ROWS + r + 1, :] = jnp.sum(apart * apart, axis=0, keepdims=True)
        per_row = jnp.where((line == r) | (line == ROWS + r), width.astype(F32), per_row)
    upper = line < ROWS
    held = st[...]
    grouped = exact(held, member_t)
    group_mean = exact(jnp.where(upper, grouped / (per_row * (CH // GROUPS)), 0.0), member)
    spread = jnp.where(upper, held / per_row - group_mean, 0.0)
    extra = exact(per_row * spread * spread, member_t)
    lower = pltpu.roll(extra, ROWS, 0)
    return jnp.where(upper, grouped, grouped + lower)


def gather_sums(gat, send_sems, recv_sems):
    tile, frame, x, y, z = place()
    peer = tile_at(x, y, z + 1)
    copy = remote(gat.at[tile], gat.at[tile], send_sems.at[0], recv_sems.at[0], peer, frame)
    copy.start()
    copy.wait()
    mine = pl.ds(tile - z, 2)
    copies = []
    for d in range(1, 4):
        peer = tile_at(x, y + d, z)
        copies.append(
            remote(gat.at[mine], gat.at[mine], send_sems.at[d], recv_sems.at[d], peer, frame)
        )
    for copy in copies:
        copy.start()
    for copy in copies:
        copy.wait()
    mine = pl.ds(x * 8, 8)
    copies = []
    for d in range(1, 4):
        peer = tile_at(x + d, y, z)
        copies.append(
            remote(
                gat.at[mine], gat.at[mine], send_sems.at[3 + d], recv_sems.at[3 + d], peer, frame
            )
        )
    for copy in copies:
        copy.start()
    for copy in copies:
        copy.wait()


def combine_sums(gat, onehot_sum, onehot_sum_t, onehot_both, row_cells, inverse, member):
    held = gat[...].reshape(TILES * 8, LANES)
    mean = exact(onehot_sum, held) * inverse
    mean_rows = exact(onehot_sum_t, mean)
    upper = lax.rem(lax.broadcasted_iota(jnp.int32, (TILES * 8, 1), 0), 8) < ROWS
    off = held / row_cells - mean_rows
    spread = jnp.where(upper, row_cells * off * off, held)
    variance = exact(onehot_both, spread) * inverse
    scale = lax.rsqrt(variance + EPSILON)
    return exact(mean, member), exact(scale, member)


def front_kernel(
    labels, widths, lat, onehot_sum, onehot_sum_t, onehot_both, row_cells, inverse, member,
    member_t, gain, shift, weight_hbm, bias, out,
    main, top, bot, gat, st, tabs, hid, weight, acc,
    stat_send, stat_recv, main_send, main_recv, halo_send, halo_recv, tab_send, tab_recv,
    weight_sem,
):
    tile, frame, x, y, z = place()
    first = tile * ROWS + 1
    load = pltpu.make_async_copy(weight_hbm, weight, weight_sem)
    load.start()
    barrier = pltpu.get_barrier_semaphore()
    greet(barrier, tile_at(x, y, z + 1), frame)
    for d in range(1, 4):
        greet(barrier, tile_at(x, y + d, z), frame)
        greet(barrier, tile_at(x + d, y, z), frame)
    awaited = 7
    for step in (-2, -1, 1, 2):
        there = (frame + step >= 0) & (frame + step < FRAMES)

        @pl.when(there)
        def _():
            greet(barrier, tile, frame + step)

        awaited = awaited + there.astype(jnp.int32)
    for step in (-1, 1):
        there = (tile + step >= 0) & (tile + step < TILES)

        @pl.when(there)
        def _():
            greet(barrier, tile + step, frame)

        awaited = awaited + there.astype(jnp.int32)
    pl.semaphore_wait(barrier, awaited)

    even = lax.rem(frame, 2) == 0
    next_frame = frame + 1 < FRAMES
    skip_frame = even & (frame + 2 < FRAMES)
    relay = even & (frame >= 2)
    has = {1: frame >= 1, 0: frame >= 2}
    above = tile >= 1
    below = tile + 1 < TILES

    to_next = remote(lat, main.at[1], main_send.at[1], main_recv.at[1], tile, frame + 1)
    to_skip = remote(lat, main.at[0], main_send.at[0], main_recv.at[0], tile, frame + 2)
    to_relay = remote(main.at[1], main.at[0], main_send.at[2], main_recv.at[0], tile, frame + 1)

    def halo(a):
        src = lat if a == 2 else main.at[a]
        up = remote(
            src.at[pl.ds(0, WIDE)], bot.at[a], halo_send.at[a, 0], halo_recv.at[a, 0],
            tile - 1, frame,
        )
        down = remote(
            src.at[pl.ds(LAST, WIDE)], top.at[a], halo_send.at[a, 1], halo_recv.at[a, 1],
            tile + 1, frame,
        )
        return up, down

    def start_halo(a):
        up, down = halo(a)

        @pl.when(above)
        def _():
            up.start()

        @pl.when(below)
        def _():
            down.start()

    def wait_halo(a):
        up, down = halo(a)

        @pl.when(below)
        def _():
            up.wait_recv()

        @pl.when(above)
        def _():
            down.wait_recv()

    def end_halo(a):
        up, down = halo(a)

        @pl.when(above)
        def _():
            up.wait_send()

        @pl.when(below)
        def _():
            down.wait_send()

    @pl.when(skip_frame)
    def _():
        to_skip.start()

    @pl.when(next_frame)
    def _():
        to_next.start()

    start_halo(2)

    source = lat[...].astype(F32)
    gat[tile] = local_sums(source, labels, widths, first, member[...], member_t[...], st)
    gather_sums(gat, stat_send, stat_recv)
    mean, scale = combine_sums(
        gat, onehot_sum[...], onehot_sum_t[...], onehot_both[...], row_cells[...], inverse[...],
        member[...],
    )
    tabs[2, 0:8, :] = mean
    tabs[2, 8:16, :] = scale
    tab_next = remote(tabs.at[2], tabs.at[1], tab_send.at[1], tab_recv.at[1], tile, frame + 1)
    tab_skip = remote(tabs.at[2], tabs.at[0], tab_send.at[0], tab_recv.at[0], tile, frame + 2)

    @pl.when(next_frame)
    def _():
        tab_next.start()

    @pl.when(frame + 2 < FRAMES)
    def _():
        tab_skip.start()

    column = lax.broadcasted_iota(jnp.int32, (COLS, CH), 0)

    def activate(a, row, cells):
        label = labels[first - 1 + row]
        width = widths[first - 1 + row]
        row_mean, row_scale = pick(tabs[a], label)
        normed = (cells - row_mean) * row_scale * gain[...] + shift[...]
        hidden = normed / (1.0 + jnp.exp(-normed))
        hidden = jnp.where(column < width, hidden, 0.0)
        hidden = jnp.concatenate([hidden, jnp.zeros((WIDE - COLS, CH), F32)], axis=0)
        lines = pl.ds(row * WIDE, WIDE)
        hid[a, lines, 0:CH] = pltpu.roll(hidden, 1, 0).astype(BF16)
        hid[a, lines, CH : 2 * CH] = hidden.astype(BF16)
        hid[a, lines, 2 * CH : 3 * CH] = pltpu.roll(hidden, WIDE - 1, 0).astype(BF16)

    def activate_main(a):
        cells = lat[...].astype(F32) if a == 2 else main[a].astype(F32)
        for r in range(ROWS):
            activate(a, r + 1, cells[r * COLS : (r + 1) * COLS])

    def activate_halo(a):
        activate(a, 0, top[a].astype(F32)[WIDE - COLS :])
        activate(a, ROWS + 1, bot[a].astype(F32)[:COLS])

    def convolve(a):
        def tap(b, carry):
            lines = pl.ds(pl.multiple_of(b * WIDE, 16), PADDED)
            product = jnp.dot(hid[a, lines, :], weight[a * 3 + b], preferred_element_type=F32)
            if a == 2:
                acc[b] = product
            else:
                acc[b] = acc[b] + product
            return carry

        lax.fori_loop(0, 3, tap, 0)

    activate_main(2)

    @pl.when(has[1])
    def _():
        to_next.wait_recv()

    @pl.when(relay)
    def _():
        to_relay.start()

    @pl.when(has[1])
    def _():
        start_halo(1)

    wait_halo(2)
    activate_halo(2)
    load.wait()
    convolve(2)

    @pl.when(has[0])
    def _():
        to_skip.wait_recv()
        start_halo(0)

    @pl.when(has[1])
    def _():
        tab_next.wait_recv()
        activate_main(1)
        wait_halo(1)
        activate_halo(1)
        convolve(1)

    @pl.when(has[0])
    def _():
        tab_skip.wait_recv()
        activate_main(0)
        wait_halo(0)
        activate_halo(0)
        convolve(0)

    source = lat[...].astype(F32)
    rows = []
    for r in range(ROWS):
        own = labels[first + r]
        lines = pl.ds(r * WIDE, COLS)
        total = acc[1, lines, :]
        total = total + jnp.where(labels[first + r - 1] == own, acc[0, lines, :], 0.0)
        total = total + jnp.where(labels[first + r + 1] == own, acc[2, lines, :], 0.0)
        total = source[r * COLS : (r + 1) * COLS] + total + bias[...]
        rows.append(jnp.where(column < widths[first + r], total, 0.0))
    out[...] = jnp.concatenate(rows, axis=0).astype(BF16)

    @pl.when(next_frame)
    def _():
        to_next.wait_send()
        tab_next.wait_send()

    @pl.when(frame + 2 < FRAMES)
    def _():
        tab_skip.wait_send()

    @pl.when(skip_frame)
    def _():
        to_skip.wait_send()

    @pl.when(relay)
    def _():
        to_relay.wait_send()

    end_halo(2)

    @pl.when(has[1])
    def _():
        end_halo(1)

    @pl.when(has[0])
    def _():
        end_halo(0)


def attention_kernel(
    labels, widths, own, onehot_sum, onehot_sum_t, onehot_both, row_cells, inverse, member,
    member_t, gain, shift, triple_weight, triple_bias, output_weight, output_bias,
    result, result_top, result_bot,
    kv, qb, gat, st, tab, keys, queries, scores, sent, parts, rim, top, bot,
    stat_send, stat_recv, kv_send, kv_recv, q_send, q_recv, part_send, part_recv,
    halo_send, halo_recv,
):
    tile, frame, x, y, z = place()
    first = tile * ROWS + 1
    above = tile >= 1
    below = tile + 1 < TILES
    barrier = pltpu.get_barrier_semaphore()
    for k in range(1, 8):
        greet(barrier, tile_at(x, y + k // 2, z + k % 2), frame)
    for d in range(1, 4):
        greet(barrier, tile_at(x + d, y, z), frame)
    awaited = 10
    for there, step in ((above, -1), (below, 1)):

        @pl.when(there)
        def _():
            greet(barrier, tile + step, frame)

        awaited = awaited + there.astype(jnp.int32)
    pl.semaphore_wait(barrier, awaited)

    kv_copies = []
    for k in range(1, 8):
        peer = tile_at(x, y + k // 2, z + k % 2)
        kv_copies.append(
            remote(own, kv.at[k - 1], kv_send.at[k - 1], kv_recv.at[k - 1], peer, frame)
        )
    q_copies = []
    for d in range(1, 4):
        peer = tile_at(x + d, y, z)
        q_copies.append(remote(own, qb.at[d - 1], q_send.at[d - 1], q_recv.at[d - 1], peer, frame))
    for copy in kv_copies + q_copies:
        copy.start()

    source = own[...].astype(F32)
    gat[tile] = local_sums(source, labels, widths, first, member[...], member_t[...], st)
    gather_sums(gat, stat_send, stat_recv)
    mean, scale = combine_sums(
        gat, onehot_sum[...], onehot_sum_t[...], onehot_both[...], row_cells[...], inverse[...],
        member[...],
    )
    tab[0:8, :] = mean
    tab[8:16, :] = scale
    column = lax.broadcasted_iota(jnp.int32, (COLS, CH), 0)
    cell_column = lax.broadcasted_iota(jnp.int32, (COLS, LANES), 0)
    lane = lax.broadcasted_iota(jnp.int32, (COLS, LANES), 1)
    wide_lane = lax.broadcasted_iota(jnp.int32, (CELLS, LANES), 1)
    to_exponent = CH ** (-0.5) * math.log2(math.e)

    def normalise(block, block_tile):
        cells = block.astype(F32)
        rows = []
        for r in range(ROWS):
            at = block_tile * ROWS + 1 + r
            row_mean, row_scale = pick(tab, labels[at])
            part = cells[r * COLS : (r + 1) * COLS]
            normed = (part - row_mean) * row_scale * gain[...] + shift[...]
            rows.append(jnp.where(column < widths[at], normed, 0.0))
        return jnp.concatenate(rows, axis=0).astype(BF16)

    def put_query(slot, block, block_tile):
        normed = normalise(block, block_tile)
        plain = jnp.dot(normed, triple_weight[:, 0:CH], preferred_element_type=F32)
        plain = (plain + triple_bias[:, 0:CH]).astype(BF16)
        turned = lax.dot_general(
            plain, triple_weight[:, CH : 2 * CH], NT, preferred_element_type=F32
        )
        constant = jnp.sum(
            plain.astype(F32) * triple_bias[:, CH : 2 * CH], axis=1, keepdims=True
        )
        queries[slot, :, 0:CH] = (turned * to_exponent).astype(BF16)
        marks = []
        for r in range(ROWS):
            label = labels[block_tile * ROWS + 1 + r]
            marks.append(jnp.where(lane == label, 1.0, 0.0))
        marks = jnp.concatenate(marks, axis=0)
        marks = jnp.where(wide_lane == 4, constant * to_exponent, marks)
        queries[slot, :, CH:EXT] = marks.astype(BF16)

    def put_keys(slot, block, block_tile):
        lines = pl.ds(pl.multiple_of(slot * CELLS, 16), CELLS)
        keys[lines, 0:CH] = normalise(block, block_tile)
        marks = []
        for r in range(ROWS):
            at = block_tile * ROWS + 1 + r
            seen = (lane == labels[at]) & (cell_column < widths[at])
            mark = jnp.where(seen, 0.0, MASKED)
            marks.append(jnp.where(lane < 4, mark, jnp.where(lane == 4, 1.0, 0.0)))
        keys[lines, CH:EXT] = jnp.concatenate(marks, axis=0).astype(BF16)

    put_query(0, own[...], tile)
    put_keys(0, own[...], tile)
    for k in range(1, 8):
        kv_copies[k - 1].wait_recv()
    for d in range(1, 4):
        q_copies[d - 1].wait_recv()

    def each_query(d, carry):
        put_query(d, qb[d - 1], tile_at(x + 4 - d, y, z))
        return carry

    lax.fori_loop(1, 4, each_query, 0)

    def each_key(k, carry):
        put_keys(k, kv[k - 1], tile_at(x, y + 4 - lax.div(k, 2), z + lax.rem(k, 2)))
        return carry

    lax.fori_loop(1, 8, each_key, 0)

    def attend(d):
        slot = lax.rem(4 - d, 4)
        scores[...] = lax.dot_general(queries[slot], keys[...], NT, preferred_element_type=F32)
        held = scores[...]
        largest = jnp.max(held, axis=1, keepdims=True).astype(BF16).astype(F32)
        weights = jnp.exp2(held - largest).astype(BF16)
        mixed = jnp.dot(weights, keys[...], preferred_element_type=F32)
        sent[d, :, 0:CH] = mixed[:, 0:CH].astype(BF16)
        total = mixed[:, CH + 4 : CH + 5]
        high = total.astype(BF16).astype(F32)
        notes = jnp.where(wide_lane == 4, high, 0.0)
        notes = jnp.where(wide_lane == 5, largest, notes)
        notes = jnp.where(wide_lane == 6, total - high, notes)
        sent[d, :, CH:EXT] = notes.astype(BF16)

    def part_copy(d):
        return remote(
            sent.at[d], parts.at[d], part_send.at[d], part_recv.at[d], tile_at(x + d, y, z), frame
        )

    def each_part(n, carry):
        d = 3 - n
        attend(d)

        @pl.when(d > 0)
        def _():
            part_copy(d).start()

        return carry

    lax.fori_loop(0, 4, each_part, 0)
    for d in range(3, 0, -1):
        part_copy(d).wait_recv()

    def part(d, lanes):
        return (sent[0, :, lanes] if d == 0 else parts[d, :, lanes]).astype(F32)

    tails = [part(d, pl.ds(CH, LANES)) for d in range(4)]
    maxima = [tail[:, 5:6] for tail in tails]
    most = functools.reduce(jnp.maximum, maxima)
    factors = [jnp.exp2(m - most) for m in maxima]
    denominator = sum((t[:, 4:5] + t[:, 6:7]) * f for t, f in zip(tails, factors))
    numerator = sum(part(d, pl.ds(0, CH)) * factors[d] for d in range(4))
    averaged = (numerator / denominator).astype(BF16)
    mixed = jnp.dot(averaged, triple_weight[:, 2 * CH : 3 * CH], preferred_element_type=F32)
    mixed = (mixed + triple_bias[:, 2 * CH : 3 * CH]).astype(BF16)
    attended = jnp.dot(mixed, output_weight[...], preferred_element_type=F32)
    total = own[...].astype(F32) + attended + output_bias[...]
    rows = []
    for r in range(ROWS):
        rows.append(
            jnp.where(column < widths[first + r], total[r * COLS : (r + 1) * COLS], 0.0)
        )
    rim[...] = jnp.concatenate(rows, axis=0).astype(BF16)
    up = remote(rim.at[pl.ds(0, WIDE)], bot, halo_send.at[0], halo_recv.at[0], tile - 1, frame)
    down = remote(rim.at[pl.ds(LAST, WIDE)], top, halo_send.at[1], halo_recv.at[1], tile + 1, frame)

    @pl.when(above)
    def _():
        up.start()

    @pl.when(below)
    def _():
        down.start()

    result[...] = rim[...]
    for copy in kv_copies + q_copies:
        copy.wait_send()
    for d in range(3, 0, -1):
        part_copy(d).wait_send()

    @pl.when(below)
    def _():
        up.wait_recv()
        result_bot[...] = bot[...]
        down.wait_send()

    @pl.when(above)
    def _():
        down.wait_recv()
        result_top[...] = top[...]
        up.wait_send()

    @pl.when(jnp.logical_not(below))
    def _():
        result_bot[...] = jnp.zeros((WIDE, CH), BF16)

    @pl.when(jnp.logical_not(above))
    def _():
        result_top[...] = jnp.zeros((WIDE, CH), BF16)


def upsample_kernel(labels, widths, main, top, bot, weight, bias, out, taps, ends, low, high):
    first = lax.axis_index("tile") * ROWS + 1

    def product(k, carry):
        taps[k, :, 0:OUT] = jnp.dot(main[...], weight[k], preferred_element_type=F32)
        return carry

    lax.fori_loop(0, 9, product, 0)
    for e in range(3):
        ends[e, :, 0:OUT] = jnp.dot(top[...], weight[e], preferred_element_type=F32)
        ends[3 + e, :, 0:OUT] = jnp.dot(bot[...], weight[6 + e], preferred_element_type=F32)
    column = lax.broadcasted_iota(jnp.int32, (COLS, 2 * LANES), 0)
    for r in range(ROWS):
        own = labels[first + r]
        lines = pl.ds(r * COLS, COLS)
        for p in range(2):
            joined = []
            other = r - 1 if p == 0 else r + 1
            alike = labels[first + other] == own
            outer = 0 if p == 0 else 2
            for e in range(3):
                if other < 0:
                    far = ends[e, WIDE - COLS :, :]
                elif other == ROWS:
                    far = ends[3 + e, :COLS, :]
                else:
                    far = taps[outer * 3 + e, pl.ds(other * COLS, COLS), :]
                near = taps[3 + e, lines, :] + taps[(2 - outer) * 3 + e, lines, :]
                joined.append(near + jnp.where(alike, far, 0.0))
            before = jnp.where(column == 0, 0.0, pltpu.roll(joined[0], 1, 0))
            after = jnp.where(column == COLS - 1, 0.0, pltpu.roll(joined[2], COLS - 1, 0))
            valid = column < widths[first + r]
            left = before + joined[1] + joined[2] + bias[...]
            right = joined[0] + joined[1] + after + bias[...]
            left = jnp.where(valid, left, 0.0)
            right = jnp.where(valid, right, 0.0)
            for half, lanes in ((low, slice(0, LANES)), (high, slice(LANES, 2 * LANES))):
                half[pl.ds(0, COLS, stride=2), :] = left[:, lanes]
                half[pl.ds(1, COLS, stride=2), :] = right[:, lanes]
            out[2 * r + p, :, 0:LANES] = low[...].astype(BF16)
            out[2 * r + p, :, LANES:OUT] = high[:, 0 : OUT - LANES].astype(BF16)


def shards(
    latents,
    row_video,
    video_cols,
    first_gain,
    first_shift,
    conv_weight,
    conv_bias,
    second_gain,
    second_shift,
    triple_weight,
    triple_bias,
    output_weight,
    output_bias,
    upsample_weight,
    upsample_bias,
):
    videos = video_cols.shape[0]
    matches = row_video[:, None] == jnp.arange(videos, dtype=jnp.int32)[None, :]
    canvas_widths = jnp.sum(jnp.where(matches, video_cols[None, :], 0), axis=1)
    labels = jnp.pad(row_video, 1, constant_values=-1)
    widths = jnp.pad(canvas_widths, 1)
    lines = jnp.tile(row_video.reshape(TILES, 1, ROWS), (1, 2, 1)).reshape(TILES * 8)
    numbers = jnp.arange(8, dtype=jnp.int32)
    both = lines[None, :] == numbers[:, None]
    upper = (jnp.arange(TILES * 8) % 8 < ROWS)[None, :]
    onehot_both = both.astype(F32)
    onehot_sum = (both & upper).astype(F32)
    onehot_sum_t = ((lines[:, None] == numbers[None, :]) & upper.T).astype(F32)
    per_group = CH // GROUPS
    line_widths = jnp.tile(canvas_widths.reshape(TILES, 1, ROWS), (1, 2, 1)).reshape(-1, 1)
    row_cells = line_widths.astype(F32) * per_group
    counts = jnp.sum(jnp.where(matches, canvas_widths[:, None], 0), axis=0) * per_group
    inverse = jnp.pad(1.0 / counts.astype(F32), (0, 8 - videos))[:, None]
    member = (
        np.arange(LANES)[:, None] == np.arange(CH)[None, :] // per_group
    ).astype(np.float32)
    tables = (onehot_sum, onehot_sum_t, onehot_both, row_cells, inverse, member, member.T)

    def line(vector):
        return vector.reshape(1, -1)

    smem = pl.BlockSpec(memory_space=pltpu.SMEM)
    vmem = pl.BlockSpec(memory_space=pltpu.VMEM)
    anywhere = pl.BlockSpec(memory_space=pl.ANY)
    dma = pltpu.SemaphoreType.DMA
    after_conv = pl.pallas_call(
        front_kernel,
        out_shape=jax.ShapeDtypeStruct((CELLS, CH), BF16),
        in_specs=[smem, smem] + [vmem] * 10 + [anywhere, vmem],
        out_specs=vmem,
        scratch_shapes=[
            pltpu.VMEM((2, CELLS, CH), BF16),
            pltpu.VMEM((3, WIDE, CH), BF16),
            pltpu.VMEM((3, WIDE, CH), BF16),
            pltpu.VMEM((TILES, 8, LANES), F32),
            pltpu.VMEM((8, CH), F32),
            pltpu.VMEM((3, 16, CH), F32),
            pltpu.VMEM((3, 6 * WIDE, 3 * CH), BF16),
            pltpu.VMEM((9, 3 * CH, CH), BF16),
            pltpu.VMEM((3, PADDED, CH), F32),
            dma((7,)),
            dma((7,)),
            dma((3,)),
            dma((2,)),
            dma((3, 2)),
            dma((3, 2)),
            dma((2,)),
            dma((2,)),
            dma,
        ],
        compiler_params=pltpu.CompilerParams(
            collective_id=0, has_side_effects=True, vmem_limit_bytes=48 * 2**20
        ),
        name="norm_conv",
    )(
        labels, widths, latents.reshape(CELLS, CH), *tables, line(first_gain), line(first_shift),
        conv_weight.reshape(9, 3 * CH, CH), line(conv_bias),
    )
    edge = jax.ShapeDtypeStruct((WIDE, CH), BF16)
    rims = pl.pallas_call(
        attention_kernel,
        out_shape=[jax.ShapeDtypeStruct((CELLS, CH), BF16), edge, edge],
        in_specs=[smem, smem] + [vmem] * 14,
        out_specs=[vmem] * 3,
        scratch_shapes=[
            pltpu.VMEM((7, CELLS, CH), BF16),
            pltpu.VMEM((3, CELLS, CH), BF16),
            pltpu.VMEM((TILES, 8, LANES), F32),
            pltpu.VMEM((8, CH), F32),
            pltpu.VMEM((16, CH), F32),
            pltpu.VMEM((KEYS, EXT), BF16),
            pltpu.VMEM((4, CELLS, EXT), BF16),
            pltpu.VMEM((CELLS, KEYS), F32),
            pltpu.VMEM((4, CELLS, EXT), BF16),
            pltpu.VMEM((4, CELLS, EXT), BF16),
            pltpu.VMEM((CELLS, CH), BF16),
            pltpu.VMEM((WIDE, CH), BF16),
            pltpu.VMEM((WIDE, CH), BF16),
            dma((7,)),
            dma((7,)),
            dma((7,)),
            dma((7,)),
            dma((3,)),
            dma((3,)),
            dma((4,)),
            dma((4,)),
            dma((2,)),
            dma((2,)),
        ],
        compiler_params=pltpu.CompilerParams(
            collective_id=1, has_side_effects=True, vmem_limit_bytes=48 * 2**20
        ),
        name="attention",
    )(
        labels, widths, after_conv, *tables, line(second_gain), line(second_shift), triple_weight,
        line(triple_bias), output_weight, line(output_bias),
    )
    wide_bias = jnp.pad(line(upsample_bias), ((0, 0), (0, 2 * LANES - OUT)))
    decoded = pl.pallas_call(
        upsample_kernel,
        out_shape=jax.ShapeDtypeStruct((2 * ROWS, 2 * COLS, OUT), BF16),
        in_specs=[smem, smem] + [vmem] * 5,
        out_specs=vmem,
        scratch_shapes=[
            pltpu.VMEM((9, CELLS, 2 * LANES), F32),
            pltpu.VMEM((6, WIDE, 2 * LANES), F32),
            pltpu.VMEM((2 * COLS, LANES), F32),
            pltpu.VMEM((2 * COLS, LANES), F32),
        ],
        compiler_params=pltpu.CompilerParams(vmem_limit_bytes=32 * 2**20),
        name="upsample",
    )(labels, widths, *rims, upsample_weight.reshape(9, CH, OUT), wide_bias)
    return decoded.reshape(2 * ROWS, 1, 2 * COLS, OUT)


def solution(mesh):
    in_specs = (P("tile", "frame", None, None),) + (P(),) * 14
    out_specs = P("tile", "frame", None, None)
    return jax.shard_map(shards, mesh=mesh, in_specs=in_specs, out_specs=out_specs, check_vma=False)
```

```python
import functools
import math

import jax
import jax.numpy as jnp
from jax import lax
from jax.experimental import pallas as pl
from jax.experimental.pallas import tpu as pltpu
from jax.sharding import PartitionSpec as P

GROUPS = 32
EPSILON = 1e-05
MASKED = -1e30
HIGHEST = lax.Precision.HIGHEST
MESH = pl.DeviceIdType.MESH
F32 = jnp.float32
BF16 = jnp.bfloat16
CH = 384
OUT = 192
ROWS = 4
COLS = 104
WIDE = 112
CELLS = ROWS * COLS
PADDED = ROWS * WIDE
LAST = CELLS - WIDE
LANES = 128
EXT = CH + LANES
TILES = 32
FRAMES = 8
KEYS = 8 * CELLS
NT = (((1,), (1,)), ((), ()))


def remote(src, dst, send_sem, recv_sem, tile, frame):
    return pltpu.make_async_remote_copy(
        src_ref=src,
        dst_ref=dst,
        send_sem=send_sem,
        recv_sem=recv_sem,
        device_id={"tile": tile, "frame": frame},
        device_id_type=MESH,
    )


def place():
    tile = lax.axis_index("tile")
    frame = lax.axis_index("frame")
    x = lax.div(tile, 8)
    y = lax.rem(lax.div(tile, 2), 4)
    z = lax.rem(tile, 2)
    return tile, frame, x, y, z


def tile_at(x, y, z):
    return lax.rem(x, 4) * 8 + lax.rem(y, 4) * 2 + lax.rem(z, 2)


def greet(barrier, tile, frame):
    pl.semaphore_signal(
        barrier, inc=1, device_id={"tile": tile, "frame": frame}, device_id_type=MESH
    )


def exact(a, b):
    return jnp.dot(a, b, precision=HIGHEST, preferred_element_type=F32)


def line_of(vector, part=None):
    held = vector[...] if part is None else vector[pl.ds(part * CH, CH)]
    return held.reshape(1, held.shape[0])


def pick(table, label):
    rows = lax.broadcasted_iota(jnp.int32, (8, CH), 0)
    chosen = rows == label
    mean = jnp.sum(jnp.where(chosen, table[0:8, :], 0.0), axis=0, keepdims=True)
    scale = jnp.sum(jnp.where(chosen, table[8:16, :], 0.0), axis=0, keepdims=True)
    return mean, scale


def members():
    per_group = CH // GROUPS
    start = lax.broadcasted_iota(jnp.int32, (LANES, CH), 0) * per_group
    channel = lax.broadcasted_iota(jnp.int32, (LANES, CH), 1)
    across = jnp.where((channel >= start) & (channel < start + per_group), 1.0, 0.0)
    start = lax.broadcasted_iota(jnp.int32, (CH, LANES), 1) * per_group
    channel = lax.broadcasted_iota(jnp.int32, (CH, LANES), 0)
    down = jnp.where((channel >= start) & (channel < start + per_group), 1.0, 0.0)
    return across, down


def local_sums(values, width_of, first, st):
    member, member_t = members()
    column = lax.broadcasted_iota(jnp.int32, (COLS, CH), 0)
    line = lax.broadcasted_iota(jnp.int32, (8, 1), 0)
    per_row = jnp.ones((8, 1), F32)
    for r in range(ROWS):
        width = width_of(first + r)
        mask = column < width
        cells = values[r * COLS : (r + 1) * COLS]
        total = jnp.sum(jnp.where(mask, cells, 0.0), axis=0, keepdims=True)
        mean = total / width.astype(F32)
        apart = jnp.where(mask, cells - mean, 0.0)
        st[r : r + 1, :] = total
        st[ROWS + r : ROWS + r + 1, :] = jnp.sum(apart * apart, axis=0, keepdims=True)
        per_row = jnp.where((line == r) | (line == ROWS + r), width.astype(F32), per_row)
    upper = line < ROWS
    held = st[...]
    grouped = exact(held, member_t)
    group_mean = exact(jnp.where(upper, grouped / (per_row * (CH // GROUPS)), 0.0), member)
    spread = jnp.where(upper, held / per_row - group_mean, 0.0)
    extra = exact(per_row * spread * spread, member_t)
    lower = pltpu.roll(extra, ROWS, 0)
    return jnp.where(upper, grouped, grouped + lower)


def combine_sums(gat, onehot, row_cells):
    member, _ = members()
    held = gat.reshape(TILES * 8, LANES)
    upper = lax.rem(lax.broadcasted_iota(jnp.int32, (TILES * 8, LANES), 0), 8) < ROWS
    by_video = jnp.transpose(onehot)[0:8]
    counts = exact(by_video, jnp.where(upper, row_cells, 0.0))
    inverse = jnp.where(counts > 0.0, 1.0 / counts, 0.0)
    mean = exact(by_video, jnp.where(upper, held, 0.0)) * inverse
    mean_rows = exact(onehot[:, 0:8], mean)
    off = held / row_cells - mean_rows
    spread = jnp.where(upper, row_cells * off * off, held)
    variance = exact(by_video, spread) * inverse
    scale = lax.rsqrt(variance + EPSILON)
    return exact(mean, member), exact(scale, member)


def whole_kernel(
    videos, cols, lat_hbm, first_gain, first_shift, conv_hbm, conv_bias, second_gain, second_shift,
    triple_weight, triple_bias, output_weight, output_bias, up_weight, up_bias, out,
    lat, main, top, bot, gat, onehot, row_cells, st, tabs, hid, weight, acc,
    own, kv, qb, tab, keys, queries, scores, sent, parts, rim, rim_top, rim_bot,
    taps, ends, low, high, wide_bias,
    stat_send, stat_recv, main_send, main_recv, halo_send, halo_recv, tab_send, tab_recv,
    load_sem, kv_send, kv_recv, q_send, q_recv, part_send, part_recv, rim_send, rim_recv,
):
    tile, frame, x, y, z = place()
    first = tile * ROWS
    load_lat = pltpu.make_async_copy(lat_hbm, lat, load_sem.at[0])
    load_lat.start()
    load = pltpu.make_async_copy(conv_hbm, weight, load_sem.at[1])
    load.start()

    def label_of(row):
        inside = (row >= 0) & (row < TILES * ROWS)
        return jnp.where(inside, videos[jnp.clip(row, 0, TILES * ROWS - 1)], -1)

    def width_of(row):
        inside = (row >= 0) & (row < TILES * ROWS)
        return jnp.where(inside, cols[videos[jnp.clip(row, 0, TILES * ROWS - 1)]], 0)

    barrier = pltpu.get_barrier_semaphore()

    def greet_tile(d, carry):
        greet(barrier, lax.rem(tile + d, TILES), frame)
        return carry

    lax.fori_loop(1, TILES, greet_tile, 0)
    awaited = TILES - 1
    for step in (-2, -1, 1, 2):
        there = (frame + step >= 0) & (frame + step < FRAMES)

        @pl.when(there)
        def _():
            greet(barrier, tile, frame + step)

        awaited = awaited + there.astype(jnp.int32)

    slot_line = lax.rem(lax.broadcasted_iota(jnp.int32, (8, LANES), 0), ROWS)
    slot_lane = lax.broadcasted_iota(jnp.int32, (8, LANES), 1)

    def fill(t, carry):
        label = jnp.full((8, LANES), -1, jnp.int32)
        width = jnp.zeros((8, LANES), jnp.int32)
        for r in range(ROWS):
            number = videos[t * ROWS + r]
            label = jnp.where(slot_line == r, number, label)
            width = jnp.where(slot_line == r, cols[number], width)
        lines = pl.ds(pl.multiple_of(t * 8, 8), 8)
        onehot[lines, :] = jnp.where(label == slot_lane, 1.0, 0.0)
        row_cells[lines, :] = width.astype(F32) * (CH // GROUPS)
        return carry

    lax.fori_loop(0, TILES, fill, 0)
    wide_bias[...] = jnp.zeros((1, 2 * LANES), F32)
    wide_bias[:, 0:OUT] = line_of(up_bias)
    load_lat.wait()
    source = lat[...].astype(F32)
    gat[0, tile] = local_sums(source, width_of, first, st)
    pl.semaphore_wait(barrier, awaited)

    def sum_copy(which, d):
        peer = lax.rem(tile + d, TILES)
        return remote(
            gat.at[which, tile], gat.at[which, tile], stat_send.at[which], stat_recv.at[which],
            peer, frame,
        )

    def send_sums(which):
        def one(d, carry):
            sum_copy(which, d).start()
            return carry

        lax.fori_loop(1, TILES, one, 0)

    def all_sums(which):
        others = pl.ds(0, TILES - 1)
        return remote(
            gat.at[which, others], gat.at[which, others], stat_send.at[which],
            stat_recv.at[which], lax.rem(tile + 1, TILES), frame,
        )

    send_sums(0)

    even = lax.rem(frame, 2) == 0
    next_frame = frame + 1 < FRAMES
    skip_frame = even & (frame + 2 < FRAMES)
    relay = even & (frame >= 2)
    has = {1: frame >= 1, 0: frame >= 2}
    above = tile >= 1
    below = tile + 1 < TILES

    to_next = remote(lat, main.at[1], main_send.at[1], main_recv.at[1], tile, frame + 1)
    to_skip = remote(lat, main.at[0], main_send.at[0], main_recv.at[0], tile, frame + 2)
    to_relay = remote(main.at[1], main.at[0], main_send.at[2], main_recv.at[0], tile, frame + 1)

    def halo(a):
        src = lat if a == 2 else main.at[a]
        up = remote(
            src.at[pl.ds(0, WIDE)], bot.at[a], halo_send.at[a, 0], halo_recv.at[a, 0],
            tile - 1, frame,
        )
        down = remote(
            src.at[pl.ds(LAST, WIDE)], top.at[a], halo_send.at[a, 1], halo_recv.at[a, 1],
            tile + 1, frame,
        )
        return up, down

    def start_halo(a):
        up, down = halo(a)

        @pl.when(above)
        def _():
            up.start()

        @pl.when(below)
        def _():
            down.start()

    def wait_halo(a):
        up, down = halo(a)

        @pl.when(below)
        def _():
            up.wait_recv()

        @pl.when(above)
        def _():
            down.wait_recv()

    def end_halo(a):
        up, down = halo(a)

        @pl.when(above)
        def _():
            up.wait_send()

        @pl.when(below)
        def _():
            down.wait_send()

    @pl.when(next_frame)
    def _():
        to_next.start()

    start_halo(2)

    all_sums(0).wait_recv()

    @pl.when(skip_frame)
    def _():
        to_skip.start()

    mean, scale = combine_sums(gat[0], onehot[...], row_cells[...])
    tabs[2, 0:8, :] = mean
    tabs[2, 8:16, :] = scale
    tab_next = remote(tabs.at[2], tabs.at[1], tab_send.at[1], tab_recv.at[1], tile, frame + 1)
    tab_skip = remote(tabs.at[2], tabs.at[0], tab_send.at[0], tab_recv.at[0], tile, frame + 2)

    @pl.when(next_frame)
    def _():
        tab_next.start()

    @pl.when(frame + 2 < FRAMES)
    def _():
        tab_skip.start()

    column = lax.broadcasted_iota(jnp.int32, (COLS, CH), 0)

    def activate(a, row, cells):
        label = label_of(first - 1 + row)
        width = width_of(first - 1 + row)
        row_mean, row_scale = pick(tabs[a], label)
        normed = (cells - row_mean) * row_scale * line_of(first_gain) + line_of(first_shift)
        hidden = normed / (1.0 + jnp.exp(-normed))
        hidden = jnp.where(column < width, hidden, 0.0)
        hidden = jnp.concatenate([hidden, jnp.zeros((WIDE - COLS, CH), F32)], axis=0)
        lines = pl.ds(row * WIDE, WIDE)
        hid[a, lines, 0:CH] = pltpu.roll(hidden, 1, 0).astype(BF16)
        hid[a, lines, CH : 2 * CH] = hidden.astype(BF16)
        hid[a, lines, 2 * CH : 3 * CH] = pltpu.roll(hidden, WIDE - 1, 0).astype(BF16)

    def activate_main(a):
        cells = lat[...].astype(F32) if a == 2 else main[a].astype(F32)
        for r in range(ROWS):
            activate(a, r + 1, cells[r * COLS : (r + 1) * COLS])

    def activate_halo(a):
        activate(a, 0, top[a].astype(F32)[WIDE - COLS :])
        activate(a, ROWS + 1, bot[a].astype(F32)[:COLS])

    def convolve(a):
        def tap(b, carry):
            lines = pl.ds(pl.multiple_of(b * WIDE, 16), PADDED)
            product = jnp.dot(hid[a, lines, :], weight[a * 3 + b], preferred_element_type=F32)
            if a == 2:
                acc[b] = product
            else:
                acc[b] = acc[b] + product
            return carry

        lax.fori_loop(0, 3, tap, 0)

    activate_main(2)
    wait_halo(2)
    activate_halo(2)
    load.wait()
    convolve(2)

    @pl.when(has[1])
    def _():
        to_next.wait_recv()

    @pl.when(relay)
    def _():
        to_relay.start()

    @pl.when(has[1])
    def _():
        start_halo(1)
        tab_next.wait_recv()
        activate_main(1)

    @pl.when(has[0])
    def _():
        to_skip.wait_recv()
        start_halo(0)

    @pl.when(has[1])
    def _():
        wait_halo(1)
        activate_halo(1)
        convolve(1)

    @pl.when(has[0])
    def _():
        tab_skip.wait_recv()
        activate_main(0)
        wait_halo(0)
        activate_halo(0)
        convolve(0)

    source = lat[...].astype(F32)
    rows = []
    for r in range(ROWS):
        label = label_of(first + r)
        lines = pl.ds(r * WIDE, COLS)
        total = acc[1, lines, :]
        total = total + jnp.where(label_of(first + r - 1) == label, acc[0, lines, :], 0.0)
        total = total + jnp.where(label_of(first + r + 1) == label, acc[2, lines, :], 0.0)
        total = source[r * COLS : (r + 1) * COLS] + total + line_of(conv_bias)
        rows.append(jnp.where(column < width_of(first + r), total, 0.0))
    own[...] = jnp.concatenate(rows, axis=0).astype(BF16)

    source = own[...].astype(F32)
    gat[1, tile] = local_sums(source, width_of, first, st)
    send_sums(1)

    half = CELLS // 2
    upper_half, lower_half = pl.ds(0, half), pl.ds(half, half)
    ahead, behind, across = tile_at(x, y + 1, z), tile_at(x, y + 3, z), tile_at(x, y, z + 1)

    def pass_on(k, src, slot, peer, lines=None):
        dst = kv.at[slot]
        if lines is not None:
            src, dst = src.at[lines], dst.at[lines]
        return remote(src, dst, kv_send.at[k], kv_recv.at[k], peer, frame)

    kv_across = pass_on(0, own, 4, across)
    kv_copies = [kv_across]
    relays = []
    for zz in range(2):
        base = own if zz == 0 else kv.at[4]
        near = (pass_on(1 + 4 * zz, base, zz * 4 + 1, ahead),
                pass_on(2 + 4 * zz, base, zz * 4 + 3, behind))
        far = (pass_on(3 + 4 * zz, kv.at[zz * 4 + 1], zz * 4 + 2, ahead, upper_half),
               pass_on(4 + 4 * zz, kv.at[zz * 4 + 3], zz * 4 + 2, behind, lower_half))
        relays.append((near, far))
        kv_copies += list(near) + list(far)
    q_copies = []
    for d in range(1, 4):
        peer = tile_at(x + d, y, z)
        q_copies.append(remote(own, qb.at[d - 1], q_send.at[d - 1], q_recv.at[d - 1], peer, frame))
    kv_across.start()
    for copy in relays[0][0]:
        copy.start()
    for copy in q_copies:
        copy.start()
    kv_across.wait_recv()
    for copy in relays[1][0]:
        copy.start()
    all_sums(1).wait_recv()
    mean, scale = combine_sums(gat[1], onehot[...], row_cells[...])
    tab[0:8, :] = mean
    tab[8:16, :] = scale
    column = lax.broadcasted_iota(jnp.int32, (COLS, CH), 0)
    cell_column = lax.broadcasted_iota(jnp.int32, (COLS, LANES), 0)
    lane = lax.broadcasted_iota(jnp.int32, (COLS, LANES), 1)
    wide_lane = lax.broadcasted_iota(jnp.int32, (CELLS, LANES), 1)
    to_exponent = CH ** (-0.5) * math.log2(math.e)

    def normalise(block, block_tile):
        cells = block.astype(F32)
        rows = []
        for r in range(ROWS):
            at = block_tile * ROWS + r
            row_mean, row_scale = pick(tab, label_of(at))
            part = cells[r * COLS : (r + 1) * COLS]
            normed = (part - row_mean) * row_scale * line_of(second_gain) + line_of(second_shift)
            rows.append(jnp.where(column < width_of(at), normed, 0.0))
        return jnp.concatenate(rows, axis=0).astype(BF16)

    def put_query(slot, block, block_tile):
        normed = normalise(block, block_tile)
        plain = jnp.dot(normed, triple_weight[:, 0:CH], preferred_element_type=F32)
        plain = (plain + line_of(triple_bias, 0)).astype(BF16)
        turned = lax.dot_general(
            plain, triple_weight[:, CH : 2 * CH], NT, preferred_element_type=F32
        )
        constant = jnp.sum(
            plain.astype(F32) * line_of(triple_bias, 1), axis=1, keepdims=True
        )
        queries[slot, :, 0:CH] = (turned * to_exponent).astype(BF16)
        marks = []
        for r in range(ROWS):
            label = label_of(block_tile * ROWS + r)
            marks.append(jnp.where(lane == label, 1.0, 0.0))
        marks = jnp.concatenate(marks, axis=0)
        marks = jnp.where(wide_lane == 4, constant * to_exponent, marks)
        queries[slot, :, CH:EXT] = marks.astype(BF16)

    def put_keys(slot, block, block_tile):
        lines = pl.ds(pl.multiple_of(slot * CELLS, 16), CELLS)
        keys[lines, 0:CH] = normalise(block, block_tile)
        marks = []
        for r in range(ROWS):
            at = block_tile * ROWS + r
            seen = (lane == label_of(at)) & (cell_column < width_of(at))
            mark = jnp.where(seen, 0.0, MASKED)
            marks.append(jnp.where(lane < 4, mark, jnp.where(lane == 4, 1.0, 0.0)))
        keys[lines, CH:EXT] = jnp.concatenate(marks, axis=0).astype(BF16)

    def key_tile(slot):
        return tile_at(x, y + 4 - lax.rem(slot, 4), z + lax.div(slot, 4))

    put_query(0, own[...], tile)
    put_keys(0, own[...], tile)
    for copy in relays[0][0]:
        copy.wait_recv()
    for copy in relays[0][1]:
        copy.start()
    put_keys(4, kv[4], across)
    for d in range(1, 4):
        q_copies[d - 1].wait_recv()

    def each_query(d, carry):
        put_query(d, qb[d - 1], tile_at(x + 4 - d, y, z))
        return carry

    lax.fori_loop(1, 4, each_query, 0)

    def put_pair(low_slot):
        def each_key(n, carry):
            slot = low_slot + 2 * n
            put_keys(slot, kv[slot], key_tile(slot))
            return carry

        lax.fori_loop(0, 2, each_key, 0)

    put_pair(1)
    for copy in relays[1][0]:
        copy.wait_recv()
    for copy in relays[1][1]:
        copy.start()
    put_pair(5)
    for zz in range(2):
        for copy in relays[zz][1]:
            copy.wait_recv()
        put_keys(zz * 4 + 2, kv[zz * 4 + 2], key_tile(jnp.int32(zz * 4 + 2)))

    def attend(d):
        slot = lax.rem(4 - d, 4)
        scores[...] = lax.dot_general(queries[slot], keys[...], NT, preferred_element_type=F32)
        held = scores[...]
        largest = jnp.max(held, axis=1, keepdims=True).astype(BF16).astype(F32)
        weights = jnp.exp2(held - largest).astype(BF16)
        mixed = jnp.dot(weights, keys[...], preferred_element_type=F32)
        sent[d, :, 0:CH] = mixed[:, 0:CH].astype(BF16)
        total = mixed[:, CH + 4 : CH + 5]
        high = total.astype(BF16).astype(F32)
        notes = jnp.where(wide_lane == 4, high, 0.0)
        notes = jnp.where(wide_lane == 5, largest, notes)
        notes = jnp.where(wide_lane == 6, total - high, notes)
        sent[d, :, CH:EXT] = notes.astype(BF16)

    def part_copy(d):
        return remote(
            sent.at[d], parts.at[d], part_send.at[d], part_recv.at[d], tile_at(x + d, y, z), frame
        )

    def each_part(n, carry):
        d = 3 - n
        attend(d)

        @pl.when(d > 0)
        def _():
            part_copy(d).start()

        return carry

    lax.fori_loop(0, 4, each_part, 0)
    for d in range(3, 0, -1):
        part_copy(d).wait_recv()

    def part(d, lanes):
        return (sent[0, :, lanes] if d == 0 else parts[d, :, lanes]).astype(F32)

    tails = [part(d, pl.ds(CH, LANES)) for d in range(4)]
    maxima = [tail[:, 5:6] for tail in tails]
    most = functools.reduce(jnp.maximum, maxima)
    factors = [jnp.exp2(m - most) for m in maxima]
    denominator = sum((t[:, 4:5] + t[:, 6:7]) * f for t, f in zip(tails, factors))
    numerator = sum(part(d, pl.ds(0, CH)) * factors[d] for d in range(4))
    averaged = (numerator / denominator).astype(BF16)
    mixed = jnp.dot(averaged, triple_weight[:, 2 * CH : 3 * CH], preferred_element_type=F32)
    mixed = (mixed + line_of(triple_bias, 2)).astype(BF16)
    attended = jnp.dot(mixed, output_weight[...], preferred_element_type=F32)
    total = own[...].astype(F32) + attended + line_of(output_bias)
    rows = []
    for r in range(ROWS):
        rows.append(
            jnp.where(column < width_of(first + r), total[r * COLS : (r + 1) * COLS], 0.0)
        )
    rim[...] = jnp.concatenate(rows, axis=0).astype(BF16)
    up = remote(
        rim.at[pl.ds(0, WIDE)], rim_bot, rim_send.at[0], rim_recv.at[0], tile - 1, frame
    )
    down = remote(
        rim.at[pl.ds(LAST, WIDE)], rim_top, rim_send.at[1], rim_recv.at[1], tile + 1, frame
    )

    @pl.when(above)
    def _():
        up.start()

    @pl.when(below)
    def _():
        down.start()

    def product(k, carry):
        taps[k, :, 0:OUT] = lax.dot_general(
            rim[...], up_weight[k], NT, preferred_element_type=F32
        )
        return carry

    lax.fori_loop(0, 9, product, 0)

    @pl.when(below)
    def _():
        up.wait_recv()
        down.wait_send()

    @pl.when(above)
    def _():
        down.wait_recv()
        up.wait_send()

    for e in range(3):
        ends[e, :, 0:OUT] = lax.dot_general(
            rim_top[...], up_weight[e], NT, preferred_element_type=F32
        )
        ends[3 + e, :, 0:OUT] = lax.dot_general(
            rim_bot[...], up_weight[6 + e], NT, preferred_element_type=F32
        )
    up_column = lax.broadcasted_iota(jnp.int32, (COLS, 2 * LANES), 0)
    for r in range(ROWS):
        label = label_of(first + r)
        lines = pl.ds(r * COLS, COLS)
        for p in range(2):
            joined = []
            other = r - 1 if p == 0 else r + 1
            alike = label_of(first + other) == label
            outer = 0 if p == 0 else 2
            for e in range(3):
                if other < 0:
                    far = ends[e, WIDE - COLS :, :]
                elif other == ROWS:
                    far = ends[3 + e, :COLS, :]
                else:
                    far = taps[outer * 3 + e, pl.ds(other * COLS, COLS), :]
                near = taps[3 + e, lines, :] + taps[(2 - outer) * 3 + e, lines, :]
                joined.append(near + jnp.where(alike, far, 0.0))
            before = jnp.where(up_column == 0, 0.0, pltpu.roll(joined[0], 1, 0))
            after = jnp.where(up_column == COLS - 1, 0.0, pltpu.roll(joined[2], COLS - 1, 0))
            valid = up_column < width_of(first + r)
            left = before + joined[1] + joined[2] + wide_bias[...]
            right = joined[0] + joined[1] + after + wide_bias[...]
            left = jnp.where(valid, left, 0.0)
            right = jnp.where(valid, right, 0.0)
            for half, lanes in ((low, slice(0, LANES)), (high, slice(LANES, 2 * LANES))):
                half[pl.ds(0, COLS, stride=2), :] = left[:, lanes]
                half[pl.ds(1, COLS, stride=2), :] = right[:, lanes]
            out[2 * r + p, :, 0:LANES] = low[...].astype(BF16)
            out[2 * r + p, :, LANES:OUT] = high[:, 0 : OUT - LANES].astype(BF16)

    @pl.when(next_frame)
    def _():
        to_next.wait_send()
        tab_next.wait_send()

    @pl.when(frame + 2 < FRAMES)
    def _():
        tab_skip.wait_send()

    @pl.when(skip_frame)
    def _():
        to_skip.wait_send()

    @pl.when(relay)
    def _():
        to_relay.wait_send()

    end_halo(2)

    @pl.when(has[1])
    def _():
        end_halo(1)

    @pl.when(has[0])
    def _():
        end_halo(0)
    all_sums(0).wait_send()
    all_sums(1).wait_send()
    for copy in kv_copies + q_copies:
        copy.wait_send()
    for d in range(3, 0, -1):
        part_copy(d).wait_send()


def shards(
    latents,
    row_video,
    video_cols,
    first_gain,
    first_shift,
    conv_weight,
    conv_bias,
    second_gain,
    second_shift,
    triple_weight,
    triple_bias,
    output_weight,
    output_bias,
    upsample_weight,
    upsample_bias,
):
    smem = pl.BlockSpec(memory_space=pltpu.SMEM)
    vmem = pl.BlockSpec(memory_space=pltpu.VMEM)
    anywhere = pl.BlockSpec(memory_space=pl.ANY)
    dma = pltpu.SemaphoreType.DMA
    block = (CELLS, CH)
    edge = (WIDE, CH)
    decoded = pl.pallas_call(
        whole_kernel,
        out_shape=jax.ShapeDtypeStruct((2 * ROWS, 2 * COLS, OUT), BF16),
        in_specs=[smem, smem, anywhere, vmem, vmem, anywhere] + [vmem] * 9,
        out_specs=vmem,
        scratch_shapes=[
            pltpu.VMEM(block, BF16),
            pltpu.VMEM((2,) + block, BF16),
            pltpu.VMEM((3,) + edge, BF16),
            pltpu.VMEM((3,) + edge, BF16),
            pltpu.VMEM((2, TILES, 8, LANES), F32),
            pltpu.VMEM((TILES * 8, LANES), F32),
            pltpu.VMEM((TILES * 8, LANES), F32),
            pltpu.VMEM((8, CH), F32),
            pltpu.VMEM((3, 16, CH), F32),
            pltpu.VMEM((3, 6 * WIDE, 3 * CH), BF16),
            pltpu.VMEM((9, 3 * CH, CH), BF16),
            pltpu.VMEM((3, PADDED, CH), F32),
            pltpu.VMEM(block, BF16),
            pltpu.VMEM((8,) + block, BF16),
            pltpu.VMEM((3,) + block, BF16),
            pltpu.VMEM((16, CH), F32),
            pltpu.VMEM((KEYS, EXT), BF16),
            pltpu.VMEM((4, CELLS, EXT), BF16),
            pltpu.VMEM((CELLS, KEYS), F32),
            pltpu.VMEM((4, CELLS, EXT), BF16),
            pltpu.VMEM((4, CELLS, EXT), BF16),
            pltpu.VMEM(block, BF16),
            pltpu.VMEM(edge, BF16),
            pltpu.VMEM(edge, BF16),
            pltpu.VMEM((9, CELLS, 2 * LANES), F32),
            pltpu.VMEM((6, WIDE, 2 * LANES), F32),
            pltpu.VMEM((2 * COLS, LANES), F32),
            pltpu.VMEM((2 * COLS, LANES), F32),
            pltpu.VMEM((1, 2 * LANES), F32),
            dma((2,)),
            dma((2,)),
            dma((3,)),
            dma((2,)),
            dma((3, 2)),
            dma((3, 2)),
            dma((2,)),
            dma((2,)),
            dma((2,)),
            dma((9,)),
            dma((9,)),
            dma((3,)),
            dma((3,)),
            dma((4,)),
            dma((4,)),
            dma((2,)),
            dma((2,)),
        ],
        compiler_params=pltpu.CompilerParams(
            collective_id=0, has_side_effects=True, vmem_limit_bytes=56 * 2**20
        ),
        name="decoder_window",
    )(
        row_video, video_cols, latents.reshape(CELLS, CH), first_gain, first_shift,
        conv_weight.reshape(9, 3 * CH, CH), conv_bias, second_gain, second_shift, triple_weight,
        triple_bias, output_weight, output_bias,
        jnp.transpose(upsample_weight, (0, 1, 3, 2)).reshape(9, OUT, CH), upsample_bias,
    )
    return decoded.reshape(2 * ROWS, 1, 2 * COLS, OUT)


def solution(mesh):
    in_specs = (P("tile", "frame", None, None),) + (P(),) * 14
    out_specs = P("tile", "frame", None, None)
    return jax.shard_map(shards, mesh=mesh, in_specs=in_specs, out_specs=out_specs, check_vma=False)
```

```python
import functools
import math

import jax
import jax.numpy as jnp
from jax import lax
from jax.experimental import pallas as pl
from jax.experimental.pallas import tpu as pltpu
from jax.sharding import PartitionSpec as P

GROUPS = 32
EPSILON = 1e-05
MASKED = -1e30
HIGHEST = lax.Precision.HIGHEST
MESH = pl.DeviceIdType.MESH
F32 = jnp.float32
BF16 = jnp.bfloat16
CH = 384
OUT = 192
ROWS = 4
COLS = 104
WIDE = 112
CELLS = ROWS * COLS
PADDED = ROWS * WIDE
LAST = CELLS - WIDE
LANES = 128
EXT = CH + LANES
TILES = 32
FRAMES = 8
KEYS = 8 * CELLS
NT = (((1,), (1,)), ((), ()))


def remote(src, dst, send_sem, recv_sem, tile, frame):
    return pltpu.make_async_remote_copy(
        src_ref=src,
        dst_ref=dst,
        send_sem=send_sem,
        recv_sem=recv_sem,
        device_id={"tile": tile, "frame": frame},
        device_id_type=MESH,
    )


def place():
    tile = lax.axis_index("tile")
    frame = lax.axis_index("frame")
    x = lax.div(tile, 8)
    y = lax.rem(lax.div(tile, 2), 4)
    z = lax.rem(tile, 2)
    return tile, frame, x, y, z


def tile_at(x, y, z):
    return lax.rem(x, 4) * 8 + lax.rem(y, 4) * 2 + lax.rem(z, 2)


def greet(barrier, tile, frame):
    pl.semaphore_signal(
        barrier, inc=1, device_id={"tile": tile, "frame": frame}, device_id_type=MESH
    )


def exact(a, b):
    return jnp.dot(a, b, precision=HIGHEST, preferred_element_type=F32)


def line_of(vector, part=None):
    held = vector[...] if part is None else vector[pl.ds(part * CH, CH)]
    return held.reshape(1, held.shape[0])


def pick(table, label):
    rows = lax.broadcasted_iota(jnp.int32, (8, CH), 0)
    chosen = rows == label
    mean = jnp.sum(jnp.where(chosen, table[0:8, :], 0.0), axis=0, keepdims=True)
    scale = jnp.sum(jnp.where(chosen, table[8:16, :], 0.0), axis=0, keepdims=True)
    return mean, scale


def members():
    per_group = CH // GROUPS
    start = lax.broadcasted_iota(jnp.int32, (LANES, CH), 0) * per_group
    channel = lax.broadcasted_iota(jnp.int32, (LANES, CH), 1)
    across = jnp.where((channel >= start) & (channel < start + per_group), 1.0, 0.0)
    start = lax.broadcasted_iota(jnp.int32, (CH, LANES), 1) * per_group
    channel = lax.broadcasted_iota(jnp.int32, (CH, LANES), 0)
    down = jnp.where((channel >= start) & (channel < start + per_group), 1.0, 0.0)
    return across, down


def local_sums(values, width_of, first, st):
    member, member_t = members()
    column = lax.broadcasted_iota(jnp.int32, (COLS, CH), 0)
    line = lax.broadcasted_iota(jnp.int32, (8, 1), 0)
    per_row = jnp.ones((8, 1), F32)
    for r in range(ROWS):
        width = width_of(first + r)
        mask = column < width
        cells = values[r * COLS : (r + 1) * COLS]
        total = jnp.sum(jnp.where(mask, cells, 0.0), axis=0, keepdims=True)
        mean = total / width.astype(F32)
        apart = jnp.where(mask, cells - mean, 0.0)
        st[r : r + 1, :] = total
        st[ROWS + r : ROWS + r + 1, :] = jnp.sum(apart * apart, axis=0, keepdims=True)
        per_row = jnp.where((line == r) | (line == ROWS + r), width.astype(F32), per_row)
    upper = line < ROWS
    held = st[...]
    grouped = exact(held, member_t)
    group_mean = exact(jnp.where(upper, grouped / (per_row * (CH // GROUPS)), 0.0), member)
    spread = jnp.where(upper, held / per_row - group_mean, 0.0)
    extra = exact(per_row * spread * spread, member_t)
    lower = pltpu.roll(extra, ROWS, 0)
    return jnp.where(upper, grouped, grouped + lower)


def combine_sums(gat, onehot, row_cells):
    member, _ = members()
    held = gat.reshape(TILES * 8, LANES)
    upper = lax.rem(lax.broadcasted_iota(jnp.int32, (TILES * 8, LANES), 0), 8) < ROWS
    by_video = jnp.transpose(onehot)[0:8]
    counts = exact(by_video, jnp.where(upper, row_cells, 0.0))
    inverse = jnp.where(counts > 0.0, 1.0 / counts, 0.0)
    mean = exact(by_video, jnp.where(upper, held, 0.0)) * inverse
    mean_rows = exact(onehot[:, 0:8], mean)
    off = held / row_cells - mean_rows
    spread = jnp.where(upper, row_cells * off * off, held)
    variance = exact(by_video, spread) * inverse
    scale = lax.rsqrt(variance + EPSILON)
    return exact(mean, member), exact(scale, member)


def whole_kernel(
    videos, cols, lat_hbm, first_gain, first_shift, conv_hbm, conv_bias, second_gain, second_shift,
    triple_weight, triple_bias, output_weight, output_bias, up_weight, up_bias, out,
    lat, main, top, bot, gat, onehot, row_cells, st, tabs, hid, weight, acc,
    own, kv, qb, tab, keys, queries, scores, sent, parts, sent_notes, part_notes, rim, rim_top, rim_bot,
    taps, ends, low, high, wide_bias,
    stat_send, stat_recv, main_send, main_recv, halo_send, halo_recv, tab_send, tab_recv,
    load_sem, kv_send, kv_recv, q_send, q_recv, part_send, part_recv, note_send, note_recv,
    rim_send, rim_recv,
):
    tile, frame, x, y, z = place()
    first = tile * ROWS
    load_lat = pltpu.make_async_copy(lat_hbm, lat, load_sem.at[0])
    load_lat.start()
    load = pltpu.make_async_copy(conv_hbm, weight, load_sem.at[1])
    load.start()

    def label_of(row):
        inside = (row >= 0) & (row < TILES * ROWS)
        return jnp.where(inside, videos[jnp.clip(row, 0, TILES * ROWS - 1)], -1)

    def width_of(row):
        inside = (row >= 0) & (row < TILES * ROWS)
        return jnp.where(inside, cols[videos[jnp.clip(row, 0, TILES * ROWS - 1)]], 0)

    barrier = pltpu.get_barrier_semaphore()

    def greet_tile(d, carry):
        greet(barrier, lax.rem(tile + d, TILES), frame)
        return carry

    lax.fori_loop(1, TILES, greet_tile, 0)
    awaited = TILES - 1
    for step in (-2, -1, 1, 2):
        there = (frame + step >= 0) & (frame + step < FRAMES)

        @pl.when(there)
        def _():
            greet(barrier, tile, frame + step)

        awaited = awaited + there.astype(jnp.int32)

    partner = frame + 1 - 2 * lax.rem(frame, 2)
    for step in (-1, 1):
        there = (tile + step >= 0) & (tile + step < TILES)

        @pl.when(there)
        def _():
            greet(barrier, tile + step, partner)

        awaited = awaited + there.astype(jnp.int32)

    slot_line = lax.rem(lax.broadcasted_iota(jnp.int32, (8, LANES), 0), ROWS)
    slot_lane = lax.broadcasted_iota(jnp.int32, (8, LANES), 1)

    def fill(t, carry):
        label = jnp.full((8, LANES), -1, jnp.int32)
        width = jnp.zeros((8, LANES), jnp.int32)
        for r in range(ROWS):
            number = videos[t * ROWS + r]
            label = jnp.where(slot_line == r, number, label)
            width = jnp.where(slot_line == r, cols[number], width)
        lines = pl.ds(pl.multiple_of(t * 8, 8), 8)
        onehot[lines, :] = jnp.where(label == slot_lane, 1.0, 0.0)
        row_cells[lines, :] = width.astype(F32) * (CH // GROUPS)
        return carry

    lax.fori_loop(0, TILES, fill, 0)
    wide_bias[...] = jnp.zeros((1, 2 * LANES), F32)
    wide_bias[:, 0:OUT] = line_of(up_bias)
    load_lat.wait()
    source = lat[...].astype(F32)
    gat[0, tile] = local_sums(source, width_of, first, st)
    pl.semaphore_wait(barrier, awaited)

    def sum_copy(which, d):
        peer = lax.rem(tile + d, TILES)
        return remote(
            gat.at[which, tile], gat.at[which, tile], stat_send.at[which], stat_recv.at[which],
            peer, frame,
        )

    def send_sums(which):
        def one(d, carry):
            sum_copy(which, d).start()
            return carry

        lax.fori_loop(1, TILES, one, 0)

    def all_sums(which):
        others = pl.ds(0, TILES - 1)
        return remote(
            gat.at[which, others], gat.at[which, others], stat_send.at[which],
            stat_recv.at[which], lax.rem(tile + 1, TILES), frame,
        )

    send_sums(0)

    even = lax.rem(frame, 2) == 0
    next_frame = frame + 1 < FRAMES
    skip_frame = even & (frame + 2 < FRAMES)
    relay = even & (frame >= 2)
    has = {1: frame >= 1, 0: frame >= 2}
    above = tile >= 1
    below = tile + 1 < TILES

    pieces = (pl.ds(0, WIDE), pl.ds(LAST, WIDE), pl.ds(WIDE, LAST - WIDE))

    def frame_copies(kind, src, a, to_frame):
        return [
            remote(
                src.at[p], main.at[a].at[p], main_send.at[kind, i], main_recv.at[a, i], tile,
                to_frame,
            )
            for i, p in enumerate(pieces)
        ]

    to_next = frame_copies(1, lat, 1, frame + 1)
    to_skip = frame_copies(0, lat, 0, frame + 2)
    to_relay = frame_copies(2, main.at[1], 0, frame + 1)
    diagonal_up = remote(
        main.at[1].at[pieces[0]], bot.at[0], halo_send.at[3, 0], halo_recv.at[0, 0], tile - 1,
        frame + 1,
    )
    diagonal_down = remote(
        main.at[1].at[pieces[1]], top.at[0], halo_send.at[3, 1], halo_recv.at[0, 1], tile + 1,
        frame + 1,
    )

    def halo(a):
        src = lat if a == 2 else main.at[a]
        up = remote(
            src.at[pl.ds(0, WIDE)], bot.at[a], halo_send.at[a, 0], halo_recv.at[a, 0],
            tile - 1, frame,
        )
        down = remote(
            src.at[pl.ds(LAST, WIDE)], top.at[a], halo_send.at[a, 1], halo_recv.at[a, 1],
            tile + 1, frame,
        )
        return up, down

    def start_halo(a):
        up, down = halo(a)

        @pl.when(above)
        def _():
            up.start()

        @pl.when(below)
        def _():
            down.start()

    def wait_halo(a):
        up, down = halo(a)

        @pl.when(below)
        def _():
            up.wait_recv()

        @pl.when(above)
        def _():
            down.wait_recv()

    def end_halo(a):
        up, down = halo(a)

        @pl.when(above)
        def _():
            up.wait_send()

        @pl.when(below)
        def _():
            down.wait_send()

    @pl.when(next_frame)
    def _():
        for copy in to_next:
            copy.start()

    start_halo(2)

    all_sums(0).wait_recv()

    @pl.when(skip_frame)
    def _():
        for copy in to_skip:
            copy.start()

    mean, scale = combine_sums(gat[0], onehot[...], row_cells[...])
    tabs[2, 0:8, :] = mean
    tabs[2, 8:16, :] = scale
    tab_next = remote(tabs.at[2], tabs.at[1], tab_send.at[1], tab_recv.at[1], tile, frame + 1)
    tab_skip = remote(tabs.at[2], tabs.at[0], tab_send.at[0], tab_recv.at[0], tile, frame + 2)

    @pl.when(next_frame)
    def _():
        tab_next.start()

    @pl.when(frame + 2 < FRAMES)
    def _():
        tab_skip.start()

    column = lax.broadcasted_iota(jnp.int32, (COLS, CH), 0)

    def activate(a, row, cells):
        label = label_of(first - 1 + row)
        width = width_of(first - 1 + row)
        row_mean, row_scale = pick(tabs[a], label)
        normed = (cells - row_mean) * row_scale * line_of(first_gain) + line_of(first_shift)
        half_normed = 0.5 * normed
        hidden = half_normed + half_normed * jnp.tanh(half_normed)
        hidden = jnp.where(column < width, hidden, 0.0)
        hidden = jnp.concatenate([hidden, jnp.zeros((WIDE - COLS, CH), F32)], axis=0)
        lines = pl.ds(row * WIDE, WIDE)
        hid[a, lines, 0:CH] = pltpu.roll(hidden, 1, 0).astype(BF16)
        hid[a, lines, CH : 2 * CH] = hidden.astype(BF16)
        hid[a, lines, 2 * CH : 3 * CH] = pltpu.roll(hidden, WIDE - 1, 0).astype(BF16)

    def activate_main(a):
        cells = lat[...].astype(F32) if a == 2 else main[a].astype(F32)
        for r in range(ROWS):
            activate(a, r + 1, cells[r * COLS : (r + 1) * COLS])

    def activate_halo(a):
        activate(a, 0, top[a].astype(F32)[WIDE - COLS :])
        activate(a, ROWS + 1, bot[a].astype(F32)[:COLS])

    def convolve(a):
        def tap(b, carry):
            lines = pl.ds(pl.multiple_of(b * WIDE, 16), PADDED)
            product = jnp.dot(hid[a, lines, :], weight[a * 3 + b], preferred_element_type=F32)
            if a == 2:
                acc[b] = product
            else:
                acc[b] = acc[b] + product
            return carry

        lax.fori_loop(0, 3, tap, 0)

    @pl.when(has[1])
    def _():
        to_next[0].wait_recv()
        to_next[1].wait_recv()
        start_halo(1)

    @pl.when(relay)
    def _():
        to_relay[0].start()
        to_relay[1].start()

    @pl.when(relay & above)
    def _():
        diagonal_up.start()

    @pl.when(relay & below)
    def _():
        diagonal_down.start()

    activate_main(2)

    @pl.when(relay)
    def _():
        to_next[2].wait_recv()
        to_relay[2].start()

    wait_halo(2)
    activate_halo(2)
    load.wait()
    convolve(2)

    @pl.when(has[1] & jnp.logical_not(relay))
    def _():
        to_next[2].wait_recv()

    @pl.when(relay)
    def _():
        to_skip[0].wait_recv()
        to_skip[1].wait_recv()
        start_halo(0)

    @pl.when(has[1])
    def _():
        tab_next.wait_recv()
        activate_main(1)
        wait_halo(1)
        activate_halo(1)
        convolve(1)

    @pl.when(has[0] & jnp.logical_not(relay))
    def _():
        to_skip[0].wait_recv()
        to_skip[1].wait_recv()

    @pl.when(has[0])
    def _():
        to_skip[2].wait_recv()
        tab_skip.wait_recv()
        activate_main(0)
        wait_halo(0)
        activate_halo(0)
        convolve(0)

    source = lat[...].astype(F32)
    rows = []
    for r in range(ROWS):
        label = label_of(first + r)
        lines = pl.ds(r * WIDE, COLS)
        total = acc[1, lines, :]
        total = total + jnp.where(label_of(first + r - 1) == label, acc[0, lines, :], 0.0)
        total = total + jnp.where(label_of(first + r + 1) == label, acc[2, lines, :], 0.0)
        total = source[r * COLS : (r + 1) * COLS] + total + line_of(conv_bias)
        rows.append(jnp.where(column < width_of(first + r), total, 0.0))
    own[...] = jnp.concatenate(rows, axis=0).astype(BF16)

    source = own[...].astype(F32)
    gat[1, tile] = local_sums(source, width_of, first, st)
    send_sums(1)

    half = CELLS // 2
    upper_half, lower_half = pl.ds(0, half), pl.ds(half, half)
    ahead, behind, across = tile_at(x, y + 1, z), tile_at(x, y + 3, z), tile_at(x, y, z + 1)

    def pass_on(k, src, slot, peer, lines=None):
        dst = kv.at[slot]
        if lines is not None:
            src, dst = src.at[lines], dst.at[lines]
        return remote(src, dst, kv_send.at[k], kv_recv.at[k], peer, frame)

    kv_across = pass_on(0, own, 4, across)
    kv_copies = [kv_across]
    relays = []
    for zz in range(2):
        base = own if zz == 0 else kv.at[4]
        near = (pass_on(1 + 4 * zz, base, zz * 4 + 1, ahead),
                pass_on(2 + 4 * zz, base, zz * 4 + 3, behind))
        far = (pass_on(3 + 4 * zz, kv.at[zz * 4 + 1], zz * 4 + 2, ahead, upper_half),
               pass_on(4 + 4 * zz, kv.at[zz * 4 + 3], zz * 4 + 2, behind, lower_half))
        relays.append((near, far))
        kv_copies += list(near) + list(far)
    q_copies = []
    for d in range(1, 4):
        peer = tile_at(x + d, y, z)
        q_copies.append(remote(own, qb.at[d - 1], q_send.at[d - 1], q_recv.at[d - 1], peer, frame))
    kv_across.start()
    for copy in relays[0][0]:
        copy.start()
    for copy in q_copies:
        copy.start()
    kv_across.wait_recv()
    for copy in relays[1][0]:
        copy.start()
    all_sums(1).wait_recv()
    mean, scale = combine_sums(gat[1], onehot[...], row_cells[...])
    tab[0:8, :] = mean
    tab[8:16, :] = scale
    column = lax.broadcasted_iota(jnp.int32, (COLS, CH), 0)
    cell_column = lax.broadcasted_iota(jnp.int32, (COLS, LANES), 0)
    lane = lax.broadcasted_iota(jnp.int32, (COLS, LANES), 1)
    wide_lane = lax.broadcasted_iota(jnp.int32, (CELLS, LANES), 1)
    to_exponent = CH ** (-0.5) * math.log2(math.e)

    def normalise(block, block_tile):
        cells = block.astype(F32)
        rows = []
        for r in range(ROWS):
            at = block_tile * ROWS + r
            row_mean, row_scale = pick(tab, label_of(at))
            part = cells[r * COLS : (r + 1) * COLS]
            normed = (part - row_mean) * row_scale * line_of(second_gain) + line_of(second_shift)
            rows.append(jnp.where(column < width_of(at), normed, 0.0))
        return jnp.concatenate(rows, axis=0).astype(BF16)

    def put_query(slot, block, block_tile):
        normed = normalise(block, block_tile)
        plain = jnp.dot(normed, triple_weight[:, 0:CH], preferred_element_type=F32)
        plain = (plain + line_of(triple_bias, 0)).astype(BF16)
        turned = lax.dot_general(
            plain, triple_weight[:, CH : 2 * CH], NT, preferred_element_type=F32
        )
        constant = jnp.sum(
            plain.astype(F32) * line_of(triple_bias, 1), axis=1, keepdims=True
        )
        queries[slot, :, 0:CH] = (turned * to_exponent).astype(BF16)
        marks = []
        for r in range(ROWS):
            label = label_of(block_tile * ROWS + r)
            marks.append(jnp.where(lane == label, 1.0, 0.0))
        marks = jnp.concatenate(marks, axis=0)
        marks = jnp.where(wide_lane == 4, constant * to_exponent, marks)
        queries[slot, :, CH:EXT] = marks.astype(BF16)

    def put_keys(slot, block, block_tile):
        lines = pl.ds(pl.multiple_of(slot * CELLS, 16), CELLS)
        keys[lines, 0:CH] = normalise(block, block_tile)
        marks = []
        for r in range(ROWS):
            at = block_tile * ROWS + r
            seen = (lane == label_of(at)) & (cell_column < width_of(at))
            mark = jnp.where(seen, 0.0, MASKED)
            marks.append(jnp.where(lane < 4, mark, jnp.where(lane == 4, 1.0, 0.0)))
        keys[lines, CH:EXT] = jnp.concatenate(marks, axis=0).astype(BF16)

    def key_tile(slot):
        return tile_at(x, y + 4 - lax.rem(slot, 4), z + lax.div(slot, 4))

    put_query(0, own[...], tile)
    put_keys(0, own[...], tile)
    for copy in relays[0][0]:
        copy.wait_recv()
    for copy in relays[0][1]:
        copy.start()
    put_keys(4, kv[4], across)

    def put_pair(low_slot):
        def each_key(n, carry):
            slot = low_slot + 2 * n
            put_keys(slot, kv[slot], key_tile(slot))
            return carry

        lax.fori_loop(0, 2, each_key, 0)

    put_pair(1)
    for copy in relays[1][0]:
        copy.wait_recv()
    for copy in relays[1][1]:
        copy.start()
    put_pair(5)
    for d in range(1, 4):
        q_copies[d - 1].wait_recv()

    def each_query(d, carry):
        put_query(d, qb[d - 1], tile_at(x + 4 - d, y, z))
        return carry

    lax.fori_loop(1, 4, each_query, 0)
    for zz in range(2):
        for copy in relays[zz][1]:
            copy.wait_recv()
        put_keys(zz * 4 + 2, kv[zz * 4 + 2], key_tile(jnp.int32(zz * 4 + 2)))

    def attend(d):
        slot = lax.rem(4 - d, 4)
        scores[...] = lax.dot_general(queries[slot], keys[...], NT, preferred_element_type=F32)
        held = scores[...]
        largest = jnp.max(held, axis=1, keepdims=True)
        weights = jnp.exp2(held - largest).astype(BF16)
        mixed = jnp.dot(weights, keys[...], preferred_element_type=F32)
        sent[d] = mixed[:, 0:CH].astype(BF16)
        notes = jnp.where(wide_lane == 0, mixed[:, CH + 4 : CH + 5], 0.0)
        notes = jnp.where(wide_lane == 1, largest, notes)
        notes = jnp.concatenate([notes, jnp.zeros((4 * LANES - CELLS, LANES), F32)], axis=0)
        sent_notes[d] = jnp.transpose(notes)[0:8]

    def part_copy(d):
        return remote(
            sent.at[d], parts.at[d], part_send.at[d], part_recv.at[d], tile_at(x + d, y, z), frame
        )

    def note_copy(d):
        return remote(
            sent_notes.at[d], part_notes.at[d], note_send.at[d], note_recv.at[d],
            tile_at(x + d, y, z), frame,
        )

    def each_part(n, carry):
        d = 3 - n
        attend(d)

        @pl.when(d > 0)
        def _():
            note_copy(d).start()
            part_copy(d).start()

        return carry

    lax.fori_loop(0, 4, each_part, 0)
    for d in range(3, 0, -1):
        note_copy(d).wait_recv()
        part_copy(d).wait_recv()

    def part(d):
        return (sent[0] if d == 0 else parts[d]).astype(F32)

    def note(d):
        held = sent_notes[0] if d == 0 else part_notes[d]
        held = jnp.concatenate([held, jnp.zeros((LANES - 8, 4 * LANES), F32)], axis=0)
        return jnp.transpose(held)[:CELLS]

    tails = [note(d) for d in range(4)]
    maxima = [tail[:, 1:2] for tail in tails]
    most = functools.reduce(jnp.maximum, maxima)
    factors = [jnp.exp2(m - most) for m in maxima]
    denominator = sum(t[:, 0:1] * f for t, f in zip(tails, factors))
    numerator = sum(part(d) * factors[d] for d in range(4))
    averaged = (numerator / denominator).astype(BF16)
    mixed = jnp.dot(averaged, triple_weight[:, 2 * CH : 3 * CH], preferred_element_type=F32)
    mixed = (mixed + line_of(triple_bias, 2)).astype(BF16)
    attended = jnp.dot(mixed, output_weight[...], preferred_element_type=F32)
    total = own[...].astype(F32) + attended + line_of(output_bias)
    rows = []
    for r in range(ROWS):
        rows.append(
            jnp.where(column < width_of(first + r), total[r * COLS : (r + 1) * COLS], 0.0)
        )
    rim[...] = jnp.concatenate(rows, axis=0).astype(BF16)
    up = remote(
        rim.at[pl.ds(0, WIDE)], rim_bot, rim_send.at[0], rim_recv.at[0], tile - 1, frame
    )
    down = remote(
        rim.at[pl.ds(LAST, WIDE)], rim_top, rim_send.at[1], rim_recv.at[1], tile + 1, frame
    )

    @pl.when(above)
    def _():
        up.start()

    @pl.when(below)
    def _():
        down.start()

    def product(k, carry):
        taps[k, :, 0:OUT] = lax.dot_general(
            rim[...], up_weight[k], NT, preferred_element_type=F32
        )
        return carry

    lax.fori_loop(0, 9, product, 0)

    @pl.when(below)
    def _():
        up.wait_recv()
        down.wait_send()

    @pl.when(above)
    def _():
        down.wait_recv()
        up.wait_send()

    for e in range(3):
        ends[e, :, 0:OUT] = lax.dot_general(
            rim_top[...], up_weight[e], NT, preferred_element_type=F32
        )
        ends[3 + e, :, 0:OUT] = lax.dot_general(
            rim_bot[...], up_weight[6 + e], NT, preferred_element_type=F32
        )
    up_column = lax.broadcasted_iota(jnp.int32, (COLS, 2 * LANES), 0)
    for r in range(ROWS):
        label = label_of(first + r)
        lines = pl.ds(r * COLS, COLS)
        for p in range(2):
            joined = []
            other = r - 1 if p == 0 else r + 1
            alike = label_of(first + other) == label
            outer = 0 if p == 0 else 2
            for e in range(3):
                if other < 0:
                    far = ends[e, WIDE - COLS :, :]
                elif other == ROWS:
                    far = ends[3 + e, :COLS, :]
                else:
                    far = taps[outer * 3 + e, pl.ds(other * COLS, COLS), :]
                near = taps[3 + e, lines, :] + taps[(2 - outer) * 3 + e, lines, :]
                joined.append(near + jnp.where(alike, far, 0.0))
            before = jnp.where(up_column == 0, 0.0, pltpu.roll(joined[0], 1, 0))
            after = jnp.where(up_column == COLS - 1, 0.0, pltpu.roll(joined[2], COLS - 1, 0))
            valid = up_column < width_of(first + r)
            left = before + joined[1] + joined[2] + wide_bias[...]
            right = joined[0] + joined[1] + after + wide_bias[...]
            left = jnp.where(valid, left, 0.0)
            right = jnp.where(valid, right, 0.0)
            for half, lanes in ((low, slice(0, LANES)), (high, slice(LANES, 2 * LANES))):
                half[pl.ds(0, COLS, stride=2), :] = left[:, lanes]
                half[pl.ds(1, COLS, stride=2), :] = right[:, lanes]
            out[2 * r + p, :, 0:LANES] = low[...].astype(BF16)
            out[2 * r + p, :, LANES:OUT] = high[:, 0 : OUT - LANES].astype(BF16)

    @pl.when(next_frame)
    def _():
        for copy in to_next:
            copy.wait_send()
        tab_next.wait_send()

    @pl.when(frame + 2 < FRAMES)
    def _():
        tab_skip.wait_send()

    @pl.when(skip_frame)
    def _():
        for copy in to_skip:
            copy.wait_send()

    @pl.when(relay)
    def _():
        for copy in to_relay:
            copy.wait_send()
        end_halo(0)

    @pl.when(relay & above)
    def _():
        diagonal_up.wait_send()

    @pl.when(relay & below)
    def _():
        diagonal_down.wait_send()

    end_halo(2)

    @pl.when(has[1])
    def _():
        end_halo(1)

    all_sums(0).wait_send()
    all_sums(1).wait_send()
    for copy in kv_copies + q_copies:
        copy.wait_send()
    for d in range(3, 0, -1):
        part_copy(d).wait_send()
        note_copy(d).wait_send()


def shards(
    latents,
    row_video,
    video_cols,
    first_gain,
    first_shift,
    conv_weight,
    conv_bias,
    second_gain,
    second_shift,
    triple_weight,
    triple_bias,
    output_weight,
    output_bias,
    upsample_weight,
    upsample_bias,
):
    smem = pl.BlockSpec(memory_space=pltpu.SMEM)
    vmem = pl.BlockSpec(memory_space=pltpu.VMEM)
    anywhere = pl.BlockSpec(memory_space=pl.ANY)
    dma = pltpu.SemaphoreType.DMA
    block = (CELLS, CH)
    edge = (WIDE, CH)
    decoded = pl.pallas_call(
        whole_kernel,
        out_shape=jax.ShapeDtypeStruct((2 * ROWS, 2 * COLS, OUT), BF16),
        in_specs=[smem, smem, anywhere, vmem, vmem, anywhere] + [vmem] * 9,
        out_specs=vmem,
        scratch_shapes=[
            pltpu.VMEM(block, BF16),
            pltpu.VMEM((2,) + block, BF16),
            pltpu.VMEM((3,) + edge, BF16),
            pltpu.VMEM((3,) + edge, BF16),
            pltpu.VMEM((2, TILES, 8, LANES), F32),
            pltpu.VMEM((TILES * 8, LANES), F32),
            pltpu.VMEM((TILES * 8, LANES), F32),
            pltpu.VMEM((8, CH), F32),
            pltpu.VMEM((3, 16, CH), F32),
            pltpu.VMEM((3, 6 * WIDE, 3 * CH), BF16),
            pltpu.VMEM((9, 3 * CH, CH), BF16),
            pltpu.VMEM((3, PADDED, CH), F32),
            pltpu.VMEM(block, BF16),
            pltpu.VMEM((8,) + block, BF16),
            pltpu.VMEM((3,) + block, BF16),
            pltpu.VMEM((16, CH), F32),
            pltpu.VMEM((KEYS, EXT), BF16),
            pltpu.VMEM((4, CELLS, EXT), BF16),
            pltpu.VMEM((CELLS, KEYS), F32),
            pltpu.VMEM((4,) + block, BF16),
            pltpu.VMEM((4,) + block, BF16),
            pltpu.VMEM((4, 8, 4 * LANES), F32),
            pltpu.VMEM((4, 8, 4 * LANES), F32),
            pltpu.VMEM(block, BF16),
            pltpu.VMEM(edge, BF16),
            pltpu.VMEM(edge, BF16),
            pltpu.VMEM((9, CELLS, 2 * LANES), F32),
            pltpu.VMEM((6, WIDE, 2 * LANES), F32),
            pltpu.VMEM((2 * COLS, LANES), F32),
            pltpu.VMEM((2 * COLS, LANES), F32),
            pltpu.VMEM((1, 2 * LANES), F32),
            dma((2,)),
            dma((2,)),
            dma((3, 3)),
            dma((2, 3)),
            dma((4, 2)),
            dma((3, 2)),
            dma((2,)),
            dma((2,)),
            dma((2,)),
            dma((9,)),
            dma((9,)),
            dma((3,)),
            dma((3,)),
            dma((4,)),
            dma((4,)),
            dma((4,)),
            dma((4,)),
            dma((2,)),
            dma((2,)),
        ],
        compiler_params=pltpu.CompilerParams(
            collective_id=0, has_side_effects=True, vmem_limit_bytes=56 * 2**20
        ),
        name="decoder_window",
    )(
        row_video, video_cols, latents.reshape(CELLS, CH), first_gain, first_shift,
        conv_weight.reshape(9, 3 * CH, CH), conv_bias, second_gain, second_shift, triple_weight,
        triple_bias, output_weight, output_bias,
        jnp.transpose(upsample_weight, (0, 1, 3, 2)).reshape(9, OUT, CH), upsample_bias,
    )
    return decoded.reshape(2 * ROWS, 1, 2 * COLS, OUT)


def solution(mesh):
    in_specs = (P("tile", "frame", None, None),) + (P(),) * 14
    out_specs = P("tile", "frame", None, None)
    return jax.shard_map(shards, mesh=mesh, in_specs=in_specs, out_specs=out_specs, check_vma=False)
```

```python
import functools
import math

import jax
import jax.numpy as jnp
from jax import lax
from jax.experimental import pallas as pl
from jax.experimental.pallas import tpu as pltpu
from jax.sharding import PartitionSpec as P

GROUPS = 32
EPSILON = 1e-05
MASKED = -1e30
HIGHEST = lax.Precision.HIGHEST
MESH = pl.DeviceIdType.MESH
F32 = jnp.float32
BF16 = jnp.bfloat16
CH = 384
OUT = 192
ROWS = 4
COLS = 104
WIDE = 112
CELLS = ROWS * COLS
PADDED = ROWS * WIDE
LAST = CELLS - WIDE
LANES = 128
EXT = CH + LANES
TILES = 32
FRAMES = 8
KEYS = 8 * CELLS
NT = (((1,), (1,)), ((), ()))


def remote(src, dst, send_sem, recv_sem, tile, frame):
    return pltpu.make_async_remote_copy(
        src_ref=src,
        dst_ref=dst,
        send_sem=send_sem,
        recv_sem=recv_sem,
        device_id={"tile": tile, "frame": frame},
        device_id_type=MESH,
    )


def place():
    tile = lax.axis_index("tile")
    frame = lax.axis_index("frame")
    x = lax.div(tile, 8)
    y = lax.rem(lax.div(tile, 2), 4)
    z = lax.rem(tile, 2)
    return tile, frame, x, y, z


def tile_at(x, y, z):
    return lax.rem(x, 4) * 8 + lax.rem(y, 4) * 2 + lax.rem(z, 2)


def greet(barrier, tile, frame):
    pl.semaphore_signal(
        barrier, inc=1, device_id={"tile": tile, "frame": frame}, device_id_type=MESH
    )


def exact(a, b):
    return jnp.dot(a, b, precision=HIGHEST, preferred_element_type=F32)


def line_of(vector, part=None):
    held = vector[...] if part is None else vector[pl.ds(part * CH, CH)]
    return held.reshape(1, held.shape[0])


def pick(table, label):
    rows = lax.broadcasted_iota(jnp.int32, (8, CH), 0)
    chosen = rows == label
    mean = jnp.sum(jnp.where(chosen, table[0:8, :], 0.0), axis=0, keepdims=True)
    scale = jnp.sum(jnp.where(chosen, table[8:16, :], 0.0), axis=0, keepdims=True)
    return mean, scale


def members():
    per_group = CH // GROUPS
    start = lax.broadcasted_iota(jnp.int32, (LANES, CH), 0) * per_group
    channel = lax.broadcasted_iota(jnp.int32, (LANES, CH), 1)
    across = jnp.where((channel >= start) & (channel < start + per_group), 1.0, 0.0)
    start = lax.broadcasted_iota(jnp.int32, (CH, LANES), 1) * per_group
    channel = lax.broadcasted_iota(jnp.int32, (CH, LANES), 0)
    down = jnp.where((channel >= start) & (channel < start + per_group), 1.0, 0.0)
    return across, down


def local_sums(values, width_of, first, st):
    member, member_t = members()
    column = lax.broadcasted_iota(jnp.int32, (COLS, CH), 0)
    line = lax.broadcasted_iota(jnp.int32, (8, 1), 0)
    per_row = jnp.ones((8, 1), F32)
    for r in range(ROWS):
        width = width_of(first + r)
        mask = column < width
        cells = values[r * COLS : (r + 1) * COLS]
        total = jnp.sum(jnp.where(mask, cells, 0.0), axis=0, keepdims=True)
        mean = total / width.astype(F32)
        apart = jnp.where(mask, cells - mean, 0.0)
        st[r : r + 1, :] = total
        st[ROWS + r : ROWS + r + 1, :] = jnp.sum(apart * apart, axis=0, keepdims=True)
        per_row = jnp.where((line == r) | (line == ROWS + r), width.astype(F32), per_row)
    upper = line < ROWS
    held = st[...]
    grouped = exact(held, member_t)
    group_mean = exact(jnp.where(upper, grouped / (per_row * (CH // GROUPS)), 0.0), member)
    spread = jnp.where(upper, held / per_row - group_mean, 0.0)
    extra = exact(per_row * spread * spread, member_t)
    lower = pltpu.roll(extra, ROWS, 0)
    return jnp.where(upper, grouped, grouped + lower)


def combine_sums(gat, onehot, row_cells):
    member, _ = members()
    held = gat.reshape(TILES * 8, LANES)
    upper = lax.rem(lax.broadcasted_iota(jnp.int32, (TILES * 8, LANES), 0), 8) < ROWS
    by_video = jnp.transpose(onehot)[0:8]
    counts = exact(by_video, jnp.where(upper, row_cells, 0.0))
    inverse = jnp.where(counts > 0.0, 1.0 / counts, 0.0)
    mean = exact(by_video, jnp.where(upper, held, 0.0)) * inverse
    mean_rows = exact(onehot[:, 0:8], mean)
    off = held / row_cells - mean_rows
    spread = jnp.where(upper, row_cells * off * off, held)
    variance = exact(by_video, spread) * inverse
    scale = lax.rsqrt(variance + EPSILON)
    return exact(mean, member), exact(scale, member)


def whole_kernel(
    videos, cols, lat_hbm, first_gain, first_shift, conv_hbm, conv_bias, second_gain, second_shift,
    triple_hbm, triple_bias, output_hbm, output_bias, up_hbm, up_bias, out,
    triple_weight, output_weight, up_weight, lat, main, top, bot, gat, onehot, row_cells, st, tabs, hid, weight, acc,
    own, kv, qb, tab, keys, queries, scores, sent, parts, sent_notes, part_notes, rim, rim_top, rim_bot,
    taps, ends, low, high, wide_bias,
    stat_send, stat_recv, main_send, main_recv, halo_send, halo_recv, tab_send, tab_recv,
    load_sem, kv_send, kv_recv, q_send, q_recv, part_send, part_recv, note_send, note_recv,
    rim_send, rim_recv,
):
    tile, frame, x, y, z = place()
    first = tile * ROWS
    load_lat = pltpu.make_async_copy(lat_hbm, lat, load_sem.at[0])
    load_lat.start()
    load = pltpu.make_async_copy(conv_hbm, weight, load_sem.at[1])
    load.start()
    load_rest = [
        pltpu.make_async_copy(triple_hbm, triple_weight, load_sem.at[2]),
        pltpu.make_async_copy(output_hbm, output_weight, load_sem.at[3]),
        pltpu.make_async_copy(up_hbm, up_weight, load_sem.at[4]),
    ]
    for copy in load_rest:
        copy.start()

    def label_of(row):
        inside = (row >= 0) & (row < TILES * ROWS)
        return jnp.where(inside, videos[jnp.clip(row, 0, TILES * ROWS - 1)], -1)

    def width_of(row):
        inside = (row >= 0) & (row < TILES * ROWS)
        return jnp.where(inside, cols[videos[jnp.clip(row, 0, TILES * ROWS - 1)]], 0)

    barrier = pltpu.get_barrier_semaphore()

    def greet_tile(d, carry):
        greet(barrier, lax.rem(tile + d, TILES), frame)
        return carry

    lax.fori_loop(1, TILES, greet_tile, 0)
    awaited = TILES - 1
    for step in (-2, -1, 1, 2):
        there = (frame + step >= 0) & (frame + step < FRAMES)

        @pl.when(there)
        def _():
            greet(barrier, tile, frame + step)

        awaited = awaited + there.astype(jnp.int32)

    partner = frame + 1 - 2 * lax.rem(frame, 2)
    for step in (-1, 1):
        there = (tile + step >= 0) & (tile + step < TILES)

        @pl.when(there)
        def _():
            greet(barrier, tile + step, partner)

        awaited = awaited + there.astype(jnp.int32)

    slot_line = lax.rem(lax.broadcasted_iota(jnp.int32, (8, LANES), 0), ROWS)
    slot_lane = lax.broadcasted_iota(jnp.int32, (8, LANES), 1)

    def fill(t, carry):
        label = jnp.full((8, LANES), -1, jnp.int32)
        width = jnp.zeros((8, LANES), jnp.int32)
        for r in range(ROWS):
            number = videos[t * ROWS + r]
            label = jnp.where(slot_line == r, number, label)
            width = jnp.where(slot_line == r, cols[number], width)
        lines = pl.ds(pl.multiple_of(t * 8, 8), 8)
        onehot[lines, :] = jnp.where(label == slot_lane, 1.0, 0.0)
        row_cells[lines, :] = width.astype(F32) * (CH // GROUPS)
        return carry

    lax.fori_loop(0, TILES, fill, 0)
    wide_bias[...] = jnp.zeros((1, 2 * LANES), F32)
    wide_bias[:, 0:OUT] = line_of(up_bias)
    load_lat.wait()
    source = lat[...].astype(F32)
    gat[0, tile] = local_sums(source, width_of, first, st)
    pl.semaphore_wait(barrier, awaited)

    def sum_copy(which, d):
        peer = lax.rem(tile + d, TILES)
        return remote(
            gat.at[which, tile], gat.at[which, tile], stat_send.at[which], stat_recv.at[which],
            peer, frame,
        )

    def send_sums(which):
        def one(d, carry):
            sum_copy(which, d).start()
            return carry

        lax.fori_loop(1, TILES, one, 0)

    def all_sums(which):
        others = pl.ds(0, TILES - 1)
        return remote(
            gat.at[which, others], gat.at[which, others], stat_send.at[which],
            stat_recv.at[which], lax.rem(tile + 1, TILES), frame,
        )

    send_sums(0)

    even = lax.rem(frame, 2) == 0
    next_frame = frame + 1 < FRAMES
    skip_frame = even & (frame + 2 < FRAMES)
    relay = even & (frame >= 2)
    has = {1: frame >= 1, 0: frame >= 2}
    above = tile >= 1
    below = tile + 1 < TILES

    pieces = (pl.ds(0, WIDE), pl.ds(LAST, WIDE), pl.ds(WIDE, LAST - WIDE))

    def frame_copies(kind, src, a, to_frame):
        return [
            remote(
                src.at[p], main.at[a].at[p], main_send.at[kind, i], main_recv.at[a, i], tile,
                to_frame,
            )
            for i, p in enumerate(pieces)
        ]

    to_next = frame_copies(1, lat, 1, frame + 1)
    to_skip = frame_copies(0, lat, 0, frame + 2)
    to_relay = frame_copies(2, main.at[1], 0, frame + 1)
    diagonal_up = remote(
        main.at[1].at[pieces[0]], bot.at[0], halo_send.at[3, 0], halo_recv.at[0, 0], tile - 1,
        frame + 1,
    )
    diagonal_down = remote(
        main.at[1].at[pieces[1]], top.at[0], halo_send.at[3, 1], halo_recv.at[0, 1], tile + 1,
        frame + 1,
    )

    def halo(a):
        src = lat if a == 2 else main.at[a]
        up = remote(
            src.at[pl.ds(0, WIDE)], bot.at[a], halo_send.at[a, 0], halo_recv.at[a, 0],
            tile - 1, frame,
        )
        down = remote(
            src.at[pl.ds(LAST, WIDE)], top.at[a], halo_send.at[a, 1], halo_recv.at[a, 1],
            tile + 1, frame,
        )
        return up, down

    def start_halo(a):
        up, down = halo(a)

        @pl.when(above)
        def _():
            up.start()

        @pl.when(below)
        def _():
            down.start()

    def wait_halo(a):
        up, down = halo(a)

        @pl.when(below)
        def _():
            up.wait_recv()

        @pl.when(above)
        def _():
            down.wait_recv()

    def end_halo(a):
        up, down = halo(a)

        @pl.when(above)
        def _():
            up.wait_send()

        @pl.when(below)
        def _():
            down.wait_send()

    @pl.when(next_frame)
    def _():
        for copy in to_next:
            copy.start()

    start_halo(2)

    all_sums(0).wait_recv()

    @pl.when(skip_frame)
    def _():
        for copy in to_skip:
            copy.start()

    mean, scale = combine_sums(gat[0], onehot[...], row_cells[...])
    tabs[2, 0:8, :] = mean
    tabs[2, 8:16, :] = scale
    tab_next = remote(tabs.at[2], tabs.at[1], tab_send.at[1], tab_recv.at[1], tile, frame + 1)
    tab_skip = remote(tabs.at[2], tabs.at[0], tab_send.at[0], tab_recv.at[0], tile, frame + 2)

    @pl.when(next_frame)
    def _():
        tab_next.start()

    @pl.when(frame + 2 < FRAMES)
    def _():
        tab_skip.start()

    column = lax.broadcasted_iota(jnp.int32, (COLS, CH), 0)

    def activate(a, row, cells):
        label = label_of(first - 1 + row)
        width = width_of(first - 1 + row)
        row_mean, row_scale = pick(tabs[a], label)
        normed = (cells - row_mean) * row_scale * line_of(first_gain) + line_of(first_shift)
        half_normed = 0.5 * normed
        hidden = half_normed + half_normed * jnp.tanh(half_normed)
        hidden = jnp.where(column < width, hidden, 0.0)
        hidden = jnp.concatenate([hidden, jnp.zeros((WIDE - COLS, CH), F32)], axis=0)
        lines = pl.ds(row * WIDE, WIDE)
        hid[a, lines, 0:CH] = pltpu.roll(hidden, 1, 0).astype(BF16)
        hid[a, lines, CH : 2 * CH] = hidden.astype(BF16)
        hid[a, lines, 2 * CH : 3 * CH] = pltpu.roll(hidden, WIDE - 1, 0).astype(BF16)

    def activate_main(a):
        cells = lat[...].astype(F32) if a == 2 else main[a].astype(F32)
        for r in range(ROWS):
            activate(a, r + 1, cells[r * COLS : (r + 1) * COLS])

    def activate_halo(a):
        activate(a, 0, top[a].astype(F32)[WIDE - COLS :])
        activate(a, ROWS + 1, bot[a].astype(F32)[:COLS])

    def convolve(a):
        def tap(b, carry):
            lines = pl.ds(pl.multiple_of(b * WIDE, 16), PADDED)
            product = jnp.dot(hid[a, lines, :], weight[a * 3 + b], preferred_element_type=F32)
            if a == 2:
                acc[b] = product
            else:
                acc[b] = acc[b] + product
            return carry

        lax.fori_loop(0, 3, tap, 0)

    @pl.when(has[1])
    def _():
        to_next[0].wait_recv()
        to_next[1].wait_recv()
        start_halo(1)

    @pl.when(relay)
    def _():
        to_relay[0].start()
        to_relay[1].start()

    @pl.when(relay & above)
    def _():
        diagonal_up.start()

    @pl.when(relay & below)
    def _():
        diagonal_down.start()

    activate_main(2)

    @pl.when(relay)
    def _():
        to_next[2].wait_recv()
        to_relay[2].start()

    wait_halo(2)
    activate_halo(2)
    load.wait()
    convolve(2)

    @pl.when(has[1] & jnp.logical_not(relay))
    def _():
        to_next[2].wait_recv()

    @pl.when(relay)
    def _():
        to_skip[0].wait_recv()
        to_skip[1].wait_recv()
        start_halo(0)

    @pl.when(has[1])
    def _():
        tab_next.wait_recv()
        activate_main(1)
        wait_halo(1)
        activate_halo(1)
        convolve(1)

    @pl.when(has[0] & jnp.logical_not(relay))
    def _():
        to_skip[0].wait_recv()
        to_skip[1].wait_recv()

    @pl.when(has[0])
    def _():
        to_skip[2].wait_recv()
        tab_skip.wait_recv()
        activate_main(0)
        wait_halo(0)
        activate_halo(0)
        convolve(0)

    source = lat[...].astype(F32)
    rows = []
    for r in range(ROWS):
        label = label_of(first + r)
        lines = pl.ds(r * WIDE, COLS)
        total = acc[1, lines, :]
        total = total + jnp.where(label_of(first + r - 1) == label, acc[0, lines, :], 0.0)
        total = total + jnp.where(label_of(first + r + 1) == label, acc[2, lines, :], 0.0)
        total = source[r * COLS : (r + 1) * COLS] + total + line_of(conv_bias)
        rows.append(jnp.where(column < width_of(first + r), total, 0.0))
    own[...] = jnp.concatenate(rows, axis=0).astype(BF16)

    half = CELLS // 2
    halves = (pl.ds(0, half), pl.ds(half, half))
    ahead, behind, across = tile_at(x, y + 1, z), tile_at(x, y + 3, z), tile_at(x, y, z + 1)

    def pass_on(src, slot, h, peer):
        return remote(
            src.at[halves[h]], kv.at[slot].at[halves[h]], kv_send.at[slot, h],
            kv_recv.at[slot, h], peer, frame,
        )

    kv_across = [pass_on(own, 4, h, across) for h in range(2)]
    kv_copies = list(kv_across)
    to_ahead, to_behind, relays = [], [], []
    for zz in range(2):
        base = own if zz == 0 else kv.at[4]
        to_ahead.append([pass_on(base, zz * 4 + 1, h, ahead) for h in range(2)])
        to_behind.append([pass_on(base, zz * 4 + 3, h, behind) for h in range(2)])
        relays.append([pass_on(kv.at[zz * 4 + 1], zz * 4 + 2, 0, ahead),
                       pass_on(kv.at[zz * 4 + 3], zz * 4 + 2, 1, behind)])
        kv_copies += to_ahead[zz] + to_behind[zz] + relays[zz]
    q_copies = []
    for d in range(1, 4):
        peer = tile_at(x + d, y, z)
        q_copies.append(remote(own, qb.at[d - 1], q_send.at[d - 1], q_recv.at[d - 1], peer, frame))
    kv_across[0].start()
    to_ahead[0][0].start()
    to_behind[0][1].start()
    kv_across[1].start()
    to_ahead[0][1].start()
    to_behind[0][0].start()
    for copy in q_copies:
        copy.start()
    source = own[...].astype(F32)
    gat[1, tile] = local_sums(source, width_of, first, st)
    send_sums(1)
    kv_across[0].wait_recv()
    to_ahead[1][0].start()
    kv_across[1].wait_recv()
    to_behind[1][1].start()
    to_ahead[0][0].wait_recv()
    relays[0][0].start()
    to_behind[0][1].wait_recv()
    relays[0][1].start()
    to_ahead[1][1].start()
    to_behind[1][0].start()
    all_sums(1).wait_recv()
    mean, scale = combine_sums(gat[1], onehot[...], row_cells[...])
    tab[0:8, :] = mean
    tab[8:16, :] = scale
    column = lax.broadcasted_iota(jnp.int32, (COLS, CH), 0)
    cell_column = lax.broadcasted_iota(jnp.int32, (COLS, LANES), 0)
    lane = lax.broadcasted_iota(jnp.int32, (COLS, LANES), 1)
    wide_lane = lax.broadcasted_iota(jnp.int32, (CELLS, LANES), 1)
    to_exponent = CH ** (-0.5) * math.log2(math.e)

    def normalise(block, block_tile):
        cells = block.astype(F32)
        rows = []
        for r in range(ROWS):
            at = block_tile * ROWS + r
            row_mean, row_scale = pick(tab, label_of(at))
            part = cells[r * COLS : (r + 1) * COLS]
            normed = (part - row_mean) * row_scale * line_of(second_gain) + line_of(second_shift)
            rows.append(jnp.where(column < width_of(at), normed, 0.0))
        return jnp.concatenate(rows, axis=0).astype(BF16)

    def put_query(slot, block, block_tile):
        normed = normalise(block, block_tile)
        plain = jnp.dot(normed, triple_weight[:, 0:CH], preferred_element_type=F32)
        plain = (plain + line_of(triple_bias, 0)).astype(BF16)
        turned = lax.dot_general(
            plain, triple_weight[:, CH : 2 * CH], NT, preferred_element_type=F32
        )
        constant = jnp.sum(
            plain.astype(F32) * line_of(triple_bias, 1), axis=1, keepdims=True
        )
        queries[slot, :, 0:CH] = (turned * to_exponent).astype(BF16)
        marks = []
        for r in range(ROWS):
            label = label_of(block_tile * ROWS + r)
            marks.append(jnp.where(lane == label, 1.0, 0.0))
        marks = jnp.concatenate(marks, axis=0)
        marks = jnp.where(wide_lane == 4, constant * to_exponent, marks)
        queries[slot, :, CH:EXT] = marks.astype(BF16)

    def put_keys(slot, block, block_tile):
        lines = pl.ds(pl.multiple_of(slot * CELLS, 16), CELLS)
        keys[lines, 0:CH] = normalise(block, block_tile)
        marks = []
        for r in range(ROWS):
            at = block_tile * ROWS + r
            seen = (lane == label_of(at)) & (cell_column < width_of(at))
            mark = jnp.where(seen, 0.0, MASKED)
            marks.append(jnp.where(lane < 4, mark, jnp.where(lane == 4, 1.0, 0.0)))
        keys[lines, CH:EXT] = jnp.concatenate(marks, axis=0).astype(BF16)

    def key_tile(slot):
        return tile_at(x, y + 4 - lax.rem(slot, 4), z + lax.div(slot, 4))

    for copy in load_rest:
        copy.wait()
    put_query(0, own[...], tile)
    put_keys(0, own[...], tile)
    put_keys(4, kv[4], across)
    to_ahead[0][1].wait_recv()
    to_behind[0][0].wait_recv()

    def put_pair(low_slot):
        def each_key(n, carry):
            slot = low_slot + 2 * n
            put_keys(slot, kv[slot], key_tile(slot))
            return carry

        lax.fori_loop(0, 2, each_key, 0)

    put_pair(1)
    to_ahead[1][0].wait_recv()
    relays[1][0].start()
    to_behind[1][1].wait_recv()
    relays[1][1].start()
    for d in range(1, 4):
        q_copies[d - 1].wait_recv()

    def each_query(d, carry):
        put_query(d, qb[d - 1], tile_at(x + 4 - d, y, z))
        return carry

    lax.fori_loop(1, 4, each_query, 0)
    to_ahead[1][1].wait_recv()
    to_behind[1][0].wait_recv()
    put_pair(5)
    for zz in range(2):
        for copy in relays[zz]:
            copy.wait_recv()
        put_keys(zz * 4 + 2, kv[zz * 4 + 2], key_tile(jnp.int32(zz * 4 + 2)))

    def attend(d):
        slot = lax.rem(4 - d, 4)
        scores[...] = lax.dot_general(queries[slot], keys[...], NT, preferred_element_type=F32)
        held = scores[...]
        largest = jnp.max(held, axis=1, keepdims=True)
        weights = jnp.exp2(held - largest).astype(BF16)
        mixed = jnp.dot(weights, keys[...], preferred_element_type=F32)
        sent[d] = mixed[:, 0:CH].astype(BF16)
        notes = jnp.where(wide_lane == 0, mixed[:, CH + 4 : CH + 5], 0.0)
        notes = jnp.where(wide_lane == 1, largest, notes)
        notes = jnp.concatenate([notes, jnp.zeros((4 * LANES - CELLS, LANES), F32)], axis=0)
        sent_notes[d] = jnp.transpose(notes)[0:8]

    def part_copy(d):
        return remote(
            sent.at[d], parts.at[d], part_send.at[d], part_recv.at[d], tile_at(x + d, y, z), frame
        )

    def note_copy(d):
        return remote(
            sent_notes.at[d], part_notes.at[d], note_send.at[d], note_recv.at[d],
            tile_at(x + d, y, z), frame,
        )

    def each_part(n, carry):
        d = 3 - n
        attend(d)

        @pl.when(d > 0)
        def _():
            note_copy(d).start()
            part_copy(d).start()

        return carry

    lax.fori_loop(0, 4, each_part, 0)
    for d in range(3, 0, -1):
        note_copy(d).wait_recv()
        part_copy(d).wait_recv()

    def part(d):
        return (sent[0] if d == 0 else parts[d]).astype(F32)

    def note(d):
        held = sent_notes[0] if d == 0 else part_notes[d]
        held = jnp.concatenate([held, jnp.zeros((LANES - 8, 4 * LANES), F32)], axis=0)
        return jnp.transpose(held)[:CELLS]

    tails = [note(d) for d in range(4)]
    maxima = [tail[:, 1:2] for tail in tails]
    most = functools.reduce(jnp.maximum, maxima)
    factors = [jnp.exp2(m - most) for m in maxima]
    denominator = sum(t[:, 0:1] * f for t, f in zip(tails, factors))
    numerator = sum(part(d) * factors[d] for d in range(4))
    averaged = (numerator / denominator).astype(BF16)
    mixed = jnp.dot(averaged, triple_weight[:, 2 * CH : 3 * CH], preferred_element_type=F32)
    mixed = (mixed + line_of(triple_bias, 2)).astype(BF16)
    attended = jnp.dot(mixed, output_weight[...], preferred_element_type=F32)
    total = own[...].astype(F32) + attended + line_of(output_bias)
    rows = []
    for r in range(ROWS):
        rows.append(
            jnp.where(column < width_of(first + r), total[r * COLS : (r + 1) * COLS], 0.0)
        )
    rim[...] = jnp.concatenate(rows, axis=0).astype(BF16)
    up = remote(
        rim.at[pl.ds(0, WIDE)], rim_bot, rim_send.at[0], rim_recv.at[0], tile - 1, frame
    )
    down = remote(
        rim.at[pl.ds(LAST, WIDE)], rim_top, rim_send.at[1], rim_recv.at[1], tile + 1, frame
    )

    @pl.when(above)
    def _():
        up.start()

    @pl.when(below)
    def _():
        down.start()

    def product(k, carry):
        taps[k, :, 0:OUT] = lax.dot_general(
            rim[...], up_weight[k], NT, preferred_element_type=F32
        )
        return carry

    lax.fori_loop(0, 9, product, 0)

    @pl.when(below)
    def _():
        up.wait_recv()
        down.wait_send()

    @pl.when(above)
    def _():
        down.wait_recv()
        up.wait_send()

    for e in range(3):
        ends[e, :, 0:OUT] = lax.dot_general(
            rim_top[...], up_weight[e], NT, preferred_element_type=F32
        )
        ends[3 + e, :, 0:OUT] = lax.dot_general(
            rim_bot[...], up_weight[6 + e], NT, preferred_element_type=F32
        )
    up_column = lax.broadcasted_iota(jnp.int32, (COLS, 2 * LANES), 0)
    for r in range(ROWS):
        label = label_of(first + r)
        lines = pl.ds(r * COLS, COLS)
        for p in range(2):
            joined = []
            other = r - 1 if p == 0 else r + 1
            alike = label_of(first + other) == label
            outer = 0 if p == 0 else 2
            for e in range(3):
                if other < 0:
                    far = ends[e, WIDE - COLS :, :]
                elif other == ROWS:
                    far = ends[3 + e, :COLS, :]
                else:
                    far = taps[outer * 3 + e, pl.ds(other * COLS, COLS), :]
                near = taps[3 + e, lines, :] + taps[(2 - outer) * 3 + e, lines, :]
                joined.append(near + jnp.where(alike, far, 0.0))
            before = jnp.where(up_column == 0, 0.0, pltpu.roll(joined[0], 1, 0))
            after = jnp.where(up_column == COLS - 1, 0.0, pltpu.roll(joined[2], COLS - 1, 0))
            valid = up_column < width_of(first + r)
            left = before + joined[1] + joined[2] + wide_bias[...]
            right = joined[0] + joined[1] + after + wide_bias[...]
            left = jnp.where(valid, left, 0.0)
            right = jnp.where(valid, right, 0.0)
            for half, lanes in ((low, slice(0, LANES)), (high, slice(LANES, 2 * LANES))):
                half[pl.ds(0, COLS, stride=2), :] = left[:, lanes]
                half[pl.ds(1, COLS, stride=2), :] = right[:, lanes]
            out[2 * r + p, :, 0:LANES] = low[...].astype(BF16)
            out[2 * r + p, :, LANES:OUT] = high[:, 0 : OUT - LANES].astype(BF16)

    @pl.when(next_frame)
    def _():
        for copy in to_next:
            copy.wait_send()
        tab_next.wait_send()

    @pl.when(frame + 2 < FRAMES)
    def _():
        tab_skip.wait_send()

    @pl.when(skip_frame)
    def _():
        for copy in to_skip:
            copy.wait_send()

    @pl.when(relay)
    def _():
        for copy in to_relay:
            copy.wait_send()
        end_halo(0)

    @pl.when(relay & above)
    def _():
        diagonal_up.wait_send()

    @pl.when(relay & below)
    def _():
        diagonal_down.wait_send()

    end_halo(2)

    @pl.when(has[1])
    def _():
        end_halo(1)

    all_sums(0).wait_send()
    all_sums(1).wait_send()
    for copy in kv_copies + q_copies:
        copy.wait_send()
    for d in range(3, 0, -1):
        part_copy(d).wait_send()
        note_copy(d).wait_send()


def shards(
    latents,
    row_video,
    video_cols,
    first_gain,
    first_shift,
    conv_weight,
    conv_bias,
    second_gain,
    second_shift,
    triple_weight,
    triple_bias,
    output_weight,
    output_bias,
    upsample_weight,
    upsample_bias,
):
    smem = pl.BlockSpec(memory_space=pltpu.SMEM)
    vmem = pl.BlockSpec(memory_space=pltpu.VMEM)
    anywhere = pl.BlockSpec(memory_space=pl.ANY)
    dma = pltpu.SemaphoreType.DMA
    block = (CELLS, CH)
    edge = (WIDE, CH)
    decoded = pl.pallas_call(
        whole_kernel,
        out_shape=jax.ShapeDtypeStruct((2 * ROWS, 2 * COLS, OUT), BF16),
        in_specs=[smem, smem, anywhere, vmem, vmem, anywhere, vmem, vmem, vmem]
        + [anywhere, vmem] * 3,
        out_specs=vmem,
        scratch_shapes=[
            pltpu.VMEM((CH, 3 * CH), BF16),
            pltpu.VMEM((CH, CH), BF16),
            pltpu.VMEM((9, OUT, CH), BF16),
            pltpu.VMEM(block, BF16),
            pltpu.VMEM((2,) + block, BF16),
            pltpu.VMEM((3,) + edge, BF16),
            pltpu.VMEM((3,) + edge, BF16),
            pltpu.VMEM((2, TILES, 8, LANES), F32),
            pltpu.VMEM((TILES * 8, LANES), F32),
            pltpu.VMEM((TILES * 8, LANES), F32),
            pltpu.VMEM((8, CH), F32),
            pltpu.VMEM((3, 16, CH), F32),
            pltpu.VMEM((3, 6 * WIDE, 3 * CH), BF16),
            pltpu.VMEM((9, 3 * CH, CH), BF16),
            pltpu.VMEM((3, PADDED, CH), F32),
            pltpu.VMEM(block, BF16),
            pltpu.VMEM((8,) + block, BF16),
            pltpu.VMEM((3,) + block, BF16),
            pltpu.VMEM((16, CH), F32),
            pltpu.VMEM((KEYS, EXT), BF16),
            pltpu.VMEM((4, CELLS, EXT), BF16),
            pltpu.VMEM((CELLS, KEYS), F32),
            pltpu.VMEM((4,) + block, BF16),
            pltpu.VMEM((4,) + block, BF16),
            pltpu.VMEM((4, 8, 4 * LANES), F32),
            pltpu.VMEM((4, 8, 4 * LANES), F32),
            pltpu.VMEM(block, BF16),
            pltpu.VMEM(edge, BF16),
            pltpu.VMEM(edge, BF16),
            pltpu.VMEM((9, CELLS, 2 * LANES), F32),
            pltpu.VMEM((6, WIDE, 2 * LANES), F32),
            pltpu.VMEM((2 * COLS, LANES), F32),
            pltpu.VMEM((2 * COLS, LANES), F32),
            pltpu.VMEM((1, 2 * LANES), F32),
            dma((2,)),
            dma((2,)),
            dma((3, 3)),
            dma((2, 3)),
            dma((4, 2)),
            dma((3, 2)),
            dma((2,)),
            dma((2,)),
            dma((5,)),
            dma((8, 2)),
            dma((8, 2)),
            dma((3,)),
            dma((3,)),
            dma((4,)),
            dma((4,)),
            dma((4,)),
            dma((4,)),
            dma((2,)),
            dma((2,)),
        ],
        compiler_params=pltpu.CompilerParams(
            collective_id=0, has_side_effects=True, vmem_limit_bytes=56 * 2**20
        ),
        name="decoder_window",
    )(
        row_video, video_cols, latents.reshape(CELLS, CH), first_gain, first_shift,
        conv_weight.reshape(9, 3 * CH, CH), conv_bias, second_gain, second_shift, triple_weight,
        triple_bias, output_weight, output_bias,
        jnp.transpose(upsample_weight, (0, 1, 3, 2)).reshape(9, OUT, CH), upsample_bias,
    )
    return decoded.reshape(2 * ROWS, 1, 2 * COLS, OUT)


def solution(mesh):
    in_specs = (P("tile", "frame", None, None),) + (P(),) * 14
    out_specs = P("tile", "frame", None, None)
    return jax.shard_map(shards, mesh=mesh, in_specs=in_specs, out_specs=out_specs, check_vma=False)
```

```python
import functools
import math

import jax
import jax.numpy as jnp
from jax import lax
from jax.experimental import pallas as pl
from jax.experimental.pallas import tpu as pltpu
from jax.sharding import PartitionSpec as P

GROUPS = 32
EPSILON = 1e-05
MASKED = -1e30
HIGHEST = lax.Precision.HIGHEST
MESH = pl.DeviceIdType.MESH
F32 = jnp.float32
BF16 = jnp.bfloat16
CH = 384
OUT = 192
ROWS = 4
COLS = 104
WIDE = 112
CELLS = ROWS * COLS
PADDED = ROWS * WIDE
LAST = CELLS - WIDE
LANES = 128
EXT = CH + LANES
TILES = 32
FRAMES = 8
KEYS = 8 * CELLS
NT = (((1,), (1,)), ((), ()))


def remote(src, dst, send_sem, recv_sem, tile, frame):
    return pltpu.make_async_remote_copy(
        src_ref=src,
        dst_ref=dst,
        send_sem=send_sem,
        recv_sem=recv_sem,
        device_id={"tile": tile, "frame": frame},
        device_id_type=MESH,
    )


def place():
    tile = lax.axis_index("tile")
    frame = lax.axis_index("frame")
    x = lax.div(tile, 8)
    y = lax.rem(lax.div(tile, 2), 4)
    z = lax.rem(tile, 2)
    return tile, frame, x, y, z


def tile_at(x, y, z):
    return lax.rem(x, 4) * 8 + lax.rem(y, 4) * 2 + lax.rem(z, 2)


def greet(barrier, tile, frame):
    pl.semaphore_signal(
        barrier, inc=1, device_id={"tile": tile, "frame": frame}, device_id_type=MESH
    )


def exact(a, b):
    return jnp.dot(a, b, precision=HIGHEST, preferred_element_type=F32)


def line_of(vector, part=None):
    held = vector[...] if part is None else vector[pl.ds(part * CH, CH)]
    return held.reshape(1, held.shape[0])


def pick(table, label):
    rows = lax.broadcasted_iota(jnp.int32, (8, CH), 0)
    chosen = rows == label
    mean = jnp.sum(jnp.where(chosen, table[0:8, :], 0.0), axis=0, keepdims=True)
    scale = jnp.sum(jnp.where(chosen, table[8:16, :], 0.0), axis=0, keepdims=True)
    return mean, scale


def members():
    per_group = CH // GROUPS
    start = lax.broadcasted_iota(jnp.int32, (LANES, CH), 0) * per_group
    channel = lax.broadcasted_iota(jnp.int32, (LANES, CH), 1)
    across = jnp.where((channel >= start) & (channel < start + per_group), 1.0, 0.0)
    start = lax.broadcasted_iota(jnp.int32, (CH, LANES), 1) * per_group
    channel = lax.broadcasted_iota(jnp.int32, (CH, LANES), 0)
    down = jnp.where((channel >= start) & (channel < start + per_group), 1.0, 0.0)
    return across, down


def local_sums(values, width_of, first, st):
    member, member_t = members()
    column = lax.broadcasted_iota(jnp.int32, (COLS, CH), 0)
    line = lax.broadcasted_iota(jnp.int32, (8, 1), 0)
    per_row = jnp.ones((8, 1), F32)
    for r in range(ROWS):
        width = width_of(first + r)
        mask = column < width
        cells = values[r * COLS : (r + 1) * COLS]
        total = jnp.sum(jnp.where(mask, cells, 0.0), axis=0, keepdims=True)
        mean = total / width.astype(F32)
        apart = jnp.where(mask, cells - mean, 0.0)
        st[r : r + 1, :] = total
        st[ROWS + r : ROWS + r + 1, :] = jnp.sum(apart * apart, axis=0, keepdims=True)
        per_row = jnp.where((line == r) | (line == ROWS + r), width.astype(F32), per_row)
    upper = line < ROWS
    held = st[...]
    grouped = exact(held, member_t)
    group_mean = exact(jnp.where(upper, grouped / (per_row * (CH // GROUPS)), 0.0), member)
    spread = jnp.where(upper, held / per_row - group_mean, 0.0)
    extra = exact(per_row * spread * spread, member_t)
    lower = pltpu.roll(extra, ROWS, 0)
    return jnp.where(upper, grouped, grouped + lower)


def combine_sums(gat, onehot, row_cells):
    member, _ = members()
    held = gat.reshape(TILES * 8, LANES)
    upper = lax.rem(lax.broadcasted_iota(jnp.int32, (TILES * 8, LANES), 0), 8) < ROWS
    by_video = jnp.transpose(onehot)[0:8]
    counts = exact(by_video, jnp.where(upper, row_cells, 0.0))
    inverse = jnp.where(counts > 0.0, 1.0 / counts, 0.0)
    mean = exact(by_video, jnp.where(upper, held, 0.0)) * inverse
    mean_rows = exact(onehot[:, 0:8], mean)
    off = held / row_cells - mean_rows
    spread = jnp.where(upper, row_cells * off * off, held)
    variance = exact(by_video, spread) * inverse
    scale = lax.rsqrt(variance + EPSILON)
    return exact(mean, member), exact(scale, member)


def whole_kernel(
    videos, cols, lat_hbm, first_gain, first_shift, conv_hbm, conv_bias, second_gain, second_shift,
    triple_hbm, triple_bias, output_hbm, output_bias, up_hbm, up_bias, out,
    triple_weight, output_weight, up_weight, lat, main, top, bot, gat, onehot, row_cells, st, tabs, hid, weight, acc,
    own, kv, qb, tab, keys, queries, scores, sent, parts, sent_notes, part_notes, rim, rim_top, rim_bot,
    taps, ends, low, high, wide_bias,
    stat_send, stat_recv, main_send, main_recv, halo_send, halo_recv, tab_send, tab_recv,
    load_sem, kv_send, kv_recv, q_send, q_recv, part_send, part_recv, note_send, note_recv,
    rim_send, rim_recv,
):
    tile, frame, x, y, z = place()
    first = tile * ROWS
    load_lat = pltpu.make_async_copy(lat_hbm, lat, load_sem.at[0])
    load_lat.start()
    load = pltpu.make_async_copy(conv_hbm, weight, load_sem.at[1])
    load.start()
    load_rest = [
        pltpu.make_async_copy(triple_hbm, triple_weight, load_sem.at[2]),
        pltpu.make_async_copy(output_hbm, output_weight, load_sem.at[3]),
        pltpu.make_async_copy(up_hbm, up_weight, load_sem.at[4]),
    ]
    for copy in load_rest:
        copy.start()

    def label_of(row):
        inside = (row >= 0) & (row < TILES * ROWS)
        return jnp.where(inside, videos[jnp.clip(row, 0, TILES * ROWS - 1)], -1)

    def width_of(row):
        inside = (row >= 0) & (row < TILES * ROWS)
        return jnp.where(inside, cols[videos[jnp.clip(row, 0, TILES * ROWS - 1)]], 0)

    barrier = pltpu.get_barrier_semaphore()

    def greet_tile(d, carry):
        greet(barrier, lax.rem(tile + d, TILES), frame)
        return carry

    lax.fori_loop(1, TILES, greet_tile, 0)
    awaited = TILES - 1
    for step in (-2, -1, 1, 2):
        there = (frame + step >= 0) & (frame + step < FRAMES)

        @pl.when(there)
        def _():
            greet(barrier, tile, frame + step)

        awaited = awaited + there.astype(jnp.int32)

    partner = frame + 1 - 2 * lax.rem(frame, 2)
    for step in (-1, 1):
        there = (tile + step >= 0) & (tile + step < TILES)

        @pl.when(there)
        def _():
            greet(barrier, tile + step, partner)

        awaited = awaited + there.astype(jnp.int32)

    slot_line = lax.rem(lax.broadcasted_iota(jnp.int32, (8, LANES), 0), ROWS)
    slot_lane = lax.broadcasted_iota(jnp.int32, (8, LANES), 1)

    def fill(t, carry):
        label = jnp.full((8, LANES), -1, jnp.int32)
        width = jnp.zeros((8, LANES), jnp.int32)
        for r in range(ROWS):
            number = videos[t * ROWS + r]
            label = jnp.where(slot_line == r, number, label)
            width = jnp.where(slot_line == r, cols[number], width)
        lines = pl.ds(pl.multiple_of(t * 8, 8), 8)
        onehot[lines, :] = jnp.where(label == slot_lane, 1.0, 0.0)
        row_cells[lines, :] = width.astype(F32) * (CH // GROUPS)
        return carry

    lax.fori_loop(0, TILES, fill, 0)
    wide_bias[...] = jnp.zeros((1, 2 * LANES), F32)
    wide_bias[:, 0:OUT] = line_of(up_bias)
    load_lat.wait()
    source = lat[...].astype(F32)
    gat[0, tile] = local_sums(source, width_of, first, st)
    pl.semaphore_wait(barrier, awaited)

    def sum_copy(which, d):
        peer = lax.rem(tile + d, TILES)
        return remote(
            gat.at[which, tile], gat.at[which, tile], stat_send.at[which], stat_recv.at[which],
            peer, frame,
        )

    def send_sums(which):
        def one(d, carry):
            sum_copy(which, d).start()
            return carry

        lax.fori_loop(1, TILES, one, 0)

    def all_sums(which):
        others = pl.ds(0, TILES - 1)
        return remote(
            gat.at[which, others], gat.at[which, others], stat_send.at[which],
            stat_recv.at[which], lax.rem(tile + 1, TILES), frame,
        )

    send_sums(0)

    even = lax.rem(frame, 2) == 0
    next_frame = frame + 1 < FRAMES
    skip_frame = even & (frame + 2 < FRAMES)
    relay = even & (frame >= 2)
    has = {1: frame >= 1, 0: frame >= 2}
    above = tile >= 1
    below = tile + 1 < TILES

    pieces = (pl.ds(0, WIDE), pl.ds(LAST, WIDE), pl.ds(WIDE, LAST - WIDE))

    def frame_copies(kind, src, a, to_frame):
        return [
            remote(
                src.at[p], main.at[a].at[p], main_send.at[kind, i], main_recv.at[a, i], tile,
                to_frame,
            )
            for i, p in enumerate(pieces)
        ]

    to_next = frame_copies(1, lat, 1, frame + 1)
    to_skip = frame_copies(0, lat, 0, frame + 2)
    to_relay = frame_copies(2, main.at[1], 0, frame + 1)
    diagonal_up = remote(
        main.at[1].at[pieces[0]], bot.at[0], halo_send.at[3, 0], halo_recv.at[0, 0], tile - 1,
        frame + 1,
    )
    diagonal_down = remote(
        main.at[1].at[pieces[1]], top.at[0], halo_send.at[3, 1], halo_recv.at[0, 1], tile + 1,
        frame + 1,
    )

    def halo(a):
        src = lat if a == 2 else main.at[a]
        up = remote(
            src.at[pl.ds(0, WIDE)], bot.at[a], halo_send.at[a, 0], halo_recv.at[a, 0],
            tile - 1, frame,
        )
        down = remote(
            src.at[pl.ds(LAST, WIDE)], top.at[a], halo_send.at[a, 1], halo_recv.at[a, 1],
            tile + 1, frame,
        )
        return up, down

    def start_halo(a):
        up, down = halo(a)

        @pl.when(above)
        def _():
            up.start()

        @pl.when(below)
        def _():
            down.start()

    def wait_halo(a):
        up, down = halo(a)

        @pl.when(below)
        def _():
            up.wait_recv()

        @pl.when(above)
        def _():
            down.wait_recv()

    def end_halo(a):
        up, down = halo(a)

        @pl.when(above)
        def _():
            up.wait_send()

        @pl.when(below)
        def _():
            down.wait_send()

    @pl.when(next_frame)
    def _():
        for copy in to_next:
            copy.start()

    start_halo(2)

    all_sums(0).wait_recv()

    @pl.when(skip_frame)
    def _():
        for copy in to_skip:
            copy.start()

    mean, scale = combine_sums(gat[0], onehot[...], row_cells[...])
    tabs[2, 0:8, :] = mean
    tabs[2, 8:16, :] = scale
    tab_next = remote(tabs.at[2], tabs.at[1], tab_send.at[1], tab_recv.at[1], tile, frame + 1)
    tab_skip = remote(tabs.at[2], tabs.at[0], tab_send.at[0], tab_recv.at[0], tile, frame + 2)

    @pl.when(next_frame)
    def _():
        tab_next.start()

    @pl.when(frame + 2 < FRAMES)
    def _():
        tab_skip.start()

    column = lax.broadcasted_iota(jnp.int32, (COLS, CH), 0)

    def activate(a, row, cells):
        label = label_of(first - 1 + row)
        width = width_of(first - 1 + row)
        row_mean, row_scale = pick(tabs[a], label)
        normed = (cells - row_mean) * row_scale * line_of(first_gain) + line_of(first_shift)
        half_normed = 0.5 * normed
        hidden = half_normed + half_normed * jnp.tanh(half_normed)
        hidden = jnp.where(column < width, hidden, 0.0)
        hidden = jnp.concatenate([hidden, jnp.zeros((WIDE - COLS, CH), F32)], axis=0)
        lines = pl.ds(row * WIDE, WIDE)
        hid[a, lines, 0:CH] = pltpu.roll(hidden, 1, 0).astype(BF16)
        hid[a, lines, CH : 2 * CH] = hidden.astype(BF16)
        hid[a, lines, 2 * CH : 3 * CH] = pltpu.roll(hidden, WIDE - 1, 0).astype(BF16)

    def activate_main(a):
        cells = lat[...].astype(F32) if a == 2 else main[a].astype(F32)
        for r in range(ROWS):
            activate(a, r + 1, cells[r * COLS : (r + 1) * COLS])

    def activate_halo(a):
        activate(a, 0, top[a].astype(F32)[WIDE - COLS :])
        activate(a, ROWS + 1, bot[a].astype(F32)[:COLS])

    def convolve(a):
        def tap(b, carry):
            lines = pl.ds(pl.multiple_of(b * WIDE, 16), PADDED)
            product = jnp.dot(hid[a, lines, :], weight[a * 3 + b], preferred_element_type=F32)
            if a == 2:
                acc[b] = product
            else:
                acc[b] = acc[b] + product
            return carry

        lax.fori_loop(0, 3, tap, 0)

    @pl.when(has[1])
    def _():
        to_next[0].wait_recv()
        to_next[1].wait_recv()
        start_halo(1)

    @pl.when(relay)
    def _():
        to_relay[0].start()
        to_relay[1].start()

    @pl.when(relay & above)
    def _():
        diagonal_up.start()

    @pl.when(relay & below)
    def _():
        diagonal_down.start()

    activate_main(2)

    @pl.when(relay)
    def _():
        to_next[2].wait_recv()
        to_relay[2].start()

    wait_halo(2)
    activate_halo(2)
    load.wait()
    convolve(2)

    @pl.when(has[1] & jnp.logical_not(relay))
    def _():
        to_next[2].wait_recv()

    @pl.when(relay)
    def _():
        to_skip[0].wait_recv()
        to_skip[1].wait_recv()
        start_halo(0)

    @pl.when(has[1])
    def _():
        tab_next.wait_recv()
        activate_main(1)
        wait_halo(1)
        activate_halo(1)
        convolve(1)

    @pl.when(has[0] & jnp.logical_not(relay))
    def _():
        to_skip[0].wait_recv()
        to_skip[1].wait_recv()

    @pl.when(has[0])
    def _():
        to_skip[2].wait_recv()
        tab_skip.wait_recv()
        activate_main(0)
        wait_halo(0)
        activate_halo(0)
        convolve(0)

    source = lat[...].astype(F32)
    rows = []
    for r in range(ROWS):
        label = label_of(first + r)
        lines = pl.ds(r * WIDE, COLS)
        total = acc[1, lines, :]
        total = total + jnp.where(label_of(first + r - 1) == label, acc[0, lines, :], 0.0)
        total = total + jnp.where(label_of(first + r + 1) == label, acc[2, lines, :], 0.0)
        total = source[r * COLS : (r + 1) * COLS] + total + line_of(conv_bias)
        rows.append(jnp.where(column < width_of(first + r), total, 0.0))
    own[...] = jnp.concatenate(rows, axis=0).astype(BF16)

    half = CELLS // 2
    halves = (pl.ds(0, half), pl.ds(half, half))
    ahead, behind, across = tile_at(x, y + 1, z), tile_at(x, y + 3, z), tile_at(x, y, z + 1)

    def pass_on(src, slot, h, peer):
        return remote(
            src.at[halves[h]], kv.at[slot].at[halves[h]], kv_send.at[slot, h],
            kv_recv.at[slot, h], peer, frame,
        )

    kv_across = [pass_on(own, 4, h, across) for h in range(2)]
    kv_copies = list(kv_across)
    to_ahead, to_behind, relays = [], [], []
    for zz in range(2):
        base = own if zz == 0 else kv.at[4]
        to_ahead.append([pass_on(base, zz * 4 + 1, h, ahead) for h in range(2)])
        to_behind.append([pass_on(base, zz * 4 + 3, h, behind) for h in range(2)])
        relays.append([pass_on(kv.at[zz * 4 + 1], zz * 4 + 2, 0, ahead),
                       pass_on(kv.at[zz * 4 + 3], zz * 4 + 2, 1, behind)])
        kv_copies += to_ahead[zz] + to_behind[zz] + relays[zz]
    q_copies = []
    for d in range(1, 4):
        peer = tile_at(x + d, y, z)
        q_copies.append(remote(own, qb.at[d - 1], q_send.at[d - 1], q_recv.at[d - 1], peer, frame))
    source = own[...].astype(F32)
    gat[1, tile] = local_sums(source, width_of, first, st)
    send_sums(1)
    kv_across[0].start()
    to_ahead[0][0].start()
    to_behind[0][1].start()
    kv_across[1].start()
    to_ahead[0][1].start()
    to_behind[0][0].start()
    for copy in q_copies:
        copy.start()
    kv_across[0].wait_recv()
    to_ahead[1][0].start()
    kv_across[1].wait_recv()
    to_behind[1][1].start()
    all_sums(1).wait_recv()
    mean, scale = combine_sums(gat[1], onehot[...], row_cells[...])
    tab[0:8, :] = mean
    tab[8:16, :] = scale
    to_ahead[0][0].wait_recv()
    relays[0][0].start()
    to_behind[0][1].wait_recv()
    relays[0][1].start()
    to_ahead[1][1].start()
    to_behind[1][0].start()
    column = lax.broadcasted_iota(jnp.int32, (COLS, CH), 0)
    cell_column = lax.broadcasted_iota(jnp.int32, (COLS, LANES), 0)
    lane = lax.broadcasted_iota(jnp.int32, (COLS, LANES), 1)
    wide_lane = lax.broadcasted_iota(jnp.int32, (CELLS, LANES), 1)
    to_exponent = CH ** (-0.5) * math.log2(math.e)

    def normalise(block, block_tile):
        cells = block.astype(F32)
        rows = []
        for r in range(ROWS):
            at = block_tile * ROWS + r
            row_mean, row_scale = pick(tab, label_of(at))
            part = cells[r * COLS : (r + 1) * COLS]
            normed = (part - row_mean) * row_scale * line_of(second_gain) + line_of(second_shift)
            rows.append(jnp.where(column < width_of(at), normed, 0.0))
        return jnp.concatenate(rows, axis=0).astype(BF16)

    def put_query(slot, block, block_tile):
        normed = normalise(block, block_tile)
        plain = jnp.dot(normed, triple_weight[:, 0:CH], preferred_element_type=F32)
        plain = (plain + line_of(triple_bias, 0)).astype(BF16)
        turned = lax.dot_general(
            plain, triple_weight[:, CH : 2 * CH], NT, preferred_element_type=F32
        )
        constant = jnp.sum(
            plain.astype(F32) * line_of(triple_bias, 1), axis=1, keepdims=True
        )
        queries[slot, :, 0:CH] = (turned * to_exponent).astype(BF16)
        marks = []
        for r in range(ROWS):
            label = label_of(block_tile * ROWS + r)
            marks.append(jnp.where(lane == label, 1.0, 0.0))
        marks = jnp.concatenate(marks, axis=0)
        marks = jnp.where(wide_lane == 4, constant * to_exponent, marks)
        queries[slot, :, CH:EXT] = marks.astype(BF16)

    def put_keys(slot, block, block_tile):
        lines = pl.ds(pl.multiple_of(slot * CELLS, 16), CELLS)
        keys[lines, 0:CH] = normalise(block, block_tile)
        marks = []
        for r in range(ROWS):
            at = block_tile * ROWS + r
            seen = (lane == label_of(at)) & (cell_column < width_of(at))
            mark = jnp.where(seen, 0.0, MASKED)
            marks.append(jnp.where(lane < 4, mark, jnp.where(lane == 4, 1.0, 0.0)))
        keys[lines, CH:EXT] = jnp.concatenate(marks, axis=0).astype(BF16)

    def key_tile(slot):
        return tile_at(x, y + 4 - lax.rem(slot, 4), z + lax.div(slot, 4))

    for copy in load_rest:
        copy.wait()
    put_query(0, own[...], tile)
    put_keys(0, own[...], tile)
    put_keys(4, kv[4], across)
    to_ahead[0][1].wait_recv()
    to_behind[0][0].wait_recv()

    def put_pair(low_slot):
        def each_key(n, carry):
            slot = low_slot + 2 * n
            put_keys(slot, kv[slot], key_tile(slot))
            return carry

        lax.fori_loop(0, 2, each_key, 0)

    put_pair(1)
    to_ahead[1][0].wait_recv()
    relays[1][0].start()
    to_behind[1][1].wait_recv()
    relays[1][1].start()
    for d in range(1, 4):
        q_copies[d - 1].wait_recv()

    def each_query(d, carry):
        put_query(d, qb[d - 1], tile_at(x + 4 - d, y, z))
        return carry

    lax.fori_loop(1, 4, each_query, 0)
    to_ahead[1][1].wait_recv()
    to_behind[1][0].wait_recv()
    put_pair(5)
    for zz in range(2):
        for copy in relays[zz]:
            copy.wait_recv()
        put_keys(zz * 4 + 2, kv[zz * 4 + 2], key_tile(jnp.int32(zz * 4 + 2)))

    def attend(d):
        slot = lax.rem(4 - d, 4)
        scores[...] = lax.dot_general(queries[slot], keys[...], NT, preferred_element_type=F32)
        held = scores[...]
        largest = jnp.max(held, axis=1, keepdims=True)
        weights = jnp.exp2(held - largest).astype(BF16)
        mixed = jnp.dot(weights, keys[...], preferred_element_type=F32)
        sent[d] = mixed[:, 0:CH].astype(BF16)
        notes = jnp.where(wide_lane == 0, mixed[:, CH + 4 : CH + 5], 0.0)
        notes = jnp.where(wide_lane == 1, largest, notes)
        notes = jnp.concatenate([notes, jnp.zeros((4 * LANES - CELLS, LANES), F32)], axis=0)
        sent_notes[d] = jnp.transpose(notes)[0:8]

    def part_copy(d):
        return remote(
            sent.at[d], parts.at[d], part_send.at[d], part_recv.at[d], tile_at(x + d, y, z), frame
        )

    def note_copy(d):
        return remote(
            sent_notes.at[d], part_notes.at[d], note_send.at[d], note_recv.at[d],
            tile_at(x + d, y, z), frame,
        )

    def each_part(n, carry):
        d = jnp.where(n < 2, 2 + n, 3 - n)
        attend(d)

        @pl.when(d > 0)
        def _():
            note_copy(d).start()
            part_copy(d).start()

        return carry

    lax.fori_loop(0, 4, each_part, 0)
    for d in range(3, 0, -1):
        note_copy(d).wait_recv()
        part_copy(d).wait_recv()

    def part(d):
        return (sent[0] if d == 0 else parts[d]).astype(F32)

    def note(d):
        held = sent_notes[0] if d == 0 else part_notes[d]
        held = jnp.concatenate([held, jnp.zeros((LANES - 8, 4 * LANES), F32)], axis=0)
        return jnp.transpose(held)[:CELLS]

    tails = [note(d) for d in range(4)]
    maxima = [tail[:, 1:2] for tail in tails]
    most = functools.reduce(jnp.maximum, maxima)
    factors = [jnp.exp2(m - most) for m in maxima]
    denominator = sum(t[:, 0:1] * f for t, f in zip(tails, factors))
    numerator = sum(part(d) * factors[d] for d in range(4))
    averaged = (numerator / denominator).astype(BF16)
    mixed = jnp.dot(averaged, triple_weight[:, 2 * CH : 3 * CH], preferred_element_type=F32)
    mixed = (mixed + line_of(triple_bias, 2)).astype(BF16)
    attended = jnp.dot(mixed, output_weight[...], preferred_element_type=F32)
    total = own[...].astype(F32) + attended + line_of(output_bias)
    rows = []
    for r in range(ROWS):
        rows.append(
            jnp.where(column < width_of(first + r), total[r * COLS : (r + 1) * COLS], 0.0)
        )
    rim[...] = jnp.concatenate(rows, axis=0).astype(BF16)
    up = remote(
        rim.at[pl.ds(0, WIDE)], rim_bot, rim_send.at[0], rim_recv.at[0], tile - 1, frame
    )
    down = remote(
        rim.at[pl.ds(LAST, WIDE)], rim_top, rim_send.at[1], rim_recv.at[1], tile + 1, frame
    )

    @pl.when(above)
    def _():
        up.start()

    @pl.when(below)
    def _():
        down.start()

    def product(k, carry):
        taps[k, :, 0:OUT] = lax.dot_general(
            rim[...], up_weight[k], NT, preferred_element_type=F32
        )
        return carry

    lax.fori_loop(0, 9, product, 0)

    @pl.when(below)
    def _():
        up.wait_recv()
        down.wait_send()

    @pl.when(above)
    def _():
        down.wait_recv()
        up.wait_send()

    for e in range(3):
        ends[e, :, 0:OUT] = lax.dot_general(
            rim_top[...], up_weight[e], NT, preferred_element_type=F32
        )
        ends[3 + e, :, 0:OUT] = lax.dot_general(
            rim_bot[...], up_weight[6 + e], NT, preferred_element_type=F32
        )
    up_column = lax.broadcasted_iota(jnp.int32, (COLS, 2 * LANES), 0)
    for r in range(ROWS):
        label = label_of(first + r)
        lines = pl.ds(r * COLS, COLS)
        for p in range(2):
            joined = []
            other = r - 1 if p == 0 else r + 1
            alike = label_of(first + other) == label
            outer = 0 if p == 0 else 2
            for e in range(3):
                if other < 0:
                    far = ends[e, WIDE - COLS :, :]
                elif other == ROWS:
                    far = ends[3 + e, :COLS, :]
                else:
                    far = taps[outer * 3 + e, pl.ds(other * COLS, COLS), :]
                near = taps[3 + e, lines, :] + taps[(2 - outer) * 3 + e, lines, :]
                joined.append(near + jnp.where(alike, far, 0.0))
            before = jnp.where(up_column == 0, 0.0, pltpu.roll(joined[0], 1, 0))
            after = jnp.where(up_column == COLS - 1, 0.0, pltpu.roll(joined[2], COLS - 1, 0))
            valid = up_column < width_of(first + r)
            left = before + joined[1] + joined[2] + wide_bias[...]
            right = joined[0] + joined[1] + after + wide_bias[...]
            left = jnp.where(valid, left, 0.0)
            right = jnp.where(valid, right, 0.0)
            for half, lanes in ((low, slice(0, LANES)), (high, slice(LANES, 2 * LANES))):
                half[pl.ds(0, COLS, stride=2), :] = left[:, lanes]
                half[pl.ds(1, COLS, stride=2), :] = right[:, lanes]
            out[2 * r + p, :, 0:LANES] = low[...].astype(BF16)
            out[2 * r + p, :, LANES:OUT] = high[:, 0 : OUT - LANES].astype(BF16)

    @pl.when(next_frame)
    def _():
        for copy in to_next:
            copy.wait_send()
        tab_next.wait_send()

    @pl.when(frame + 2 < FRAMES)
    def _():
        tab_skip.wait_send()

    @pl.when(skip_frame)
    def _():
        for copy in to_skip:
            copy.wait_send()

    @pl.when(relay)
    def _():
        for copy in to_relay:
            copy.wait_send()
        end_halo(0)

    @pl.when(relay & above)
    def _():
        diagonal_up.wait_send()

    @pl.when(relay & below)
    def _():
        diagonal_down.wait_send()

    end_halo(2)

    @pl.when(has[1])
    def _():
        end_halo(1)

    all_sums(0).wait_send()
    all_sums(1).wait_send()
    for copy in kv_copies + q_copies:
        copy.wait_send()
    for d in range(3, 0, -1):
        part_copy(d).wait_send()
        note_copy(d).wait_send()


def shards(
    latents,
    row_video,
    video_cols,
    first_gain,
    first_shift,
    conv_weight,
    conv_bias,
    second_gain,
    second_shift,
    triple_weight,
    triple_bias,
    output_weight,
    output_bias,
    upsample_weight,
    upsample_bias,
):
    smem = pl.BlockSpec(memory_space=pltpu.SMEM)
    vmem = pl.BlockSpec(memory_space=pltpu.VMEM)
    anywhere = pl.BlockSpec(memory_space=pl.ANY)
    dma = pltpu.SemaphoreType.DMA
    block = (CELLS, CH)
    edge = (WIDE, CH)
    decoded = pl.pallas_call(
        whole_kernel,
        out_shape=jax.ShapeDtypeStruct((2 * ROWS, 2 * COLS, OUT), BF16),
        in_specs=[smem, smem, anywhere, vmem, vmem, anywhere, vmem, vmem, vmem]
        + [anywhere, vmem] * 3,
        out_specs=vmem,
        scratch_shapes=[
            pltpu.VMEM((CH, 3 * CH), BF16),
            pltpu.VMEM((CH, CH), BF16),
            pltpu.VMEM((9, OUT, CH), BF16),
            pltpu.VMEM(block, BF16),
            pltpu.VMEM((2,) + block, BF16),
            pltpu.VMEM((3,) + edge, BF16),
            pltpu.VMEM((3,) + edge, BF16),
            pltpu.VMEM((2, TILES, 8, LANES), F32),
            pltpu.VMEM((TILES * 8, LANES), F32),
            pltpu.VMEM((TILES * 8, LANES), F32),
            pltpu.VMEM((8, CH), F32),
            pltpu.VMEM((3, 16, CH), F32),
            pltpu.VMEM((3, 6 * WIDE, 3 * CH), BF16),
            pltpu.VMEM((9, 3 * CH, CH), BF16),
            pltpu.VMEM((3, PADDED, CH), F32),
            pltpu.VMEM(block, BF16),
            pltpu.VMEM((8,) + block, BF16),
            pltpu.VMEM((3,) + block, BF16),
            pltpu.VMEM((16, CH), F32),
            pltpu.VMEM((KEYS, EXT), BF16),
            pltpu.VMEM((4, CELLS, EXT), BF16),
            pltpu.VMEM((CELLS, KEYS), F32),
            pltpu.VMEM((4,) + block, BF16),
            pltpu.VMEM((4,) + block, BF16),
            pltpu.VMEM((4, 8, 4 * LANES), F32),
            pltpu.VMEM((4, 8, 4 * LANES), F32),
            pltpu.VMEM(block, BF16),
            pltpu.VMEM(edge, BF16),
            pltpu.VMEM(edge, BF16),
            pltpu.VMEM((9, CELLS, 2 * LANES), F32),
            pltpu.VMEM((6, WIDE, 2 * LANES), F32),
            pltpu.VMEM((2 * COLS, LANES), F32),
            pltpu.VMEM((2 * COLS, LANES), F32),
            pltpu.VMEM((1, 2 * LANES), F32),
            dma((2,)),
            dma((2,)),
            dma((3, 3)),
            dma((2, 3)),
            dma((4, 2)),
            dma((3, 2)),
            dma((2,)),
            dma((2,)),
            dma((5,)),
            dma((8, 2)),
            dma((8, 2)),
            dma((3,)),
            dma((3,)),
            dma((4,)),
            dma((4,)),
            dma((4,)),
            dma((4,)),
            dma((2,)),
            dma((2,)),
        ],
        compiler_params=pltpu.CompilerParams(
            collective_id=0, has_side_effects=True, vmem_limit_bytes=56 * 2**20
        ),
        name="decoder_window",
    )(
        row_video, video_cols, latents.reshape(CELLS, CH), first_gain, first_shift,
        conv_weight.reshape(9, 3 * CH, CH), conv_bias, second_gain, second_shift, triple_weight,
        triple_bias, output_weight, output_bias,
        jnp.transpose(upsample_weight, (0, 1, 3, 2)).reshape(9, OUT, CH), upsample_bias,
    )
    return decoded.reshape(2 * ROWS, 1, 2 * COLS, OUT)


def solution(mesh):
    in_specs = (P("tile", "frame", None, None),) + (P(),) * 14
    out_specs = P("tile", "frame", None, None)
    return jax.shard_map(shards, mesh=mesh, in_specs=in_specs, out_specs=out_specs, check_vma=False)
```

```python
import functools
import math

import jax
import jax.numpy as jnp
from jax import lax
from jax.experimental import pallas as pl
from jax.experimental.pallas import tpu as pltpu
from jax.sharding import PartitionSpec as P

GROUPS = 32
EPSILON = 1e-05
MASKED = -1e30
HIGHEST = lax.Precision.HIGHEST
MESH = pl.DeviceIdType.MESH
F32 = jnp.float32
BF16 = jnp.bfloat16
CH = 384
OUT = 192
ROWS = 4
COLS = 104
WIDE = 112
CELLS = ROWS * COLS
PADDED = ROWS * WIDE
LAST = CELLS - WIDE
LANES = 128
EXT = CH + LANES
TILES = 32
FRAMES = 8
KEYS = 8 * CELLS
NT = (((1,), (1,)), ((), ()))


def remote(src, dst, send_sem, recv_sem, tile, frame):
    return pltpu.make_async_remote_copy(
        src_ref=src,
        dst_ref=dst,
        send_sem=send_sem,
        recv_sem=recv_sem,
        device_id={"tile": tile, "frame": frame},
        device_id_type=MESH,
    )


def place():
    tile = lax.axis_index("tile")
    frame = lax.axis_index("frame")
    x = lax.div(tile, 8)
    y = lax.rem(lax.div(tile, 2), 4)
    z = lax.rem(tile, 2)
    return tile, frame, x, y, z


def tile_at(x, y, z):
    return lax.rem(x, 4) * 8 + lax.rem(y, 4) * 2 + lax.rem(z, 2)


def greet(barrier, tile, frame):
    pl.semaphore_signal(
        barrier, inc=1, device_id={"tile": tile, "frame": frame}, device_id_type=MESH
    )


def exact(a, b):
    return jnp.dot(a, b, precision=HIGHEST, preferred_element_type=F32)


def line_of(vector, part=None):
    held = vector[...] if part is None else vector[pl.ds(part * CH, CH)]
    return held.reshape(1, held.shape[0])


def pick(table, label):
    rows = lax.broadcasted_iota(jnp.int32, (8, CH), 0)
    chosen = rows == label
    mean = jnp.sum(jnp.where(chosen, table[0:8, :], 0.0), axis=0, keepdims=True)
    scale = jnp.sum(jnp.where(chosen, table[8:16, :], 0.0), axis=0, keepdims=True)
    return mean, scale


def members():
    per_group = CH // GROUPS
    start = lax.broadcasted_iota(jnp.int32, (LANES, CH), 0) * per_group
    channel = lax.broadcasted_iota(jnp.int32, (LANES, CH), 1)
    across = jnp.where((channel >= start) & (channel < start + per_group), 1.0, 0.0)
    start = lax.broadcasted_iota(jnp.int32, (CH, LANES), 1) * per_group
    channel = lax.broadcasted_iota(jnp.int32, (CH, LANES), 0)
    down = jnp.where((channel >= start) & (channel < start + per_group), 1.0, 0.0)
    return across, down


def local_sums(values, width_of, first, st):
    member, member_t = members()
    column = lax.broadcasted_iota(jnp.int32, (COLS, CH), 0)
    line = lax.broadcasted_iota(jnp.int32, (8, 1), 0)
    per_row = jnp.ones((8, 1), F32)
    for r in range(ROWS):
        width = width_of(first + r)
        mask = column < width
        cells = values[r * COLS : (r + 1) * COLS]
        total = jnp.sum(jnp.where(mask, cells, 0.0), axis=0, keepdims=True)
        mean = total / width.astype(F32)
        apart = jnp.where(mask, cells - mean, 0.0)
        st[r : r + 1, :] = total
        st[ROWS + r : ROWS + r + 1, :] = jnp.sum(apart * apart, axis=0, keepdims=True)
        per_row = jnp.where((line == r) | (line == ROWS + r), width.astype(F32), per_row)
    upper = line < ROWS
    held = st[...]
    grouped = exact(held, member_t)
    group_mean = exact(jnp.where(upper, grouped / (per_row * (CH // GROUPS)), 0.0), member)
    spread = jnp.where(upper, held / per_row - group_mean, 0.0)
    extra = exact(per_row * spread * spread, member_t)
    lower = pltpu.roll(extra, ROWS, 0)
    return jnp.where(upper, grouped, grouped + lower)


def combine_sums(gat, onehot, row_cells):
    member, _ = members()
    held = gat.reshape(TILES * 8, LANES)
    upper = lax.rem(lax.broadcasted_iota(jnp.int32, (TILES * 8, LANES), 0), 8) < ROWS
    by_video = jnp.transpose(onehot)[0:8]
    counts = exact(by_video, jnp.where(upper, row_cells, 0.0))
    inverse = jnp.where(counts > 0.0, 1.0 / counts, 0.0)
    mean = exact(by_video, jnp.where(upper, held, 0.0)) * inverse
    mean_rows = exact(onehot[:, 0:8], mean)
    off = held / row_cells - mean_rows
    spread = jnp.where(upper, row_cells * off * off, held)
    variance = exact(by_video, spread) * inverse
    scale = lax.rsqrt(variance + EPSILON)
    return exact(mean, member), exact(scale, member)


def whole_kernel(
    videos, cols, lat_hbm, first_gain, first_shift, conv_hbm, conv_bias, second_gain, second_shift,
    triple_hbm, triple_bias, output_hbm, output_bias, up_hbm, up_bias, out,
    triple_weight, output_weight, up_weight, lat, main, top, bot, gat, onehot, row_cells, st, tabs, hid, weight, acc,
    own, kv, qb, tab, keys, queries, scores, sent, parts, sent_notes, part_notes, rim, rim_top, rim_bot,
    taps, ends, low, high, wide_bias,
    stat_send, stat_recv, main_send, main_recv, halo_send, halo_recv, tab_send, tab_recv,
    load_sem, kv_send, kv_recv, q_send, q_recv, part_send, part_recv, note_send, note_recv,
    rim_send, rim_recv,
):
    tile, frame, x, y, z = place()
    first = tile * ROWS
    load_lat = pltpu.make_async_copy(lat_hbm, lat, load_sem.at[0])
    load_lat.start()
    load = pltpu.make_async_copy(conv_hbm, weight, load_sem.at[1])
    load.start()
    load_rest = [
        pltpu.make_async_copy(triple_hbm, triple_weight, load_sem.at[2]),
        pltpu.make_async_copy(output_hbm, output_weight, load_sem.at[3]),
        pltpu.make_async_copy(up_hbm, up_weight, load_sem.at[4]),
    ]
    for copy in load_rest:
        copy.start()

    def label_of(row):
        inside = (row >= 0) & (row < TILES * ROWS)
        return jnp.where(inside, videos[jnp.clip(row, 0, TILES * ROWS - 1)], -1)

    def width_of(row):
        inside = (row >= 0) & (row < TILES * ROWS)
        return jnp.where(inside, cols[videos[jnp.clip(row, 0, TILES * ROWS - 1)]], 0)

    barrier = pltpu.get_barrier_semaphore()

    def greet_tile(d, carry):
        greet(barrier, lax.rem(tile + d, TILES), frame)
        return carry

    lax.fori_loop(1, TILES, greet_tile, 0)
    awaited = TILES - 1
    for step in (-2, -1, 1, 2):
        there = (frame + step >= 0) & (frame + step < FRAMES)

        @pl.when(there)
        def _():
            greet(barrier, tile, frame + step)

        awaited = awaited + there.astype(jnp.int32)

    partner = frame + 1 - 2 * lax.rem(frame, 2)
    for step in (-1, 1):
        there = (tile + step >= 0) & (tile + step < TILES)

        @pl.when(there)
        def _():
            greet(barrier, tile + step, partner)

        awaited = awaited + there.astype(jnp.int32)

    slot_line = lax.rem(lax.broadcasted_iota(jnp.int32, (8, LANES), 0), ROWS)
    slot_lane = lax.broadcasted_iota(jnp.int32, (8, LANES), 1)

    def fill(t, carry):
        label = jnp.full((8, LANES), -1, jnp.int32)
        width = jnp.zeros((8, LANES), jnp.int32)
        for r in range(ROWS):
            number = videos[t * ROWS + r]
            label = jnp.where(slot_line == r, number, label)
            width = jnp.where(slot_line == r, cols[number], width)
        lines = pl.ds(pl.multiple_of(t * 8, 8), 8)
        onehot[lines, :] = jnp.where(label == slot_lane, 1.0, 0.0)
        row_cells[lines, :] = width.astype(F32) * (CH // GROUPS)
        return carry

    lax.fori_loop(0, TILES, fill, 0)
    wide_bias[...] = jnp.zeros((1, 2 * LANES), F32)
    wide_bias[:, 0:OUT] = line_of(up_bias)
    load_lat.wait()
    source = lat[...].astype(F32)
    gat[0, tile] = local_sums(source, width_of, first, st)
    pl.semaphore_wait(barrier, awaited)

    def sum_copy(which, d):
        peer = lax.rem(tile + d, TILES)
        return remote(
            gat.at[which, tile], gat.at[which, tile], stat_send.at[which], stat_recv.at[which],
            peer, frame,
        )

    def send_sums(which):
        def one(d, carry):
            sum_copy(which, d).start()
            return carry

        lax.fori_loop(1, TILES, one, 0)

    def all_sums(which):
        others = pl.ds(0, TILES - 1)
        return remote(
            gat.at[which, others], gat.at[which, others], stat_send.at[which],
            stat_recv.at[which], lax.rem(tile + 1, TILES), frame,
        )

    send_sums(0)

    even = lax.rem(frame, 2) == 0
    next_frame = frame + 1 < FRAMES
    skip_frame = even & (frame + 2 < FRAMES)
    relay = even & (frame >= 2)
    has = {1: frame >= 1, 0: frame >= 2}
    above = tile >= 1
    below = tile + 1 < TILES

    pieces = (pl.ds(0, WIDE), pl.ds(LAST, WIDE), pl.ds(WIDE, LAST - WIDE))

    def frame_copies(kind, src, a, to_frame):
        return [
            remote(
                src.at[p], main.at[a].at[p], main_send.at[kind, i], main_recv.at[a, i], tile,
                to_frame,
            )
            for i, p in enumerate(pieces)
        ]

    to_next = frame_copies(1, lat, 1, frame + 1)
    to_skip = frame_copies(0, lat, 0, frame + 2)
    to_relay = frame_copies(2, main.at[1], 0, frame + 1)
    diagonal_up = remote(
        main.at[1].at[pieces[0]], bot.at[0], halo_send.at[3, 0], halo_recv.at[0, 0], tile - 1,
        frame + 1,
    )
    diagonal_down = remote(
        main.at[1].at[pieces[1]], top.at[0], halo_send.at[3, 1], halo_recv.at[0, 1], tile + 1,
        frame + 1,
    )

    def halo(a):
        src = lat if a == 2 else main.at[a]
        up = remote(
            src.at[pl.ds(0, WIDE)], bot.at[a], halo_send.at[a, 0], halo_recv.at[a, 0],
            tile - 1, frame,
        )
        down = remote(
            src.at[pl.ds(LAST, WIDE)], top.at[a], halo_send.at[a, 1], halo_recv.at[a, 1],
            tile + 1, frame,
        )
        return up, down

    def start_halo(a):
        up, down = halo(a)

        @pl.when(above)
        def _():
            up.start()

        @pl.when(below)
        def _():
            down.start()

    def wait_halo(a):
        up, down = halo(a)

        @pl.when(below)
        def _():
            up.wait_recv()

        @pl.when(above)
        def _():
            down.wait_recv()

    def end_halo(a):
        up, down = halo(a)

        @pl.when(above)
        def _():
            up.wait_send()

        @pl.when(below)
        def _():
            down.wait_send()

    @pl.when(next_frame)
    def _():
        for copy in to_next:
            copy.start()

    start_halo(2)

    all_sums(0).wait_recv()

    @pl.when(skip_frame)
    def _():
        for copy in to_skip:
            copy.start()

    mean, scale = combine_sums(gat[0], onehot[...], row_cells[...])
    tabs[2, 0:8, :] = mean
    tabs[2, 8:16, :] = scale
    tab_next = remote(tabs.at[2], tabs.at[1], tab_send.at[1], tab_recv.at[1], tile, frame + 1)
    tab_skip = remote(tabs.at[2], tabs.at[0], tab_send.at[0], tab_recv.at[0], tile, frame + 2)

    @pl.when(next_frame)
    def _():
        tab_next.start()

    @pl.when(frame + 2 < FRAMES)
    def _():
        tab_skip.start()

    column = lax.broadcasted_iota(jnp.int32, (COLS, CH), 0)

    def activate(a, row, cells):
        label = label_of(first - 1 + row)
        width = width_of(first - 1 + row)
        row_mean, row_scale = pick(tabs[a], label)
        normed = (cells - row_mean) * row_scale * line_of(first_gain) + line_of(first_shift)
        half_normed = 0.5 * normed
        hidden = half_normed + half_normed * jnp.tanh(half_normed)
        hidden = jnp.where(column < width, hidden, 0.0)
        hidden = jnp.concatenate([hidden, jnp.zeros((WIDE - COLS, CH), F32)], axis=0)
        lines = pl.ds(row * WIDE, WIDE)
        hid[a, lines, 0:CH] = pltpu.roll(hidden, 1, 0).astype(BF16)
        hid[a, lines, CH : 2 * CH] = hidden.astype(BF16)
        hid[a, lines, 2 * CH : 3 * CH] = pltpu.roll(hidden, WIDE - 1, 0).astype(BF16)

    def activate_main(a):
        cells = lat[...].astype(F32) if a == 2 else main[a].astype(F32)
        for r in range(ROWS):
            activate(a, r + 1, cells[r * COLS : (r + 1) * COLS])

    def activate_halo(a):
        activate(a, 0, top[a].astype(F32)[WIDE - COLS :])
        activate(a, ROWS + 1, bot[a].astype(F32)[:COLS])

    def convolve(a):
        def tap(b, carry):
            lines = pl.ds(pl.multiple_of(b * WIDE, 16), PADDED)
            product = jnp.dot(hid[a, lines, :], weight[a * 3 + b], preferred_element_type=F32)
            if a == 2:
                acc[b] = product
            else:
                acc[b] = acc[b] + product
            return carry

        lax.fori_loop(0, 3, tap, 0)

    @pl.when(has[1])
    def _():
        to_next[0].wait_recv()
        to_next[1].wait_recv()
        start_halo(1)

    @pl.when(relay)
    def _():
        to_relay[0].start()
        to_relay[1].start()

    @pl.when(relay & above)
    def _():
        diagonal_up.start()

    @pl.when(relay & below)
    def _():
        diagonal_down.start()

    activate_main(2)

    @pl.when(relay)
    def _():
        to_next[2].wait_recv()
        to_relay[2].start()

    wait_halo(2)
    activate_halo(2)
    load.wait()
    convolve(2)

    @pl.when(has[1] & jnp.logical_not(relay))
    def _():
        to_next[2].wait_recv()

    @pl.when(relay)
    def _():
        to_skip[0].wait_recv()
        to_skip[1].wait_recv()
        start_halo(0)

    @pl.when(has[1])
    def _():
        tab_next.wait_recv()
        activate_main(1)
        wait_halo(1)
        activate_halo(1)
        convolve(1)

    @pl.when(has[0] & jnp.logical_not(relay))
    def _():
        to_skip[0].wait_recv()
        to_skip[1].wait_recv()

    @pl.when(has[0])
    def _():
        to_skip[2].wait_recv()
        tab_skip.wait_recv()
        activate_main(0)
        wait_halo(0)
        activate_halo(0)
        convolve(0)

    source = lat[...].astype(F32)
    rows = []
    for r in range(ROWS):
        label = label_of(first + r)
        lines = pl.ds(r * WIDE, COLS)
        total = acc[1, lines, :]
        total = total + jnp.where(label_of(first + r - 1) == label, acc[0, lines, :], 0.0)
        total = total + jnp.where(label_of(first + r + 1) == label, acc[2, lines, :], 0.0)
        total = source[r * COLS : (r + 1) * COLS] + total + line_of(conv_bias)
        rows.append(jnp.where(column < width_of(first + r), total, 0.0))
    own[...] = jnp.concatenate(rows, axis=0).astype(BF16)

    half = CELLS // 2
    halves = (pl.ds(0, half), pl.ds(half, half))
    ahead, behind, across = tile_at(x, y + 1, z), tile_at(x, y + 3, z), tile_at(x, y, z + 1)

    def pass_on(src, slot, h, peer):
        return remote(
            src.at[halves[h]], kv.at[slot].at[halves[h]], kv_send.at[slot, h],
            kv_recv.at[slot, h], peer, frame,
        )

    kv_across = [pass_on(own, 4, h, across) for h in range(2)]
    kv_copies = list(kv_across)
    to_ahead, to_behind, relays = [], [], []
    for zz in range(2):
        base = own if zz == 0 else kv.at[4]
        to_ahead.append([pass_on(base, zz * 4 + 1, h, ahead) for h in range(2)])
        to_behind.append([pass_on(base, zz * 4 + 3, h, behind) for h in range(2)])
        relays.append([pass_on(kv.at[zz * 4 + 1], zz * 4 + 2, 0, ahead),
                       pass_on(kv.at[zz * 4 + 3], zz * 4 + 2, 1, behind)])
        kv_copies += to_ahead[zz] + to_behind[zz] + relays[zz]
    q_copies = []
    for d in range(1, 4):
        peer = tile_at(x + d, y, z)
        q_copies.append(remote(own, qb.at[d - 1], q_send.at[d - 1], q_recv.at[d - 1], peer, frame))
    source = own[...].astype(F32)
    gat[1, tile] = local_sums(source, width_of, first, st)
    send_sums(1)
    kv_across[0].start()
    to_ahead[0][0].start()
    to_behind[0][1].start()
    q_copies[1].start()
    kv_across[1].start()
    to_ahead[0][1].start()
    to_behind[0][0].start()
    q_copies[2].start()
    q_copies[0].start()
    kv_across[0].wait_recv()
    to_ahead[1][0].start()
    kv_across[1].wait_recv()
    to_behind[1][1].start()
    all_sums(1).wait_recv()
    mean, scale = combine_sums(gat[1], onehot[...], row_cells[...])
    tab[0:8, :] = mean
    tab[8:16, :] = scale
    to_ahead[0][0].wait_recv()
    relays[0][0].start()
    to_behind[0][1].wait_recv()
    relays[0][1].start()
    to_ahead[1][1].start()
    to_behind[1][0].start()
    column = lax.broadcasted_iota(jnp.int32, (COLS, CH), 0)
    cell_column = lax.broadcasted_iota(jnp.int32, (COLS, LANES), 0)
    lane = lax.broadcasted_iota(jnp.int32, (COLS, LANES), 1)
    wide_lane = lax.broadcasted_iota(jnp.int32, (CELLS, LANES), 1)
    to_exponent = CH ** (-0.5) * math.log2(math.e)

    def normalise(block, block_tile):
        cells = block.astype(F32)
        rows = []
        for r in range(ROWS):
            at = block_tile * ROWS + r
            row_mean, row_scale = pick(tab, label_of(at))
            part = cells[r * COLS : (r + 1) * COLS]
            normed = (part - row_mean) * row_scale * line_of(second_gain) + line_of(second_shift)
            rows.append(jnp.where(column < width_of(at), normed, 0.0))
        return jnp.concatenate(rows, axis=0).astype(BF16)

    def put_query(slot, block, block_tile):
        normed = normalise(block, block_tile)
        plain = jnp.dot(normed, triple_weight[:, 0:CH], preferred_element_type=F32)
        plain = (plain + line_of(triple_bias, 0)).astype(BF16)
        turned = lax.dot_general(
            plain, triple_weight[:, CH : 2 * CH], NT, preferred_element_type=F32
        )
        constant = jnp.sum(
            plain.astype(F32) * line_of(triple_bias, 1), axis=1, keepdims=True
        )
        queries[slot, :, 0:CH] = (turned * to_exponent).astype(BF16)
        marks = []
        for r in range(ROWS):
            label = label_of(block_tile * ROWS + r)
            marks.append(jnp.where(lane == label, 1.0, 0.0))
        marks = jnp.concatenate(marks, axis=0)
        marks = jnp.where(wide_lane == 4, constant * to_exponent, marks)
        queries[slot, :, CH:EXT] = marks.astype(BF16)

    def put_keys(slot, block, block_tile):
        lines = pl.ds(pl.multiple_of(slot * CELLS, 16), CELLS)
        keys[lines, 0:CH] = normalise(block, block_tile)
        marks = []
        for r in range(ROWS):
            at = block_tile * ROWS + r
            seen = (lane == label_of(at)) & (cell_column < width_of(at))
            mark = jnp.where(seen, 0.0, MASKED)
            marks.append(jnp.where(lane < 4, mark, jnp.where(lane == 4, 1.0, 0.0)))
        keys[lines, CH:EXT] = jnp.concatenate(marks, axis=0).astype(BF16)

    def key_tile(slot):
        return tile_at(x, y + 4 - lax.rem(slot, 4), z + lax.div(slot, 4))

    for copy in load_rest:
        copy.wait()
    put_query(0, own[...], tile)
    put_keys(0, own[...], tile)
    put_keys(4, kv[4], across)
    to_ahead[0][1].wait_recv()
    to_behind[0][0].wait_recv()

    def put_pair(low_slot):
        def each_key(n, carry):
            slot = low_slot + 2 * n
            put_keys(slot, kv[slot], key_tile(slot))
            return carry

        lax.fori_loop(0, 2, each_key, 0)

    put_pair(1)
    to_ahead[1][0].wait_recv()
    relays[1][0].start()
    to_behind[1][1].wait_recv()
    relays[1][1].start()
    for d in range(1, 4):
        q_copies[d - 1].wait_recv()

    def each_query(d, carry):
        put_query(d, qb[d - 1], tile_at(x + 4 - d, y, z))
        return carry

    lax.fori_loop(1, 4, each_query, 0)
    to_ahead[1][1].wait_recv()
    to_behind[1][0].wait_recv()
    put_pair(5)
    for zz in range(2):
        for copy in relays[zz]:
            copy.wait_recv()
        put_keys(zz * 4 + 2, kv[zz * 4 + 2], key_tile(jnp.int32(zz * 4 + 2)))

    def attend(d):
        slot = lax.rem(4 - d, 4)
        scores[...] = lax.dot_general(queries[slot], keys[...], NT, preferred_element_type=F32)
        held = scores[...]
        largest = jnp.max(held, axis=1, keepdims=True)
        weights = jnp.exp2(held - largest).astype(BF16)
        mixed = jnp.dot(weights, keys[...], preferred_element_type=F32)
        sent[d] = mixed[:, 0:CH].astype(BF16)
        notes = jnp.where(wide_lane == 0, mixed[:, CH + 4 : CH + 5], 0.0)
        notes = jnp.where(wide_lane == 1, largest, notes)
        notes = jnp.concatenate([notes, jnp.zeros((4 * LANES - CELLS, LANES), F32)], axis=0)
        sent_notes[d] = jnp.transpose(notes)[0:8]

    def part_copy(d):
        return remote(
            sent.at[d], parts.at[d], part_send.at[d], part_recv.at[d], tile_at(x + d, y, z), frame
        )

    def note_copy(d):
        return remote(
            sent_notes.at[d], part_notes.at[d], note_send.at[d], note_recv.at[d],
            tile_at(x + d, y, z), frame,
        )

    def each_part(n, carry):
        d = jnp.where(n < 2, 2 + n, 3 - n)
        attend(d)

        @pl.when(d > 0)
        def _():
            note_copy(d).start()
            part_copy(d).start()

        return carry

    lax.fori_loop(0, 4, each_part, 0)
    for d in range(3, 0, -1):
        note_copy(d).wait_recv()
        part_copy(d).wait_recv()

    def part(d):
        return (sent[0] if d == 0 else parts[d]).astype(F32)

    def note(d):
        held = sent_notes[0] if d == 0 else part_notes[d]
        held = jnp.concatenate([held, jnp.zeros((LANES - 8, 4 * LANES), F32)], axis=0)
        return jnp.transpose(held)[:CELLS]

    tails = [note(d) for d in range(4)]
    maxima = [tail[:, 1:2] for tail in tails]
    most = functools.reduce(jnp.maximum, maxima)
    factors = [jnp.exp2(m - most) for m in maxima]
    denominator = sum(t[:, 0:1] * f for t, f in zip(tails, factors))
    numerator = sum(part(d) * factors[d] for d in range(4))
    averaged = (numerator / denominator).astype(BF16)
    mixed = jnp.dot(averaged, triple_weight[:, 2 * CH : 3 * CH], preferred_element_type=F32)
    mixed = (mixed + line_of(triple_bias, 2)).astype(BF16)
    attended = jnp.dot(mixed, output_weight[...], preferred_element_type=F32)
    total = own[...].astype(F32) + attended + line_of(output_bias)
    rows = []
    for r in range(ROWS):
        rows.append(
            jnp.where(column < width_of(first + r), total[r * COLS : (r + 1) * COLS], 0.0)
        )
    rim[...] = jnp.concatenate(rows, axis=0).astype(BF16)
    up = remote(
        rim.at[pl.ds(0, WIDE)], rim_bot, rim_send.at[0], rim_recv.at[0], tile - 1, frame
    )
    down = remote(
        rim.at[pl.ds(LAST, WIDE)], rim_top, rim_send.at[1], rim_recv.at[1], tile + 1, frame
    )

    @pl.when(above)
    def _():
        up.start()

    @pl.when(below)
    def _():
        down.start()

    def product(k, carry):
        taps[k, :, 0:OUT] = lax.dot_general(
            rim[...], up_weight[k], NT, preferred_element_type=F32
        )
        return carry

    lax.fori_loop(0, 9, product, 0)

    @pl.when(below)
    def _():
        up.wait_recv()
        down.wait_send()

    @pl.when(above)
    def _():
        down.wait_recv()
        up.wait_send()

    for e in range(3):
        ends[e, :, 0:OUT] = lax.dot_general(
            rim_top[...], up_weight[e], NT, preferred_element_type=F32
        )
        ends[3 + e, :, 0:OUT] = lax.dot_general(
            rim_bot[...], up_weight[6 + e], NT, preferred_element_type=F32
        )
    up_column = lax.broadcasted_iota(jnp.int32, (COLS, 2 * LANES), 0)
    for r in range(ROWS):
        label = label_of(first + r)
        lines = pl.ds(r * COLS, COLS)
        for p in range(2):
            joined = []
            other = r - 1 if p == 0 else r + 1
            alike = label_of(first + other) == label
            outer = 0 if p == 0 else 2
            for e in range(3):
                if other < 0:
                    far = ends[e, WIDE - COLS :, :]
                elif other == ROWS:
                    far = ends[3 + e, :COLS, :]
                else:
                    far = taps[outer * 3 + e, pl.ds(other * COLS, COLS), :]
                near = taps[3 + e, lines, :] + taps[(2 - outer) * 3 + e, lines, :]
                joined.append(near + jnp.where(alike, far, 0.0))
            before = jnp.where(up_column == 0, 0.0, pltpu.roll(joined[0], 1, 0))
            after = jnp.where(up_column == COLS - 1, 0.0, pltpu.roll(joined[2], COLS - 1, 0))
            valid = up_column < width_of(first + r)
            left = before + joined[1] + joined[2] + wide_bias[...]
            right = joined[0] + joined[1] + after + wide_bias[...]
            left = jnp.where(valid, left, 0.0)
            right = jnp.where(valid, right, 0.0)
            for half, lanes in ((low, slice(0, LANES)), (high, slice(LANES, 2 * LANES))):
                half[pl.ds(0, COLS, stride=2), :] = left[:, lanes]
                half[pl.ds(1, COLS, stride=2), :] = right[:, lanes]
            out[2 * r + p, :, 0:LANES] = low[...].astype(BF16)
            out[2 * r + p, :, LANES:OUT] = high[:, 0 : OUT - LANES].astype(BF16)

    @pl.when(next_frame)
    def _():
        for copy in to_next:
            copy.wait_send()
        tab_next.wait_send()

    @pl.when(frame + 2 < FRAMES)
    def _():
        tab_skip.wait_send()

    @pl.when(skip_frame)
    def _():
        for copy in to_skip:
            copy.wait_send()

    @pl.when(relay)
    def _():
        for copy in to_relay:
            copy.wait_send()
        end_halo(0)

    @pl.when(relay & above)
    def _():
        diagonal_up.wait_send()

    @pl.when(relay & below)
    def _():
        diagonal_down.wait_send()

    end_halo(2)

    @pl.when(has[1])
    def _():
        end_halo(1)

    all_sums(0).wait_send()
    all_sums(1).wait_send()
    for copy in kv_copies + q_copies:
        copy.wait_send()
    for d in range(3, 0, -1):
        part_copy(d).wait_send()
        note_copy(d).wait_send()


def shards(
    latents,
    row_video,
    video_cols,
    first_gain,
    first_shift,
    conv_weight,
    conv_bias,
    second_gain,
    second_shift,
    triple_weight,
    triple_bias,
    output_weight,
    output_bias,
    upsample_weight,
    upsample_bias,
):
    smem = pl.BlockSpec(memory_space=pltpu.SMEM)
    vmem = pl.BlockSpec(memory_space=pltpu.VMEM)
    anywhere = pl.BlockSpec(memory_space=pl.ANY)
    dma = pltpu.SemaphoreType.DMA
    block = (CELLS, CH)
    edge = (WIDE, CH)
    decoded = pl.pallas_call(
        whole_kernel,
        out_shape=jax.ShapeDtypeStruct((2 * ROWS, 2 * COLS, OUT), BF16),
        in_specs=[smem, smem, anywhere, vmem, vmem, anywhere, vmem, vmem, vmem]
        + [anywhere, vmem] * 3,
        out_specs=vmem,
        scratch_shapes=[
            pltpu.VMEM((CH, 3 * CH), BF16),
            pltpu.VMEM((CH, CH), BF16),
            pltpu.VMEM((9, OUT, CH), BF16),
            pltpu.VMEM(block, BF16),
            pltpu.VMEM((2,) + block, BF16),
            pltpu.VMEM((3,) + edge, BF16),
            pltpu.VMEM((3,) + edge, BF16),
            pltpu.VMEM((2, TILES, 8, LANES), F32),
            pltpu.VMEM((TILES * 8, LANES), F32),
            pltpu.VMEM((TILES * 8, LANES), F32),
            pltpu.VMEM((8, CH), F32),
            pltpu.VMEM((3, 16, CH), F32),
            pltpu.VMEM((3, 6 * WIDE, 3 * CH), BF16),
            pltpu.VMEM((9, 3 * CH, CH), BF16),
            pltpu.VMEM((3, PADDED, CH), F32),
            pltpu.VMEM(block, BF16),
            pltpu.VMEM((8,) + block, BF16),
            pltpu.VMEM((3,) + block, BF16),
            pltpu.VMEM((16, CH), F32),
            pltpu.VMEM((KEYS, EXT), BF16),
            pltpu.VMEM((4, CELLS, EXT), BF16),
            pltpu.VMEM((CELLS, KEYS), F32),
            pltpu.VMEM((4,) + block, BF16),
            pltpu.VMEM((4,) + block, BF16),
            pltpu.VMEM((4, 8, 4 * LANES), F32),
            pltpu.VMEM((4, 8, 4 * LANES), F32),
            pltpu.VMEM(block, BF16),
            pltpu.VMEM(edge, BF16),
            pltpu.VMEM(edge, BF16),
            pltpu.VMEM((9, CELLS, 2 * LANES), F32),
            pltpu.VMEM((6, WIDE, 2 * LANES), F32),
            pltpu.VMEM((2 * COLS, LANES), F32),
            pltpu.VMEM((2 * COLS, LANES), F32),
            pltpu.VMEM((1, 2 * LANES), F32),
            dma((2,)),
            dma((2,)),
            dma((3, 3)),
            dma((2, 3)),
            dma((4, 2)),
            dma((3, 2)),
            dma((2,)),
            dma((2,)),
            dma((5,)),
            dma((8, 2)),
            dma((8, 2)),
            dma((3,)),
            dma((3,)),
            dma((4,)),
            dma((4,)),
            dma((4,)),
            dma((4,)),
            dma((2,)),
            dma((2,)),
        ],
        compiler_params=pltpu.CompilerParams(
            collective_id=0, has_side_effects=True, vmem_limit_bytes=56 * 2**20
        ),
        name="decoder_window",
    )(
        row_video, video_cols, latents.reshape(CELLS, CH), first_gain, first_shift,
        conv_weight.reshape(9, 3 * CH, CH), conv_bias, second_gain, second_shift, triple_weight,
        triple_bias, output_weight, output_bias,
        jnp.transpose(upsample_weight, (0, 1, 3, 2)).reshape(9, OUT, CH), upsample_bias,
    )
    return decoded.reshape(2 * ROWS, 1, 2 * COLS, OUT)


def solution(mesh):
    in_specs = (P("tile", "frame", None, None),) + (P(),) * 14
    out_specs = P("tile", "frame", None, None)
    return jax.shard_map(shards, mesh=mesh, in_specs=in_specs, out_specs=out_specs, check_vma=False)
```
